32 devices in a mesh: dp: 16 (over z, x, core), seq: 2 (over y).
Axes of the slice: x: 2, y: 2, z: 4, core: 2. Of those that a mesh axis runs over, the one named last changes fastest.
Arguments:
- hidden_in: bfloat16 [32, 1024, 768], P('dp', 'seq'), may hold values from -6 to 6
- memory: bfloat16 [32, 1024, 768], P('dp', 'seq'), may hold values from -6 to 6
- tgt_segment: int32 [32, 1024], P('dp', 'seq'), may hold values from 0 to 3, as said below
- src_segment: int32 [32, 1024], P('dp', 'seq'), may hold values from 0 to 3, as said below
- out_grad: bfloat16 [32, 1024, 768], P('dp', 'seq'), may hold values from -6 to 6
- self_query: bfloat16 [768, 768], replicated, may hold values from -0.21875 to 0.21875
- query_bias: bfloat16 [768], replicated, may hold values from -1.75 to 1.75
- self_key: bfloat16 [768, 768], replicated, may hold values from -0.21875 to 0.21875
- self_value: bfloat16 [768, 768], replicated, may hold values from -0.21875 to 0.21875
- value_bias: bfloat16 [768], replicated, may hold values from -0.3125 to 0.3125
- self_output: bfloat16 [768, 768], replicated, may hold values from -1.25 to 1.25
- output_bias: bfloat16 [768], replicated, may hold values from -1.75 to 1.75
- first_gain: bfloat16 [768], replicated, may hold values from 0.5 to 1.5
- first_shift: bfloat16 [768], replicated, may hold values from -1.75 to 1.75
- cross_query: bfloat16 [768, 768], replicated, may hold values from -0.21875 to 0.21875
- cross_query_bias: bfloat16 [768], replicated, may hold values from -1.75 to 1.75
- cross_key: bfloat16 [768, 768], replicated, may hold values from -0.21875 to 0.21875
- cross_value: bfloat16 [768, 768], replicated, may hold values from -0.21875 to 0.21875
- cross_value_bias: bfloat16 [768], replicated, may hold values from -0.3125 to 0.3125
- cross_output: bfloat16 [768, 768], replicated, may hold values from -1.25 to 1.25
- cross_output_bias: bfloat16 [768], replicated, may hold values from -1.75 to 1.75
- second_gain: bfloat16 [768], replicated, may hold values from 0.5 to 1.5
- second_shift: bfloat16 [768], replicated, may hold values from -1.75 to 1.75
- ffn_in: bfloat16 [768, 3072], replicated, may hold values from -0.21875 to 0.21875
- ffn_in_bias: bfloat16 [3072], replicated, may hold values from -3 to 3
- ffn_out: bfloat16 [3072, 768], replicated, may hold values from -0.109375 to 0.109375
- ffn_out_bias: bfloat16 [768], replicated, may hold values from -1.75 to 1.75
- third_gain: bfloat16 [768], replicated, may hold values from 0.5 to 1.5
- third_shift: bfloat16 [768], replicated, may hold values from -1.75 to 1.75
Outputs:
- hidden_out: bfloat16 [32, 1024, 768], P('dp', 'seq')
- hidden_grad: bfloat16 [32, 1024, 768], P('dp', 'seq')
- memory_grad: bfloat16 [32, 1024, 768], P('dp', 'seq')
- grad_self_query: float32 [768, 768], P('dp')
- grad_query_bias: float32 [768], P('dp')
- grad_self_key: float32 [768, 768], P('dp')
- grad_self_value: float32 [768, 768], P('dp')
- grad_value_bias: float32 [768], P('dp')
- grad_self_output: float32 [768, 768], P('dp')
- grad_output_bias: float32 [768], P('dp')
- grad_first_gain: float32 [768], P('dp')
- grad_first_shift: float32 [768], P('dp')
- grad_cross_query: float32 [768, 768], P('dp')
- grad_cross_query_bias: float32 [768], P('dp')
- grad_cross_key: float32 [768, 768], P('dp')
- grad_cross_value: float32 [768, 768], P('dp')
- grad_cross_value_bias: float32 [768], P('dp')
- grad_cross_output: float32 [768, 768], P('dp')
- grad_cross_output_bias: float32 [768], P('dp')
- grad_second_gain: float32 [768], P('dp')
- grad_second_shift: float32 [768], P('dp')
- grad_ffn_in: float32 [768, 3072], P('dp')
- grad_ffn_in_bias: float32 [3072], P('dp')
- grad_ffn_out: float32 [3072, 768], P('dp')
- grad_ffn_out_bias: float32 [768], P('dp')
- grad_third_gain: float32 [768], P('dp')
- grad_third_shift: float32 [768], P('dp')
The draws below stay inside these ranges and needn't reach their ends.
Inputs may be any that keep to these rules, and one draw needn't show every extreme that they name: `tgt_segment`: in every row the ids 0, 1, 2, 3 each occur and never fall; documents 0 and 1 end before position 512, document 3 starts after position 512. `src_segment`: in every row the ids 0, 1, 2, 3 each occur and never fall; documents 0 and 1 end before position 512, document 3 starts after position 512.
All inputs are finite; a program needn't handle non-finite values.
Results may differ from the reference program's by a relative error of at most 0.025.
Values may be sent and summed in bfloat16 or wider, within the bound.
No kernel may reach another device: no remote copies, remote signals or barrier semaphores. Data moves between devices by JAX's collectives and lax.ppermute only.
A program may use at most 448 MiB of HBM per device.

```python
import math
import jax
import jax.numpy as jnp
from jax import lax

D = 768
HEADS = 12
HEAD_DIM = 64
FF = 3072
SEQ = 1024
SRC = 1024
ROWS = 32
TOK_DEV = 512
SRC_DEV = 512


def segment_law(key, length, block):
    first_key, second_key, third_key = jax.random.split(key, 3)
    left_end = jax.random.randint(first_key, (ROWS,), 2, block)
    split_at = jax.random.randint(second_key, (ROWS,), 1, left_end)
    right_size = jax.random.randint(third_key, (ROWS,), 1, block)
    positions = jnp.arange(length, dtype=jnp.int32)[None, :]
    ids = (positions >= split_at[:, None]).astype(jnp.int32)
    ids = ids + (positions >= left_end[:, None]).astype(jnp.int32)
    ids = ids + (positions >= length - right_size[:, None]).astype(jnp.int32)
    return ids


def draw_tgt_segment(key, part):
    key = jax.random.fold_in(key, 11)
    return segment_law(key, SEQ, TOK_DEV)


def draw_src_segment(key, part):
    key = jax.random.fold_in(key, 12)
    return segment_law(key, SRC, SRC_DEV)


def block_scale(own_key, dims, pieces, least, high):
    level = 1.0
    for position, blocks in pieces:
        heights = jax.random.uniform(jax.random.fold_in(jax.random.fold_in(own_key, 6), position), (blocks,), jnp.float32, least / len(pieces), high / len(pieces))
        level = level * jnp.repeat(jnp.exp(heights), dims[position] // blocks).reshape((-1,) + (1,) * (len(dims) - 1 - position))
    return level


def scatter_about(key, extent, deviation, reach, cuts=(), held_as=jnp.bfloat16):
    factor_of = block_scale(key, extent, cuts, -0.22, 0.18) if cuts else 1.0
    array = jax.random.normal(key, extent, jnp.float32) * deviation * factor_of
    return jnp.minimum(jnp.maximum(array, -reach), reach).astype(held_as)


def setup_inputs(seed: int = 0) -> dict:
    key_list = jax.random.split(jax.random.key(seed), 30)
    hidden_in = scatter_about(key_list[0], (ROWS, SEQ, D), 1.0, 6.0, ((0, 16), (1, 2)))
    memory = scatter_about(key_list[1], (ROWS, SRC, D), 1.0, 6.0, ((0, 16), (1, 2)))
    tgt_segment = draw_tgt_segment(jax.random.fold_in(key_list[29], 71), 0)
    src_segment = draw_src_segment(jax.random.fold_in(key_list[29], 71), 0)
    out_grad = scatter_about(key_list[4], (ROWS, SEQ, D), 1.0, 6.0, ((0, 16), (1, 2)))
    self_query = scatter_about(key_list[5], (D, D), D ** -0.5, 0.21875)
    query_bias = scatter_about(key_list[6], (D,), 0.3, 1.75)
    self_key = scatter_about(key_list[7], (D, D), D ** -0.5, 0.21875)
    self_value = scatter_about(key_list[8], (D, D), D ** -0.5, 0.21875)
    value_bias = scatter_about(key_list[9], (D,), 0.05, 0.3125)
    self_output = scatter_about(key_list[10], (D, D), (max(D // 32, 16)) ** -0.5, 1.25)
    output_bias = scatter_about(key_list[11], (D,), 0.3, 1.75)
    first_gain = jnp.clip(1.0 + 0.1 * jax.random.normal(key_list[12], (D,), jnp.float32), 0.5, 1.5).astype(jnp.bfloat16)
    first_shift = scatter_about(key_list[13], (D,), 0.3, 1.75)
    cross_query = scatter_about(key_list[14], (D, D), D ** -0.5, 0.21875)
    cross_query_bias = scatter_about(key_list[15], (D,), 0.3, 1.75)
    cross_key = scatter_about(key_list[16], (D, D), D ** -0.5, 0.21875)
    cross_value = scatter_about(key_list[17], (D, D), D ** -0.5, 0.21875)
    cross_value_bias = scatter_about(key_list[18], (D,), 0.05, 0.3125)
    cross_output = scatter_about(key_list[19], (D, D), (max(D // 32, 16)) ** -0.5, 1.25)
    cross_output_bias = scatter_about(key_list[20], (D,), 0.3, 1.75)
    second_gain = jnp.clip(1.0 + 0.1 * jax.random.normal(key_list[21], (D,), jnp.float32), 0.5, 1.5).astype(jnp.bfloat16)
    second_shift = scatter_about(key_list[22], (D,), 0.3, 1.75)
    ffn_in = scatter_about(key_list[23], (D, FF), D ** -0.5, 0.21875)
    ffn_in_bias = scatter_about(key_list[24], (FF,), 0.5, 3.0)
    ffn_out = scatter_about(key_list[25], (FF, D), FF ** -0.5, 0.109375)
    ffn_out_bias = scatter_about(key_list[26], (D,), 0.3, 1.75)
    third_gain = jnp.clip(1.0 + 0.1 * jax.random.normal(key_list[27], (D,), jnp.float32), 0.5, 1.5).astype(jnp.bfloat16)
    third_shift = scatter_about(key_list[28], (D,), 0.3, 1.75)
    return {"hidden_in": hidden_in, "memory": memory, "tgt_segment": tgt_segment, "src_segment": src_segment, "out_grad": out_grad, "self_query": self_query, "query_bias": query_bias, "self_key": self_key, "self_value": self_value, "value_bias": value_bias, "self_output": self_output, "output_bias": output_bias, "first_gain": first_gain, "first_shift": first_shift, "cross_query": cross_query, "cross_query_bias": cross_query_bias, "cross_key": cross_key, "cross_value": cross_value, "cross_value_bias": cross_value_bias, "cross_output": cross_output, "cross_output_bias": cross_output_bias, "second_gain": second_gain, "second_shift": second_shift, "ffn_in": ffn_in, "ffn_in_bias": ffn_in_bias, "ffn_out": ffn_out, "ffn_out_bias": ffn_out_bias, "third_gain": third_gain, "third_shift": third_shift}


@jax.custom_vjp
def low(v):
    return lax.optimization_barrier(v.astype(jnp.bfloat16)).astype(jnp.float32)

@jax.custom_vjp
def low_back(v):
    return v

def low_keep(v):
    return (low(v), None)

def low_pass(kept, grad):
    return (grad,)

def back_keep(v):
    return (v, None)

def back_low(kept, grad):
    return (low(grad),)
low.defvjp(low_keep, low_pass)
low_back.defvjp(back_keep, back_low)

def low_both(values):
    return low_back(low(values))

def project(values, weight):
    return jnp.dot(values, weight, precision=lax.Precision.HIGHEST)

def layer_norm(values, norm_gain, norm_shift):
    center = values - lax.optimization_barrier(jnp.mean(values, axis=-1, keepdims=True))
    spread = lax.optimization_barrier(jnp.mean(center * center, axis=-1, keepdims=True))
    return center * lax.rsqrt(spread + 1e-05) * norm_gain + norm_shift

def exact_gelu(values):
    return jax.nn.gelu(values, approximate=False)

def attend(queries, key_rows, value_rows, query_segment, key_segment, causal):
    query_count = queries.shape[0]
    key_count = key_rows.shape[0]
    query_heads = queries.reshape(query_count, HEADS, HEAD_DIM)
    key_heads = key_rows.reshape(key_count, HEADS, HEAD_DIM)
    value_heads = value_rows.reshape(key_count, HEADS, HEAD_DIM)
    raw_scores = low_back(jnp.einsum('qhd,khd->hqk', query_heads, key_heads, precision=lax.Precision.HIGHEST))
    allowed = query_segment[:, None] == key_segment[None, :]
    if causal:
        allowed = allowed & (jnp.arange(query_count)[:, None] >= jnp.arange(key_count)[None, :])
    scores = jnp.where(allowed[None], raw_scores * (1.0 / math.sqrt(HEAD_DIM)), -1e+30)
    weights = low(jax.nn.softmax(scores, axis=-1))
    mixed_heads = jnp.einsum('hqk,khd->qhd', weights, value_heads, precision=lax.Precision.HIGHEST)
    return mixed_heads.reshape(query_count, HEADS * HEAD_DIM)

def layer(params, hidden, source, tgt_ids, src_ids):
    self_query, query_bias, self_key, self_value, value_bias, self_output, output_bias, first_gain, first_shift, cross_query, cross_query_bias, cross_key, cross_value, cross_value_bias, cross_output, cross_output_bias, second_gain, second_shift, ffn_in, ffn_in_bias, ffn_out, ffn_out_bias, third_gain, third_shift = params
    checked = jax.checkpoint(attend, static_argnums=(5,))
    queries = low_both(project(hidden, self_query) + query_bias)
    key_rows = low_both(project(hidden, self_key))
    value_rows = low_both(project(hidden, self_value) + value_bias)
    self_mixed = low_both(checked(queries, key_rows, value_rows, tgt_ids, tgt_ids, True))
    self_branch = low_back(project(self_mixed, self_output) + output_bias)
    first_norm = layer_norm(hidden + self_branch, first_gain, first_shift)
    cross_queries = low_both(project(low(first_norm), cross_query) + cross_query_bias)
    memory_keys = low_both(project(source, cross_key))
    memory_values = low_both(project(source, cross_value) + cross_value_bias)
    cross_mixed = low_both(checked(cross_queries, memory_keys, memory_values, tgt_ids, src_ids, False))
    cross_branch = low_back(project(cross_mixed, cross_output) + cross_output_bias)
    second_norm = layer_norm(first_norm + cross_branch, second_gain, second_shift)
    inner_rows = low_back(project(low(second_norm), ffn_in) + ffn_in_bias)
    ffn_branch = low_back(project(low(exact_gelu(inner_rows)), ffn_out) + ffn_out_bias)
    return layer_norm(second_norm + ffn_branch, third_gain, third_shift)

def reference(hidden_in, memory, tgt_segment, src_segment, out_grad, self_query, query_bias, self_key, self_value, value_bias, self_output, output_bias, first_gain, first_shift, cross_query, cross_query_bias, cross_key, cross_value, cross_value_bias, cross_output, cross_output_bias, second_gain, second_shift, ffn_in, ffn_in_bias, ffn_out, ffn_out_bias, third_gain, third_shift):
    params = tuple((weight.astype(jnp.float32) for weight in (self_query, query_bias, self_key, self_value, value_bias, self_output, output_bias, first_gain, first_shift, cross_query, cross_query_bias, cross_key, cross_value, cross_value_bias, cross_output, cross_output_bias, second_gain, second_shift, ffn_in, ffn_in_bias, ffn_out, ffn_out_bias, third_gain, third_shift)))

    def one_row(totals, packed):
        hidden, source, tgt_ids, src_ids, cotangent = packed

        def row_layer(weights, values, encoder):
            return layer(weights, values, encoder, tgt_ids, src_ids)
        result, pull = jax.vjp(row_layer, params, hidden, source)
        param_grads, hidden_back, source_back = pull(cotangent)
        totals = jax.tree.map(jnp.add, totals, param_grads)
        return (totals, (result.astype(jnp.bfloat16), hidden_back.astype(jnp.bfloat16), source_back.astype(jnp.bfloat16)))
    zeros = jax.tree.map(jnp.zeros_like, params)
    totals, outputs = lax.scan(one_row, zeros, (hidden_in.astype(jnp.float32), memory.astype(jnp.float32), tgt_segment, src_segment, out_grad.astype(jnp.float32)))
    return (outputs[0], outputs[1], outputs[2], totals[0], totals[1], totals[2], totals[3], totals[4], totals[5], totals[6], totals[7], totals[8], totals[9], totals[10], totals[11], totals[12], totals[13], totals[14], totals[15], totals[16], totals[17], totals[18], totals[19], totals[20], totals[21], totals[22], totals[23])
```

```python
import functools
import math

import jax
import jax.numpy as jnp
from jax import lax
from jax.experimental import pallas as pl
from jax.experimental.pallas import tpu as pltpu
from jax.sharding import PartitionSpec as P

HEADS = 12
BF=jnp.bfloat16; F32=jnp.float32
BIG=-1e30
def dot(a,b): return jnp.dot(a,b,preferred_element_type=F32)

def lane_low(shape): return lax.broadcasted_iota(jnp.int32, shape, 1) < 64

def masks(seg_q, seg_k):
    T=seg_q.shape[0]; K=seg_k.shape[0]
    r=jnp.arange(64)[:,None]
    oh=((r==seg_q[None,:])).astype(BF)
    c=jnp.arange(128)[None,:]%64
    mk=jnp.where(c<4, jnp.where(c==seg_k[:,None],0.0,BIG), jnp.where(c<7,-1.0,0.0)).astype(BF)
    return oh,mk

def fwd_kernel(q_ref,k_ref,v_ref,oh_ref,mk_ref,o_ref,l_ref,*,bq,causal):
    T=q_ref.shape[0]; K=k_ref.shape[0]
    low=lane_low((K,128))
    qT=(q_ref[...]*BF(0.125)).T
    vT=v_ref[...].T
    k=k_ref[...]; mk=mk_ref[...]; oh=oh_ref[...]
    ones=jnp.ones((16,K),BF)
    if causal:
        dm=lax.broadcasted_iota(jnp.int32,(bq,bq),0)<=lax.broadcasted_iota(jnp.int32,(bq,bq),1)
    kas=[jnp.where(low,k,mk),jnp.where(low,mk,k)]
    vas=[jnp.concatenate([vT[64*h:64*h+64],ones],0) for h in (0,1)]
    qas=[jnp.concatenate([qT[:64],oh],0),jnp.concatenate([oh,qT[64:]],0)]
    for i in range(T//bq):
        os=[]
        for h in (0,1):
            qa=qas[h][:,i*bq:(i+1)*bq]
            if causal:
                s1=jnp.where(dm,dot(kas[h][i*bq:(i+1)*bq],qa),BIG)
                m=jnp.max(s1,axis=0,keepdims=True)
                if i:
                    s0=dot(kas[h][:i*bq],qa)
                    m=jnp.maximum(m,jnp.max(s0,axis=0,keepdims=True))
                    o=dot(vas[h][:,:i*bq],jnp.exp(s0-m).astype(BF))
                    o=o+dot(vas[h][:,i*bq:(i+1)*bq],jnp.exp(s1-m).astype(BF))
                else:
                    o=dot(vas[h][:,i*bq:(i+1)*bq],jnp.exp(s1-m).astype(BF))
            else:
                s=dot(kas[h],qa)
                m=jnp.max(s,axis=0,keepdims=True)
                o=dot(vas[h],jnp.exp(s-m).astype(BF))
            l=o[64:65]
            os.append(o[:64]/l)
            l_ref[0,h:h+1,i*bq:(i+1)*bq]=m+jnp.log(l)
        o_ref[i*bq:(i+1)*bq,:]=jnp.concatenate(os,0).T.astype(BF)

def attend_fwd(q,k,v,oh,mk,causal,bq=256):
    T,D=q.shape; K=k.shape[0]; n=D//128
    pair=lambda r:pl.BlockSpec((r,128),lambda p:(0,p))
    return pl.pallas_call(functools.partial(fwd_kernel,bq=bq,causal=causal),grid=(n,),
        in_specs=[pair(T),pair(K),pair(K),pl.BlockSpec((64,T),lambda p:(0,0)),pl.BlockSpec((K,128),lambda p:(0,0))],
        out_specs=[pair(T),pl.BlockSpec((1,8,T),lambda p:(p,0,0))],
        out_shape=[jax.ShapeDtypeStruct((T,D),BF),jax.ShapeDtypeStruct((n,8,T),F32)],
        name="attend_fwd",
        compiler_params=pltpu.CompilerParams(vmem_limit_bytes=56*2**20))(q,k,v,oh,mk)

def split3(x):
    a=x.astype(BF); r=x-a.astype(F32); b=r.astype(BF); c=(r-b.astype(F32)).astype(BF)
    return a,b,c

def bwd_kernel(q_ref,k_ref,v_ref,do_ref,o_ref,l_ref,oh_ref,mk_ref,dq_ref,dk_ref,dv_ref,acc_ref,*,bk,causal):
    T=q_ref.shape[0]; K=k_ref.shape[0]
    low=lane_low((K,128))
    lowt=lane_low((T,128))
    q=q_ref[...]*BF(0.125); do=do_ref[...]
    qT=q.T; doT=do.T
    k=k_ref[...]; mk=mk_ref[...]; oh=oh_ref[...]; v=v_ref[...]
    kT=k.T
    prodT=(do.astype(F32)*o_ref[...].astype(F32)).T
    rowi=lax.broadcasted_iota(jnp.int32,(64,T),0)
    one=jnp.full((K,128),-1.0,BF)
    if causal:
        dm=lax.broadcasted_iota(jnp.int32,(bk,bk),0)<=lax.broadcasted_iota(jnp.int32,(bk,bk),1)
    qas=[];das=[]
    for h in (0,1):
        L=l_ref[0,h:h+1,:]
        a,b,c=split3(L)
        ohl=jnp.where(rowi==4,a,jnp.where(rowi==5,b,jnp.where(rowi==6,c,oh)))
        D=jnp.sum(prodT[64*h:64*h+64],axis=0,keepdims=True)
        a,b,c=split3(D)
        z=jnp.zeros((64,T),BF)
        dd=jnp.where(rowi==0,a,jnp.where(rowi==1,b,jnp.where(rowi==2,c,z)))
        if h==0:
            qas.append(jnp.concatenate([qT[:64],ohl],0)); das.append(jnp.concatenate([doT[:64],dd],0))
        else:
            qas.append(jnp.concatenate([ohl,qT[64:]],0)); das.append(jnp.concatenate([dd,doT[64:]],0))
    kas=[jnp.where(low,k,mk),jnp.where(low,mk,k)]
    vas=[jnp.where(low,v,one),jnp.where(low,one,v)]
    for j in range(K//bk):
        dks=[];dvs=[]
        q0=j*bk if causal else 0
        ks=slice(j*bk,(j+1)*bk)
        for h in (0,1):
            s=dot(kas[h][ks],qas[h][:,q0:])
            if causal:
                sd=jnp.where(dm,s[:,:bk],BIG)
                s=jnp.concatenate([sd,s[:,bk:]],1) if q0+bk<T else sd
            p=jnp.exp(s)
            dp=dot(vas[h][ks],das[h][:,q0:])
            ds=(p*dp).astype(BF)
            dvs.append(dot(p.astype(BF),do[q0:]))
            dks.append(dot(ds,q[q0:]))
            dqt=dot(kT[64*h:64*h+64,ks],ds)
            if j==0: acc_ref[64*h:64*h+64,:]=dqt
            else: acc_ref[64*h:64*h+64,q0:]+=dqt
        lw=low[:bk]
        dk_ref[ks,:]=jnp.where(lw,dks[0],dks[1]).astype(BF)
        dv_ref[ks,:]=jnp.where(lw,dvs[0],dvs[1]).astype(BF)
    dq_ref[...]=(acc_ref[...]*0.125).T.astype(BF)

def attend_bwd(q,k,v,do,o,l,oh,mk,causal,bk=256,p0=0,np_=None):
    T,D=q.shape; K=k.shape[0]; n=np_ or D//128
    pin=lambda r:pl.BlockSpec((r,128),lambda p:(0,p+p0))
    po=lambda r:pl.BlockSpec((r,128),lambda p:(0,p))
    return pl.pallas_call(functools.partial(bwd_kernel,bk=bk,causal=causal),grid=(n,),
        in_specs=[pin(T),pin(K),pin(K),pin(T),pin(T),pl.BlockSpec((1,8,T),lambda p:(p+p0,0,0)),pl.BlockSpec((64,T),lambda p:(0,0)),pl.BlockSpec((K,128),lambda p:(0,0))],
        out_specs=[po(T),po(K),po(K)],
        out_shape=[jax.ShapeDtypeStruct((T,128*n),BF),jax.ShapeDtypeStruct((K,128*n),BF),jax.ShapeDtypeStruct((K,128*n),BF)],
        scratch_shapes=[pltpu.VMEM((128,T),F32)],
        name="attend_bwd",
        compiler_params=pltpu.CompilerParams(vmem_limit_bytes=56*2**20))(q,k,v,do,o,l,oh,mk)


def project(values, weight):
    return jnp.dot(values, weight, preferred_element_type=jnp.float32)


def project_back(gradient, weight):
    return jnp.einsum("rte,de->rtd", gradient, weight, preferred_element_type=jnp.float32)


def weight_grad(values, gradient):
    return jnp.einsum("rtd,rte->de", values, gradient, preferred_element_type=jnp.float32)


def token_sum(gradient):
    return jnp.sum(gradient.astype(jnp.float32), axis=(0, 1))


def layer_norm(values, norm_gain, norm_shift):
    center = values - jnp.mean(values, axis=-1, keepdims=True)
    spread = jnp.mean(center * center, axis=-1, keepdims=True)
    return center * lax.rsqrt(spread + 1e-05) * norm_gain + norm_shift


def exact_gelu(values):
    return jax.nn.gelu(values, approximate=False)


def split_heads(values):
    return values.reshape(values.shape[0], values.shape[1], HEADS, values.shape[2] // HEADS)


def merge_heads(values):
    return values.reshape(values.shape[0], values.shape[1], values.shape[2] * values.shape[3])


def masked_scores(queries, key_rows, allowed):
    raw_scores = jnp.einsum(
        "rqhd,rkhd->rhqk",
        split_heads(queries),
        split_heads(key_rows),
        preferred_element_type=jnp.float32,
    )
    factor = 1.0 / math.sqrt(queries.shape[2] // HEADS)
    return jnp.where(allowed[:, None], raw_scores * factor, -1e30)


def attend_forward(queries, key_rows, value_rows, allowed):
    scores = masked_scores(queries, key_rows, allowed)
    highest = jnp.max(scores, axis=-1, keepdims=True)
    powers = jnp.exp(scores - highest)
    totals = jnp.sum(powers, axis=-1, keepdims=True)
    weights = (powers / totals).astype(jnp.bfloat16)
    mixed_heads = jnp.einsum(
        "rhqk,rkhd->rqhd", weights, split_heads(value_rows), preferred_element_type=jnp.float32
    )
    return (merge_heads(mixed_heads).astype(jnp.bfloat16), highest + jnp.log(totals))


def attend_backward(queries, key_rows, value_rows, allowed, log_totals, mixed_grad):
    scores = masked_scores(queries, key_rows, allowed)
    weights = jnp.exp(scores - log_totals)
    grad_heads = split_heads(mixed_grad)
    value_terms = jnp.einsum(
        "rhqk,rqhd->rkhd",
        weights.astype(jnp.bfloat16),
        grad_heads,
        preferred_element_type=jnp.float32,
    )
    weight_grads = jnp.einsum(
        "rqhd,rkhd->rhqk", grad_heads, split_heads(value_rows), preferred_element_type=jnp.float32
    )
    inner_sum = jnp.sum(weights * weight_grads, axis=-1, keepdims=True)
    factor = 1.0 / math.sqrt(queries.shape[2] // HEADS)
    score_grads = (weights * (weight_grads - inner_sum) * factor).astype(jnp.bfloat16)
    query_grads = jnp.einsum(
        "rhqk,rkhd->rqhd", score_grads, split_heads(key_rows), preferred_element_type=jnp.float32
    )
    key_terms = jnp.einsum(
        "rhqk,rqhd->rkhd", score_grads, split_heads(queries), preferred_element_type=jnp.float32
    )
    return (merge_heads(query_grads), merge_heads(key_terms), merge_heads(value_terms))


def split_rows(
    hidden_in,
    memory,
    tgt_segment,
    src_segment,
    out_grad,
    self_query,
    query_bias,
    self_key,
    self_value,
    value_bias,
    self_output,
    output_bias,
    first_gain,
    first_shift,
    cross_query,
    cross_query_bias,
    cross_key,
    cross_value,
    cross_value_bias,
    cross_output,
    cross_output_bias,
    second_gain,
    second_shift,
    ffn_in,
    ffn_in_bias,
    ffn_out,
    ffn_out_bias,
    third_gain,
    third_shift,
):
    tokens = hidden_in.shape[1]
    queries = (project(hidden_in, self_query) + query_bias.astype(jnp.float32)).astype(jnp.bfloat16)
    key_rows = project(hidden_in, self_key).astype(jnp.bfloat16)
    value_rows = (project(hidden_in, self_value) + value_bias.astype(jnp.float32)).astype(
        jnp.bfloat16
    )
    target_ids = tgt_segment.astype(jnp.bfloat16)
    all_keys, all_values, all_target = (
        lax.all_gather(key_rows, "seq", axis=1, tiled=True),
        lax.all_gather(value_rows, "seq", axis=1, tiled=True),
        lax.all_gather(target_ids, "seq", axis=1, tiled=True),
    )
    memory_keys = project(memory, cross_key).astype(jnp.bfloat16)
    memory_values = (project(memory, cross_value) + cross_value_bias.astype(jnp.float32)).astype(
        jnp.bfloat16
    )
    all_memkeys, all_memvalues, all_source = (
        lax.all_gather(memory_keys, "seq", axis=1, tiled=True),
        lax.all_gather(memory_values, "seq", axis=1, tiled=True),
        lax.all_gather(src_segment.astype(jnp.bfloat16), "seq", axis=1, tiled=True),
    )
    offset = lax.axis_index("seq") * tokens
    query_places = offset + jnp.arange(tokens, dtype=jnp.int32)
    key_places = jnp.arange(all_keys.shape[1], dtype=jnp.int32)
    self_allowed = (target_ids[:, :, None] == all_target[:, None, :]) & (
        query_places[:, None] >= key_places[None, :]
    )[None]
    cross_allowed = target_ids[:, :, None] == all_source[:, None, :]
    self_mixed, self_totals = attend_forward(queries, all_keys, all_values, self_allowed)
    self_branch = project(self_mixed, self_output) + output_bias.astype(jnp.float32)
    first_norm, first_pull = jax.vjp(
        layer_norm,
        hidden_in.astype(jnp.float32) + self_branch,
        first_gain.astype(jnp.float32),
        first_shift.astype(jnp.float32),
    )
    first_low = first_norm.astype(jnp.bfloat16)
    cross_queries = (project(first_low, cross_query) + cross_query_bias.astype(jnp.float32)).astype(
        jnp.bfloat16
    )
    cross_mixed, cross_totals = attend_forward(
        cross_queries, all_memkeys, all_memvalues, cross_allowed
    )
    cross_branch = project(cross_mixed, cross_output) + cross_output_bias.astype(jnp.float32)
    second_norm, second_pull = jax.vjp(
        layer_norm,
        first_norm + cross_branch,
        second_gain.astype(jnp.float32),
        second_shift.astype(jnp.float32),
    )
    second_low = second_norm.astype(jnp.bfloat16)
    inner_rows = project(second_low, ffn_in) + ffn_in_bias.astype(jnp.float32)
    activation_full, gelu_pull = jax.vjp(exact_gelu, inner_rows)
    activation = activation_full.astype(jnp.bfloat16)
    ffn_branch = project(activation, ffn_out) + ffn_out_bias.astype(jnp.float32)
    final_norm, third_pull = jax.vjp(
        layer_norm,
        second_norm + ffn_branch,
        third_gain.astype(jnp.float32),
        third_shift.astype(jnp.float32),
    )
    hidden_out = final_norm.astype(jnp.bfloat16)
    third_back, grad_third_gain, grad_third_shift = third_pull(out_grad.astype(jnp.float32))
    ffn_back = third_back.astype(jnp.bfloat16)
    grad_ffn_out = weight_grad(activation, ffn_back)
    grad_ffn_out_bias = token_sum(ffn_back)
    activation_back = project_back(ffn_back, ffn_out)
    inner_back = gelu_pull(activation_back)[0].astype(jnp.bfloat16)
    grad_ffn_in = weight_grad(second_low, inner_back)
    grad_ffn_in_bias = token_sum(inner_back)
    second_back, grad_second_gain, grad_second_shift = second_pull(
        third_back + project_back(inner_back, ffn_in)
    )
    cross_back = second_back.astype(jnp.bfloat16)
    grad_cross_output = weight_grad(cross_mixed, cross_back)
    grad_cross_output_bias = token_sum(cross_back)
    cross_mixed_back = project_back(cross_back, cross_output).astype(jnp.bfloat16)
    cross_query_grad, memkey_terms, memvalue_terms = attend_backward(
        cross_queries, all_memkeys, all_memvalues, cross_allowed, cross_totals, cross_mixed_back
    )
    memkey_sum, memvalue_sum = (
        lax.psum_scatter(
            memkey_terms.astype(jnp.bfloat16), "seq", scatter_dimension=1, tiled=True
        ).astype(jnp.float32),
        lax.psum_scatter(
            memvalue_terms.astype(jnp.bfloat16), "seq", scatter_dimension=1, tiled=True
        ).astype(jnp.float32),
    )
    memory_key_back = memkey_sum.astype(jnp.bfloat16)
    memory_value_back = memvalue_sum.astype(jnp.bfloat16)
    cross_query_back = cross_query_grad.astype(jnp.bfloat16)
    grad_cross_query = weight_grad(first_low, cross_query_back)
    grad_cross_query_bias = token_sum(cross_query_back)
    grad_cross_key = weight_grad(memory, memory_key_back)
    grad_cross_value = weight_grad(memory, memory_value_back)
    grad_cross_value_bias = token_sum(memory_value_back)
    memory_grad = (
        project_back(memory_key_back, cross_key) + project_back(memory_value_back, cross_value)
    ).astype(jnp.bfloat16)
    first_back, grad_first_gain, grad_first_shift = first_pull(
        second_back + project_back(cross_query_back, cross_query)
    )
    self_back = first_back.astype(jnp.bfloat16)
    grad_self_output = weight_grad(self_mixed, self_back)
    grad_output_bias = token_sum(self_back)
    self_mixed_back = project_back(self_back, self_output).astype(jnp.bfloat16)
    query_grad, key_terms, value_terms = attend_backward(
        queries, all_keys, all_values, self_allowed, self_totals, self_mixed_back
    )
    key_sum, value_sum = (
        lax.psum_scatter(
            key_terms.astype(jnp.bfloat16), "seq", scatter_dimension=1, tiled=True
        ).astype(jnp.float32),
        lax.psum_scatter(
            value_terms.astype(jnp.bfloat16), "seq", scatter_dimension=1, tiled=True
        ).astype(jnp.float32),
    )
    key_back = key_sum.astype(jnp.bfloat16)
    value_back = value_sum.astype(jnp.bfloat16)
    query_back = query_grad.astype(jnp.bfloat16)
    grad_self_query = weight_grad(hidden_in, query_back)
    grad_query_bias = token_sum(query_back)
    grad_self_key = weight_grad(hidden_in, key_back)
    grad_self_value = weight_grad(hidden_in, value_back)
    grad_value_bias = token_sum(value_back)
    hidden_grad = (
        first_back
        + project_back(query_back, self_query)
        + project_back(key_back, self_key)
        + project_back(value_back, self_value)
    ).astype(jnp.bfloat16)
    partial_grads = [
        grad_self_query,
        grad_query_bias,
        grad_self_key,
        grad_self_value,
        grad_value_bias,
        grad_self_output,
        grad_output_bias,
        grad_first_gain,
        grad_first_shift,
        grad_cross_query,
        grad_cross_query_bias,
        grad_cross_key,
        grad_cross_value,
        grad_cross_value_bias,
        grad_cross_output,
        grad_cross_output_bias,
        grad_second_gain,
        grad_second_shift,
        grad_ffn_in,
        grad_ffn_in_bias,
        grad_ffn_out,
        grad_ffn_out_bias,
        grad_third_gain,
        grad_third_shift,
    ]
    summed = (
        lax.psum_scatter(
            partial_grads[0].astype(jnp.bfloat16), "dp", scatter_dimension=0, tiled=True
        ).astype(jnp.float32),
        lax.psum_scatter(
            partial_grads[1].astype(jnp.bfloat16), "dp", scatter_dimension=0, tiled=True
        ).astype(jnp.float32),
        lax.psum_scatter(
            partial_grads[2].astype(jnp.bfloat16), "dp", scatter_dimension=0, tiled=True
        ).astype(jnp.float32),
        lax.psum_scatter(
            partial_grads[3].astype(jnp.bfloat16), "dp", scatter_dimension=0, tiled=True
        ).astype(jnp.float32),
        lax.psum_scatter(
            partial_grads[4].astype(jnp.bfloat16), "dp", scatter_dimension=0, tiled=True
        ).astype(jnp.float32),
        lax.psum_scatter(
            partial_grads[5].astype(jnp.bfloat16), "dp", scatter_dimension=0, tiled=True
        ).astype(jnp.float32),
        lax.psum_scatter(
            partial_grads[6].astype(jnp.bfloat16), "dp", scatter_dimension=0, tiled=True
        ).astype(jnp.float32),
        lax.psum_scatter(
            partial_grads[7].astype(jnp.bfloat16), "dp", scatter_dimension=0, tiled=True
        ).astype(jnp.float32),
        lax.psum_scatter(
            partial_grads[8].astype(jnp.bfloat16), "dp", scatter_dimension=0, tiled=True
        ).astype(jnp.float32),
        lax.psum_scatter(
            partial_grads[9].astype(jnp.bfloat16), "dp", scatter_dimension=0, tiled=True
        ).astype(jnp.float32),
        lax.psum_scatter(
            partial_grads[10].astype(jnp.bfloat16), "dp", scatter_dimension=0, tiled=True
        ).astype(jnp.float32),
        lax.psum_scatter(
            partial_grads[11].astype(jnp.bfloat16), "dp", scatter_dimension=0, tiled=True
        ).astype(jnp.float32),
        lax.psum_scatter(
            partial_grads[12].astype(jnp.bfloat16), "dp", scatter_dimension=0, tiled=True
        ).astype(jnp.float32),
        lax.psum_scatter(
            partial_grads[13].astype(jnp.bfloat16), "dp", scatter_dimension=0, tiled=True
        ).astype(jnp.float32),
        lax.psum_scatter(
            partial_grads[14].astype(jnp.bfloat16), "dp", scatter_dimension=0, tiled=True
        ).astype(jnp.float32),
        lax.psum_scatter(
            partial_grads[15].astype(jnp.bfloat16), "dp", scatter_dimension=0, tiled=True
        ).astype(jnp.float32),
        lax.psum_scatter(
            partial_grads[16].astype(jnp.bfloat16), "dp", scatter_dimension=0, tiled=True
        ).astype(jnp.float32),
        lax.psum_scatter(
            partial_grads[17].astype(jnp.bfloat16), "dp", scatter_dimension=0, tiled=True
        ).astype(jnp.float32),
        lax.psum_scatter(
            partial_grads[18].astype(jnp.bfloat16), "dp", scatter_dimension=0, tiled=True
        ).astype(jnp.float32),
        lax.psum_scatter(
            partial_grads[19].astype(jnp.bfloat16), "dp", scatter_dimension=0, tiled=True
        ).astype(jnp.float32),
        lax.psum_scatter(
            partial_grads[20].astype(jnp.bfloat16), "dp", scatter_dimension=0, tiled=True
        ).astype(jnp.float32),
        lax.psum_scatter(
            partial_grads[21].astype(jnp.bfloat16), "dp", scatter_dimension=0, tiled=True
        ).astype(jnp.float32),
        lax.psum_scatter(
            partial_grads[22].astype(jnp.bfloat16), "dp", scatter_dimension=0, tiled=True
        ).astype(jnp.float32),
        lax.psum_scatter(
            partial_grads[23].astype(jnp.bfloat16), "dp", scatter_dimension=0, tiled=True
        ).astype(jnp.float32),
    )
    finished = (
        lax.psum(summed[0].astype(jnp.bfloat16), "seq").astype(jnp.float32),
        lax.psum(summed[1].astype(jnp.bfloat16), "seq").astype(jnp.float32),
        lax.psum(summed[2].astype(jnp.bfloat16), "seq").astype(jnp.float32),
        lax.psum(summed[3].astype(jnp.bfloat16), "seq").astype(jnp.float32),
        lax.psum(summed[4].astype(jnp.bfloat16), "seq").astype(jnp.float32),
        lax.psum(summed[5].astype(jnp.bfloat16), "seq").astype(jnp.float32),
        lax.psum(summed[6].astype(jnp.bfloat16), "seq").astype(jnp.float32),
        lax.psum(summed[7].astype(jnp.bfloat16), "seq").astype(jnp.float32),
        lax.psum(summed[8].astype(jnp.bfloat16), "seq").astype(jnp.float32),
        lax.psum(summed[9].astype(jnp.bfloat16), "seq").astype(jnp.float32),
        lax.psum(summed[10].astype(jnp.bfloat16), "seq").astype(jnp.float32),
        lax.psum(summed[11].astype(jnp.bfloat16), "seq").astype(jnp.float32),
        lax.psum(summed[12].astype(jnp.bfloat16), "seq").astype(jnp.float32),
        lax.psum(summed[13].astype(jnp.bfloat16), "seq").astype(jnp.float32),
        lax.psum(summed[14].astype(jnp.bfloat16), "seq").astype(jnp.float32),
        lax.psum(summed[15].astype(jnp.bfloat16), "seq").astype(jnp.float32),
        lax.psum(summed[16].astype(jnp.bfloat16), "seq").astype(jnp.float32),
        lax.psum(summed[17].astype(jnp.bfloat16), "seq").astype(jnp.float32),
        lax.psum(summed[18].astype(jnp.bfloat16), "seq").astype(jnp.float32),
        lax.psum(summed[19].astype(jnp.bfloat16), "seq").astype(jnp.float32),
        lax.psum(summed[20].astype(jnp.bfloat16), "seq").astype(jnp.float32),
        lax.psum(summed[21].astype(jnp.bfloat16), "seq").astype(jnp.float32),
        lax.psum(summed[22].astype(jnp.bfloat16), "seq").astype(jnp.float32),
        lax.psum(summed[23].astype(jnp.bfloat16), "seq").astype(jnp.float32),
    )
    finished = list(finished)
    return (hidden_out, hidden_grad, memory_grad) + tuple(finished)


def swap(block, ax, bit, size):
    return lax.ppermute(block, ax, [(i, i ^ bit) for i in range(size)])


def two(s, first, second):
    return jnp.where(s == 0, jnp.concatenate([first, second], 0), jnp.concatenate([second, first], 0))


def pick(array, index, axis):
    return lax.dynamic_index_in_dim(array, index, axis, keepdims=False)


def row_in(array, s):
    own = pick(array, s, 0)
    other = swap(pick(array, 1 - s, 0), "seq", 1, 2)
    return two(s, own, other)


def row_out(array, s):
    half = array.shape[0] // 2
    parts = array.reshape(2, half, array.shape[1])
    own = pick(parts, s, 0)
    other = swap(pick(parts, 1 - s, 0), "seq", 1, 2)
    return two(s, own[None], other[None])


def reduce_group(group):
    dp = lax.axis_index("dp")
    c, x, zl, zh = dp % 2, (dp // 2) % 2, (dp // 4) % 2, dp // 8
    rest = group.shape[1:]
    g = group.reshape((2, 2, 2, 2) + rest)
    mine, got = pick(g, c, 3), swap(pick(g, 1 - c, 3), "dp", 1, 16)

    def halves(mine, got, at, axis):
        send = pick(mine, 1 - at, axis) + pick(got, 1 - at, axis)
        keep = pick(mine, at, axis) + pick(got, at, axis)
        return keep, send

    keep, send = halves(mine, got, x, 2)
    got = swap(send, "dp", 2, 16)
    keep, send = halves(keep, got, zl, 1)
    got = swap(send, "dp", 4, 16)
    keep, send = halves(keep, got, zh, 0)
    total = keep + swap(send, "dp", 8, 16)
    return total + swap(total, "seq", 1, 2)


def wgrad(values, gradient):
    return lax.dot_general(values, gradient, (((0,), (0,)), ((), ())), preferred_element_type=jnp.float32)


def back(gradient, weight):
    return lax.dot_general(gradient, weight, (((1,), (1,)), ((), ())), preferred_element_type=jnp.float32)


def col_sum(values):
    return jnp.sum(values.astype(jnp.float32), axis=0)


def whole_rows(
    hidden_in, memory, tgt_segment, src_segment, out_grad,
    self_query, query_bias, self_key, self_value, value_bias, self_output, output_bias,
    first_gain, first_shift,
    cross_query, cross_query_bias, cross_key, cross_value, cross_value_bias, cross_output,
    cross_output_bias, second_gain, second_shift,
    ffn_in, ffn_in_bias, ffn_out, ffn_out_bias, third_gain, third_shift,
):
    f32 = lambda v: v.astype(jnp.float32)
    s = lax.axis_index("seq")
    hidden = row_in(hidden_in, s)
    segs = jnp.stack([tgt_segment, src_segment], -1)
    segs = row_in(segs, s)
    source = row_in(memory, s)
    cotangent = row_in(out_grad, s)
    tgt, src = segs[:, 0], segs[:, 1]
    self_oh, self_mk = masks(tgt, tgt)
    _, cross_mk = masks(tgt, src)
    queries = (project(hidden, self_query) + f32(query_bias)).astype(BF)
    key_rows = project(hidden, self_key).astype(BF)
    value_rows = (project(hidden, self_value) + f32(value_bias)).astype(BF)
    memory_keys = project(source, cross_key).astype(BF)
    memory_values = (project(source, cross_value) + f32(cross_value_bias)).astype(BF)
    self_mixed, self_totals = attend_fwd(queries, key_rows, value_rows, self_oh, self_mk, True, 512)
    self_branch = project(self_mixed, self_output) + f32(output_bias)
    first_norm, first_pull = jax.vjp(layer_norm, f32(hidden) + self_branch, f32(first_gain), f32(first_shift))
    first_low = first_norm.astype(BF)
    cross_queries = (project(first_low, cross_query) + f32(cross_query_bias)).astype(BF)
    cross_mixed, cross_totals = attend_fwd(cross_queries, memory_keys, memory_values, self_oh, cross_mk, False, 512)
    cross_branch = project(cross_mixed, cross_output) + f32(cross_output_bias)
    second_norm, second_pull = jax.vjp(layer_norm, first_norm + cross_branch, f32(second_gain), f32(second_shift))
    second_low = second_norm.astype(BF)
    inner_rows = project(second_low, ffn_in) + f32(ffn_in_bias)
    activation_full, gelu_pull = jax.vjp(exact_gelu, inner_rows)
    activation = activation_full.astype(BF)
    ffn_branch = project(activation, ffn_out) + f32(ffn_out_bias)
    final_norm, third_pull = jax.vjp(layer_norm, second_norm + ffn_branch, f32(third_gain), f32(third_shift))
    hidden_out = row_out(final_norm.astype(BF), s)
    third_back, grad_third_gain, grad_third_shift = third_pull(f32(cotangent))
    ffn_back = third_back.astype(BF)
    pieces = lambda v: v.astype(BF).reshape((16, v.shape[0] // 16) + v.shape[1:])
    total_ffn_out = reduce_group(pieces(wgrad(activation, ffn_back)))
    activation_back = back(ffn_back, ffn_out)
    inner_back = gelu_pull(activation_back)[0].astype(BF)
    total_ffn_in = reduce_group(pieces(wgrad(second_low, inner_back)))
    second_back, grad_second_gain, grad_second_shift = second_pull(third_back + back(inner_back, ffn_in))
    cross_back = second_back.astype(BF)
    cross_mixed_back = back(cross_back, cross_output).astype(BF)
    cross_query_back, memory_key_back, memory_value_back = attend_bwd(
        cross_queries, memory_keys, memory_values, cross_mixed_back, cross_mixed, cross_totals, self_oh, cross_mk, False, 512
    )
    cross_group = jnp.concatenate(
        [
            pieces(wgrad(cross_mixed, cross_back)),
            pieces(wgrad(first_low, cross_query_back)),
            pieces(wgrad(source, memory_key_back)),
            pieces(wgrad(source, memory_value_back)),
        ],
        1,
    )
    total_cross = reduce_group(cross_group)
    memory_grad = row_out((back(memory_key_back, cross_key) + back(memory_value_back, cross_value)).astype(BF), s)
    first_back, grad_first_gain, grad_first_shift = first_pull(second_back + back(cross_query_back, cross_query))
    self_back = first_back.astype(BF)
    self_mixed_back = back(self_back, self_output).astype(BF)
    query_back, key_back, value_back = attend_bwd(
        queries, key_rows, value_rows, self_mixed_back, self_mixed, self_totals, self_oh, self_mk, True, 256
    )
    hidden_grad = row_out(
        (first_back + back(query_back, self_query) + back(key_back, self_key) + back(value_back, self_value)).astype(BF), s
    )
    vectors = [
        col_sum(query_back), col_sum(value_back), col_sum(self_back), grad_first_gain, grad_first_shift,
        col_sum(cross_query_back), col_sum(memory_value_back), col_sum(cross_back),
        grad_second_gain, grad_second_shift, col_sum(ffn_back), grad_third_gain, grad_third_shift,
        col_sum(inner_back),
    ]
    flat = jnp.concatenate([v.astype(BF).reshape(16, -1) for v in vectors], 1)
    flat = jnp.pad(flat, ((0, 0), (0, 16 * 768 - flat.shape[1]))).reshape(16, 16, 768)
    self_group = jnp.concatenate(
        [
            pieces(wgrad(hidden, query_back)),
            pieces(wgrad(hidden, key_back)),
            pieces(wgrad(hidden, value_back)),
            pieces(wgrad(self_mixed, self_back)),
            flat,
        ],
        1,
    )
    total_self = reduce_group(self_group)
    g = lambda total, i: f32(total[48 * i : 48 * i + 48])
    tail = f32(total_self[192:]).reshape(-1)
    v = [tail[48 * i : 48 * i + 48] for i in range(13)] + [tail[48 * 13 : 48 * 13 + 192]]
    return (
        hidden_out, hidden_grad, memory_grad,
        g(total_self, 0), v[0], g(total_self, 1), g(total_self, 2), v[1], g(total_self, 3), v[2], v[3], v[4],
        g(total_cross, 1), v[5], g(total_cross, 2), g(total_cross, 3), v[6], g(total_cross, 0), v[7], v[8], v[9],
        f32(total_ffn_in), v[13], f32(total_ffn_out), v[10], v[11], v[12],
    )


def solution(mesh):
    in_specs = (
        P("dp", "seq", None),
        P("dp", "seq", None),
        P("dp", "seq"),
        P("dp", "seq"),
        P("dp", "seq", None),
        P(),
        P(),
        P(),
        P(),
        P(),
        P(),
        P(),
        P(),
        P(),
        P(),
        P(),
        P(),
        P(),
        P(),
        P(),
        P(),
        P(),
        P(),
        P(),
        P(),
        P(),
        P(),
        P(),
        P(),
    )
    out_specs = (
        P("dp", "seq", None),
        P("dp", "seq", None),
        P("dp", "seq", None),
        P("dp", None),
        P("dp"),
        P("dp", None),
        P("dp", None),
        P("dp"),
        P("dp", None),
        P("dp"),
        P("dp"),
        P("dp"),
        P("dp", None),
        P("dp"),
        P("dp", None),
        P("dp", None),
        P("dp"),
        P("dp", None),
        P("dp"),
        P("dp"),
        P("dp"),
        P("dp", None),
        P("dp"),
        P("dp", None),
        P("dp"),
        P("dp"),
        P("dp"),
    )
    rows_form = mesh.shape["seq"] == 2 and mesh.shape["dp"] == 16

    def on_device(*arrays):
        if rows_form and arrays[0].shape[0] == 2:
            return whole_rows(*arrays)
        return split_rows(*arrays)

    return jax.shard_map(
        on_device, mesh=mesh, in_specs=in_specs, out_specs=out_specs, check_vma=False
    )
```

```python
import functools
import math

import jax
import jax.numpy as jnp
from jax import lax
from jax.experimental import pallas as pl
from jax.experimental.pallas import tpu as pltpu
from jax.sharding import PartitionSpec as P

HEADS = 12
BF=jnp.bfloat16; F32=jnp.float32
BIG=-1e30
def dot(a,b): return jnp.dot(a,b,preferred_element_type=F32)

def lane_low(shape): return lax.broadcasted_iota(jnp.int32, shape, 1) < 64

def masks(seg_q, seg_k):
    T=seg_q.shape[0]; K=seg_k.shape[0]
    r=jnp.arange(64)[:,None]
    oh=((r==seg_q[None,:])).astype(BF)
    c=jnp.arange(128)[None,:]%64
    mk=jnp.where(c<4, jnp.where(c==seg_k[:,None],0.0,BIG), jnp.where(c<7,-1.0,0.0)).astype(BF)
    return oh,mk

def attend_pair(q,k,v,oh,mk,put_total,bq,causal):
    T=q.shape[0]; K=k.shape[0]
    low=lane_low((K,128))
    qT=(q*BF(0.125)).T
    vT=v.T
    ones=jnp.ones((16,K),BF)
    if causal:
        dm=lax.broadcasted_iota(jnp.int32,(bq,bq),0)<=lax.broadcasted_iota(jnp.int32,(bq,bq),1)
    kas=[jnp.where(low,k,mk),jnp.where(low,mk,k)]
    vas=[jnp.concatenate([vT[64*h:64*h+64],ones],0) for h in (0,1)]
    qas=[jnp.concatenate([qT[:64],oh],0),jnp.concatenate([oh,qT[64:]],0)]
    def scores(i,h):
        qa=qas[h][:,i*bq:(i+1)*bq]
        if not causal: return [dot(kas[h],qa)]
        here=jnp.where(dm,dot(kas[h][i*bq:(i+1)*bq],qa),BIG)
        return [dot(kas[h][:i*bq],qa),here] if i else [here]
    def weigh(s):
        m=functools.reduce(jnp.maximum,[jnp.max(x,axis=0,keepdims=True) for x in s])
        return m,[jnp.exp(x-m).astype(BF) for x in s]
    def mix(i,h,m,ps):
        o=None; at=0
        for p in ps:
            t=dot(vas[h][:,at:at+p.shape[0]],p); at+=p.shape[0]
            o=t if o is None else o+t
        l=o[64:65]
        put_total(h,i,m+jnp.log(l))
        return o[:64]/l
    units=[(i,h) for i in range(T//bq) for h in (0,1)]
    os=[]
    s=scores(*units[0]); late=None
    for n,u in enumerate(units):
        coming=scores(*units[n+1]) if n+1<len(units) else None
        m,ps=weigh(s)
        if late is not None: os.append(mix(*late))
        late=(*u,m,ps)
        s=coming
    os.append(mix(*late))
    return [jnp.concatenate(os[2*i:2*i+2],0).T.astype(BF) for i in range(T//bq)]

def split3(x):
    a=x.astype(BF); r=x-a.astype(F32); b=r.astype(BF); c=(r-b.astype(F32)).astype(BF)
    return a,b,c

def attend_pair_back(q,k,v,do,o,totals,oh,mk,acc_ref,put,bk,causal):
    T=q.shape[0]; K=k.shape[0]
    low=lane_low((K,128))
    q=q*BF(0.125)
    qT=q.T; doT=do.T
    kT=k.T
    prodT=(do.astype(F32)*o.astype(F32)).T
    rowi=lax.broadcasted_iota(jnp.int32,(64,T),0)
    one=jnp.full((K,128),-1.0,BF)
    if causal:
        dm=lax.broadcasted_iota(jnp.int32,(bk,bk),0)<=lax.broadcasted_iota(jnp.int32,(bk,bk),1)
    qas=[];das=[]
    for h in (0,1):
        a,b,c=split3(totals[h])
        ohl=jnp.where(rowi==4,a,jnp.where(rowi==5,b,jnp.where(rowi==6,c,oh)))
        D=jnp.sum(prodT[64*h:64*h+64],axis=0,keepdims=True)
        a,b,c=split3(D)
        z=jnp.zeros((64,T),BF)
        dd=jnp.where(rowi==0,a,jnp.where(rowi==1,b,jnp.where(rowi==2,c,z)))
        if h==0:
            qas.append(jnp.concatenate([qT[:64],ohl],0)); das.append(jnp.concatenate([doT[:64],dd],0))
        else:
            qas.append(jnp.concatenate([ohl,qT[64:]],0)); das.append(jnp.concatenate([dd,doT[64:]],0))
    kas=[jnp.where(low,k,mk),jnp.where(low,mk,k)]
    vas=[jnp.where(low,v,one),jnp.where(low,one,v)]
    for j in range(K//bk):
        dks=[];dvs=[]
        q0=j*bk if causal else 0
        ks=slice(j*bk,(j+1)*bk)
        for h in (0,1):
            s=dot(kas[h][ks],qas[h][:,q0:])
            if causal:
                sd=jnp.where(dm,s[:,:bk],BIG)
                s=jnp.concatenate([sd,s[:,bk:]],1) if q0+bk<T else sd
            p=jnp.exp(s)
            dp=dot(vas[h][ks],das[h][:,q0:])
            ds=(p*dp).astype(BF)
            dvs.append(dot(p.astype(BF),do[q0:]))
            dks.append(dot(ds,q[q0:]))
            dqt=dot(kT[64*h:64*h+64,ks],ds)
            if j==0: acc_ref[64*h:64*h+64,:]=dqt
            else: acc_ref[64*h:64*h+64,q0:]+=dqt
        lw=low[:bk]
        put("k",ks,jnp.where(lw,dks[0],dks[1]).astype(BF))
        put("v",ks,jnp.where(lw,dvs[0],dvs[1]).astype(BF))
    put("q",slice(0,T),(acc_ref[...]*0.125).T.astype(BF))

def bwd_kernel(spot_ref,q_ref,k_ref,v_ref,do_ref,o_ref,l_ref,oh_ref,mk_ref,dq_ref,dk_ref,dv_ref,acc_ref,*,bk,causal):
    out={"q":dq_ref,"k":dk_ref,"v":dv_ref}
    def put(name,rows,block): out[name][rows,:]=block
    attend_pair_back(q_ref[...],k_ref[...],v_ref[...],do_ref[...],o_ref[...],[l_ref[0,h:h+1,:] for h in (0,1)],
                     oh_ref[...],mk_ref[...],acc_ref,put,bk,causal)

def attend_bwd(order,spots,q,k,v,do,o,l,oh,mk,causal,bk=256,p0=0,np_=None,moves=()):
    T,D=q.shape; K=k.shape[0]; n=np_ or D//128
    pin=lambda r:pl.BlockSpec((r,128),lambda p,c:(0,p+p0))
    po=lambda r:pl.BlockSpec((r,128),lambda p,c:(0,p))
    return order.call(functools.partial(bwd_kernel,bk=bk,causal=causal),spots,q,k,v,do,o,l,oh,mk,scalars=1,name="attend_bwd",us=4*n,grid=(n,),moves=moves,
        in_specs=[pin(T),pin(K),pin(K),pin(T),pin(T),pl.BlockSpec((1,8,T),lambda p,c:(p+p0,0,0)),pl.BlockSpec((64,T),lambda p,c:(0,0)),pl.BlockSpec((K,128),lambda p,c:(0,0))],
        out_specs=[po(T),po(K),po(K)],
        out_shape=[jax.ShapeDtypeStruct((T,128*n),BF),jax.ShapeDtypeStruct((K,128*n),BF),jax.ShapeDtypeStruct((K,128*n),BF)],
        scratch_shapes=[pltpu.VMEM((128,T),F32)])


def project(values, weight):
    return jnp.dot(values, weight, preferred_element_type=jnp.float32)


def project_back(gradient, weight):
    return jnp.einsum("rte,de->rtd", gradient, weight, preferred_element_type=jnp.float32)


def weight_grad(values, gradient):
    return jnp.einsum("rtd,rte->de", values, gradient, preferred_element_type=jnp.float32)


def token_sum(gradient):
    return jnp.sum(gradient.astype(jnp.float32), axis=(0, 1))


def layer_norm(values, norm_gain, norm_shift):
    center = values - jnp.mean(values, axis=-1, keepdims=True)
    spread = jnp.mean(center * center, axis=-1, keepdims=True)
    return center * lax.rsqrt(spread + 1e-05) * norm_gain + norm_shift


def exact_gelu(values):
    return jax.nn.gelu(values, approximate=False)


def split_heads(values):
    return values.reshape(values.shape[0], values.shape[1], HEADS, values.shape[2] // HEADS)


def merge_heads(values):
    return values.reshape(values.shape[0], values.shape[1], values.shape[2] * values.shape[3])


def masked_scores(queries, key_rows, allowed):
    raw_scores = jnp.einsum(
        "rqhd,rkhd->rhqk",
        split_heads(queries),
        split_heads(key_rows),
        preferred_element_type=jnp.float32,
    )
    factor = 1.0 / math.sqrt(queries.shape[2] // HEADS)
    return jnp.where(allowed[:, None], raw_scores * factor, -1e30)


def attend_forward(queries, key_rows, value_rows, allowed):
    scores = masked_scores(queries, key_rows, allowed)
    highest = jnp.max(scores, axis=-1, keepdims=True)
    powers = jnp.exp(scores - highest)
    totals = jnp.sum(powers, axis=-1, keepdims=True)
    weights = (powers / totals).astype(jnp.bfloat16)
    mixed_heads = jnp.einsum(
        "rhqk,rkhd->rqhd", weights, split_heads(value_rows), preferred_element_type=jnp.float32
    )
    return (merge_heads(mixed_heads).astype(jnp.bfloat16), highest + jnp.log(totals))


def attend_backward(queries, key_rows, value_rows, allowed, log_totals, mixed_grad):
    scores = masked_scores(queries, key_rows, allowed)
    weights = jnp.exp(scores - log_totals)
    grad_heads = split_heads(mixed_grad)
    value_terms = jnp.einsum(
        "rhqk,rqhd->rkhd",
        weights.astype(jnp.bfloat16),
        grad_heads,
        preferred_element_type=jnp.float32,
    )
    weight_grads = jnp.einsum(
        "rqhd,rkhd->rhqk", grad_heads, split_heads(value_rows), preferred_element_type=jnp.float32
    )
    inner_sum = jnp.sum(weights * weight_grads, axis=-1, keepdims=True)
    factor = 1.0 / math.sqrt(queries.shape[2] // HEADS)
    score_grads = (weights * (weight_grads - inner_sum) * factor).astype(jnp.bfloat16)
    query_grads = jnp.einsum(
        "rhqk,rkhd->rqhd", score_grads, split_heads(key_rows), preferred_element_type=jnp.float32
    )
    key_terms = jnp.einsum(
        "rhqk,rqhd->rkhd", score_grads, split_heads(queries), preferred_element_type=jnp.float32
    )
    return (merge_heads(query_grads), merge_heads(key_terms), merge_heads(value_terms))


def split_rows(
    hidden_in,
    memory,
    tgt_segment,
    src_segment,
    out_grad,
    self_query,
    query_bias,
    self_key,
    self_value,
    value_bias,
    self_output,
    output_bias,
    first_gain,
    first_shift,
    cross_query,
    cross_query_bias,
    cross_key,
    cross_value,
    cross_value_bias,
    cross_output,
    cross_output_bias,
    second_gain,
    second_shift,
    ffn_in,
    ffn_in_bias,
    ffn_out,
    ffn_out_bias,
    third_gain,
    third_shift,
):
    tokens = hidden_in.shape[1]
    queries = (project(hidden_in, self_query) + query_bias.astype(jnp.float32)).astype(jnp.bfloat16)
    key_rows = project(hidden_in, self_key).astype(jnp.bfloat16)
    value_rows = (project(hidden_in, self_value) + value_bias.astype(jnp.float32)).astype(
        jnp.bfloat16
    )
    target_ids = tgt_segment.astype(jnp.bfloat16)
    all_keys, all_values, all_target = (
        lax.all_gather(key_rows, "seq", axis=1, tiled=True),
        lax.all_gather(value_rows, "seq", axis=1, tiled=True),
        lax.all_gather(target_ids, "seq", axis=1, tiled=True),
    )
    memory_keys = project(memory, cross_key).astype(jnp.bfloat16)
    memory_values = (project(memory, cross_value) + cross_value_bias.astype(jnp.float32)).astype(
        jnp.bfloat16
    )
    all_memkeys, all_memvalues, all_source = (
        lax.all_gather(memory_keys, "seq", axis=1, tiled=True),
        lax.all_gather(memory_values, "seq", axis=1, tiled=True),
        lax.all_gather(src_segment.astype(jnp.bfloat16), "seq", axis=1, tiled=True),
    )
    offset = lax.axis_index("seq") * tokens
    query_places = offset + jnp.arange(tokens, dtype=jnp.int32)
    key_places = jnp.arange(all_keys.shape[1], dtype=jnp.int32)
    self_allowed = (target_ids[:, :, None] == all_target[:, None, :]) & (
        query_places[:, None] >= key_places[None, :]
    )[None]
    cross_allowed = target_ids[:, :, None] == all_source[:, None, :]
    self_mixed, self_totals = attend_forward(queries, all_keys, all_values, self_allowed)
    self_branch = project(self_mixed, self_output) + output_bias.astype(jnp.float32)
    first_norm, first_pull = jax.vjp(
        layer_norm,
        hidden_in.astype(jnp.float32) + self_branch,
        first_gain.astype(jnp.float32),
        first_shift.astype(jnp.float32),
    )
    first_low = first_norm.astype(jnp.bfloat16)
    cross_queries = (project(first_low, cross_query) + cross_query_bias.astype(jnp.float32)).astype(
        jnp.bfloat16
    )
    cross_mixed, cross_totals = attend_forward(
        cross_queries, all_memkeys, all_memvalues, cross_allowed
    )
    cross_branch = project(cross_mixed, cross_output) + cross_output_bias.astype(jnp.float32)
    second_norm, second_pull = jax.vjp(
        layer_norm,
        first_norm + cross_branch,
        second_gain.astype(jnp.float32),
        second_shift.astype(jnp.float32),
    )
    second_low = second_norm.astype(jnp.bfloat16)
    inner_rows = project(second_low, ffn_in) + ffn_in_bias.astype(jnp.float32)
    activation_full, gelu_pull = jax.vjp(exact_gelu, inner_rows)
    activation = activation_full.astype(jnp.bfloat16)
    ffn_branch = project(activation, ffn_out) + ffn_out_bias.astype(jnp.float32)
    final_norm, third_pull = jax.vjp(
        layer_norm,
        second_norm + ffn_branch,
        third_gain.astype(jnp.float32),
        third_shift.astype(jnp.float32),
    )
    hidden_out = final_norm.astype(jnp.bfloat16)
    third_back, grad_third_gain, grad_third_shift = third_pull(out_grad.astype(jnp.float32))
    ffn_back = third_back.astype(jnp.bfloat16)
    grad_ffn_out = weight_grad(activation, ffn_back)
    grad_ffn_out_bias = token_sum(ffn_back)
    activation_back = project_back(ffn_back, ffn_out)
    inner_back = gelu_pull(activation_back)[0].astype(jnp.bfloat16)
    grad_ffn_in = weight_grad(second_low, inner_back)
    grad_ffn_in_bias = token_sum(inner_back)
    second_back, grad_second_gain, grad_second_shift = second_pull(
        third_back + project_back(inner_back, ffn_in)
    )
    cross_back = second_back.astype(jnp.bfloat16)
    grad_cross_output = weight_grad(cross_mixed, cross_back)
    grad_cross_output_bias = token_sum(cross_back)
    cross_mixed_back = project_back(cross_back, cross_output).astype(jnp.bfloat16)
    cross_query_grad, memkey_terms, memvalue_terms = attend_backward(
        cross_queries, all_memkeys, all_memvalues, cross_allowed, cross_totals, cross_mixed_back
    )
    memkey_sum, memvalue_sum = (
        lax.psum_scatter(
            memkey_terms.astype(jnp.bfloat16), "seq", scatter_dimension=1, tiled=True
        ).astype(jnp.float32),
        lax.psum_scatter(
            memvalue_terms.astype(jnp.bfloat16), "seq", scatter_dimension=1, tiled=True
        ).astype(jnp.float32),
    )
    memory_key_back = memkey_sum.astype(jnp.bfloat16)
    memory_value_back = memvalue_sum.astype(jnp.bfloat16)
    cross_query_back = cross_query_grad.astype(jnp.bfloat16)
    grad_cross_query = weight_grad(first_low, cross_query_back)
    grad_cross_query_bias = token_sum(cross_query_back)
    grad_cross_key = weight_grad(memory, memory_key_back)
    grad_cross_value = weight_grad(memory, memory_value_back)
    grad_cross_value_bias = token_sum(memory_value_back)
    memory_grad = (
        project_back(memory_key_back, cross_key) + project_back(memory_value_back, cross_value)
    ).astype(jnp.bfloat16)
    first_back, grad_first_gain, grad_first_shift = first_pull(
        second_back + project_back(cross_query_back, cross_query)
    )
    self_back = first_back.astype(jnp.bfloat16)
    grad_self_output = weight_grad(self_mixed, self_back)
    grad_output_bias = token_sum(self_back)
    self_mixed_back = project_back(self_back, self_output).astype(jnp.bfloat16)
    query_grad, key_terms, value_terms = attend_backward(
        queries, all_keys, all_values, self_allowed, self_totals, self_mixed_back
    )
    key_sum, value_sum = (
        lax.psum_scatter(
            key_terms.astype(jnp.bfloat16), "seq", scatter_dimension=1, tiled=True
        ).astype(jnp.float32),
        lax.psum_scatter(
            value_terms.astype(jnp.bfloat16), "seq", scatter_dimension=1, tiled=True
        ).astype(jnp.float32),
    )
    key_back = key_sum.astype(jnp.bfloat16)
    value_back = value_sum.astype(jnp.bfloat16)
    query_back = query_grad.astype(jnp.bfloat16)
    grad_self_query = weight_grad(hidden_in, query_back)
    grad_query_bias = token_sum(query_back)
    grad_self_key = weight_grad(hidden_in, key_back)
    grad_self_value = weight_grad(hidden_in, value_back)
    grad_value_bias = token_sum(value_back)
    hidden_grad = (
        first_back
        + project_back(query_back, self_query)
        + project_back(key_back, self_key)
        + project_back(value_back, self_value)
    ).astype(jnp.bfloat16)
    partial_grads = [
        grad_self_query,
        grad_query_bias,
        grad_self_key,
        grad_self_value,
        grad_value_bias,
        grad_self_output,
        grad_output_bias,
        grad_first_gain,
        grad_first_shift,
        grad_cross_query,
        grad_cross_query_bias,
        grad_cross_key,
        grad_cross_value,
        grad_cross_value_bias,
        grad_cross_output,
        grad_cross_output_bias,
        grad_second_gain,
        grad_second_shift,
        grad_ffn_in,
        grad_ffn_in_bias,
        grad_ffn_out,
        grad_ffn_out_bias,
        grad_third_gain,
        grad_third_shift,
    ]
    summed = (
        lax.psum_scatter(
            partial_grads[0].astype(jnp.bfloat16), "dp", scatter_dimension=0, tiled=True
        ).astype(jnp.float32),
        lax.psum_scatter(
            partial_grads[1].astype(jnp.bfloat16), "dp", scatter_dimension=0, tiled=True
        ).astype(jnp.float32),
        lax.psum_scatter(
            partial_grads[2].astype(jnp.bfloat16), "dp", scatter_dimension=0, tiled=True
        ).astype(jnp.float32),
        lax.psum_scatter(
            partial_grads[3].astype(jnp.bfloat16), "dp", scatter_dimension=0, tiled=True
        ).astype(jnp.float32),
        lax.psum_scatter(
            partial_grads[4].astype(jnp.bfloat16), "dp", scatter_dimension=0, tiled=True
        ).astype(jnp.float32),
        lax.psum_scatter(
            partial_grads[5].astype(jnp.bfloat16), "dp", scatter_dimension=0, tiled=True
        ).astype(jnp.float32),
        lax.psum_scatter(
            partial_grads[6].astype(jnp.bfloat16), "dp", scatter_dimension=0, tiled=True
        ).astype(jnp.float32),
        lax.psum_scatter(
            partial_grads[7].astype(jnp.bfloat16), "dp", scatter_dimension=0, tiled=True
        ).astype(jnp.float32),
        lax.psum_scatter(
            partial_grads[8].astype(jnp.bfloat16), "dp", scatter_dimension=0, tiled=True
        ).astype(jnp.float32),
        lax.psum_scatter(
            partial_grads[9].astype(jnp.bfloat16), "dp", scatter_dimension=0, tiled=True
        ).astype(jnp.float32),
        lax.psum_scatter(
            partial_grads[10].astype(jnp.bfloat16), "dp", scatter_dimension=0, tiled=True
        ).astype(jnp.float32),
        lax.psum_scatter(
            partial_grads[11].astype(jnp.bfloat16), "dp", scatter_dimension=0, tiled=True
        ).astype(jnp.float32),
        lax.psum_scatter(
            partial_grads[12].astype(jnp.bfloat16), "dp", scatter_dimension=0, tiled=True
        ).astype(jnp.float32),
        lax.psum_scatter(
            partial_grads[13].astype(jnp.bfloat16), "dp", scatter_dimension=0, tiled=True
        ).astype(jnp.float32),
        lax.psum_scatter(
            partial_grads[14].astype(jnp.bfloat16), "dp", scatter_dimension=0, tiled=True
        ).astype(jnp.float32),
        lax.psum_scatter(
            partial_grads[15].astype(jnp.bfloat16), "dp", scatter_dimension=0, tiled=True
        ).astype(jnp.float32),
        lax.psum_scatter(
            partial_grads[16].astype(jnp.bfloat16), "dp", scatter_dimension=0, tiled=True
        ).astype(jnp.float32),
        lax.psum_scatter(
            partial_grads[17].astype(jnp.bfloat16), "dp", scatter_dimension=0, tiled=True
        ).astype(jnp.float32),
        lax.psum_scatter(
            partial_grads[18].astype(jnp.bfloat16), "dp", scatter_dimension=0, tiled=True
        ).astype(jnp.float32),
        lax.psum_scatter(
            partial_grads[19].astype(jnp.bfloat16), "dp", scatter_dimension=0, tiled=True
        ).astype(jnp.float32),
        lax.psum_scatter(
            partial_grads[20].astype(jnp.bfloat16), "dp", scatter_dimension=0, tiled=True
        ).astype(jnp.float32),
        lax.psum_scatter(
            partial_grads[21].astype(jnp.bfloat16), "dp", scatter_dimension=0, tiled=True
        ).astype(jnp.float32),
        lax.psum_scatter(
            partial_grads[22].astype(jnp.bfloat16), "dp", scatter_dimension=0, tiled=True
        ).astype(jnp.float32),
        lax.psum_scatter(
            partial_grads[23].astype(jnp.bfloat16), "dp", scatter_dimension=0, tiled=True
        ).astype(jnp.float32),
    )
    finished = (
        lax.psum(summed[0].astype(jnp.bfloat16), "seq").astype(jnp.float32),
        lax.psum(summed[1].astype(jnp.bfloat16), "seq").astype(jnp.float32),
        lax.psum(summed[2].astype(jnp.bfloat16), "seq").astype(jnp.float32),
        lax.psum(summed[3].astype(jnp.bfloat16), "seq").astype(jnp.float32),
        lax.psum(summed[4].astype(jnp.bfloat16), "seq").astype(jnp.float32),
        lax.psum(summed[5].astype(jnp.bfloat16), "seq").astype(jnp.float32),
        lax.psum(summed[6].astype(jnp.bfloat16), "seq").astype(jnp.float32),
        lax.psum(summed[7].astype(jnp.bfloat16), "seq").astype(jnp.float32),
        lax.psum(summed[8].astype(jnp.bfloat16), "seq").astype(jnp.float32),
        lax.psum(summed[9].astype(jnp.bfloat16), "seq").astype(jnp.float32),
        lax.psum(summed[10].astype(jnp.bfloat16), "seq").astype(jnp.float32),
        lax.psum(summed[11].astype(jnp.bfloat16), "seq").astype(jnp.float32),
        lax.psum(summed[12].astype(jnp.bfloat16), "seq").astype(jnp.float32),
        lax.psum(summed[13].astype(jnp.bfloat16), "seq").astype(jnp.float32),
        lax.psum(summed[14].astype(jnp.bfloat16), "seq").astype(jnp.float32),
        lax.psum(summed[15].astype(jnp.bfloat16), "seq").astype(jnp.float32),
        lax.psum(summed[16].astype(jnp.bfloat16), "seq").astype(jnp.float32),
        lax.psum(summed[17].astype(jnp.bfloat16), "seq").astype(jnp.float32),
        lax.psum(summed[18].astype(jnp.bfloat16), "seq").astype(jnp.float32),
        lax.psum(summed[19].astype(jnp.bfloat16), "seq").astype(jnp.float32),
        lax.psum(summed[20].astype(jnp.bfloat16), "seq").astype(jnp.float32),
        lax.psum(summed[21].astype(jnp.bfloat16), "seq").astype(jnp.float32),
        lax.psum(summed[22].astype(jnp.bfloat16), "seq").astype(jnp.float32),
        lax.psum(summed[23].astype(jnp.bfloat16), "seq").astype(jnp.float32),
    )
    finished = list(finished)
    return (hidden_out, hidden_grad, memory_grad) + tuple(finished)


def nt(a, b):
    return lax.dot_general(a, b, (((1,), (1,)), ((), ())), preferred_element_type=F32)


def tn(a, b):
    return lax.dot_general(a, b, (((0,), (0,)), ((), ())), preferred_element_type=F32)


def mean(v):
    return jnp.mean(v, axis=-1, keepdims=True)


def norm_stats(v):
    center = v - mean(v)
    r = lax.rsqrt(mean(center * center) + 1e-05)
    return center * r, r


def norm_back(e, n, r, gain):
    u = e * gain
    return r * (u - mean(u) - n * mean(u * n))


def sums(v):
    return jnp.sum(v, axis=0, keepdims=True)


TAIL = (0.24251982196758853, 0.24429374300098905, 0.2054730204591465, 0.24507896666845616,
        -0.08230106829392796, 0.3798837300580386, -0.30809352249830146, 0.07314529579847638)


def gelu_pair(x):
    d = 1.0 + (0.43 * math.sqrt(0.5)) * jnp.abs(x)
    t = pl.reciprocal(d, approx=True)
    t = t * (2.0 - d * t)
    tail = 0.5 * TAIL[-1]
    for c in TAIL[-2::-1]:
        tail = tail * t + 0.5 * c
    bell = jnp.exp(-0.5 * x * x)
    tail = tail * t * bell
    phi = jnp.where(x >= 0, 1.0 - tail, tail)
    return x * phi, phi + x * bell * (1.0 / math.sqrt(2.0 * math.pi))


def full(shape):
    return pl.BlockSpec(shape, lambda *_: (0,) * len(shape), pipeline_mode=pl.Buffered(1))


def still(shape):
    return pl.BlockSpec(shape, lambda *_: (0,) * len(shape))


def rows_of(bt, width):
    return pl.BlockSpec((bt, width), lambda i: (i, 0))


class Order:
    def __init__(self):
        self.last = []

    def call(self, kernel, *args, name, us, grid, in_specs, out_specs, out_shape, scalars=0, scratch_shapes=(), moves=()):
        at, after, n, n_out = len(args), len(self.last), len(moves), len(out_specs)
        flat = [array for pair in moves for array in pair]
        hbm = pl.BlockSpec(memory_space=pl.ANY)

        def run(*refs):
            outs = at + 2 * n + after
            plain = refs[:at] + refs[outs : outs + n_out]
            if not n:
                return kernel(*plain, *refs[outs + n_out :])
            s = refs[0][4]
            buffer, sem = refs[-2:]
            reads, writes = [], []
            for i in range(n):
                target = refs[outs + n_out + i]
                for j, place in enumerate((s, 1 - s)):
                    slot = 2 * i + j
                    reads.append(pltpu.make_async_copy(refs[at + slot], buffer.at[slot], sem.at[0, slot]))
                    writes.append(pltpu.make_async_copy(buffer.at[slot], target.at[place], sem.at[1, slot]))

            @pl.when(pl.program_id(0) == 0)
            def _():
                for c in reads:
                    c.start()

            @pl.when(pl.program_id(0) == 1)
            def _():
                for r, w in zip(reads, writes):
                    r.wait()
                    w.start()

            kernel(*plain, *refs[outs + n_out + n : -2])

            @pl.when(pl.program_id(0) == grid[0] - 1)
            def _():
                for c in writes:
                    c.wait()

        more = [pltpu.VMEM((2 * n, *flat[0].shape), BF), pltpu.SemaphoreType.DMA((2, 2 * n))] if n else []
        out = pl.pallas_call(
            run, name=name, out_shape=list(out_shape) + [shaped(2, *pair[0].shape) for pair in moves],
            grid_spec=pltpu.PrefetchScalarGridSpec(
                num_scalar_prefetch=scalars, grid=grid, in_specs=list(in_specs) + [hbm] * (2 * n + after),
                out_specs=list(out_specs) + [hbm] * n, scratch_shapes=list(scratch_shapes) + more),
            cost_estimate=pl.CostEstimate(flops=0, bytes_accessed=int(us * 7.2e6), transcendentals=0),
            compiler_params=pltpu.CompilerParams(vmem_limit_bytes=60 * 2**20),
        )(*args, *flat, *self.last)
        self.last = [out[n_out - 1]]
        return out


def shaped(*shape, dtype=BF):
    return jax.ShapeDtypeStruct(shape, dtype)


(V_QB, V_VB, V_OB, V_G1, V_B1, V_CQB, V_CVB, V_COB, V_G2, V_B2, V_FOB, V_G3, V_B3) = range(13)


def near_kernel(spot_ref, x_ref, y_ref, vec_ref, wq_ref, wk_ref, wv_ref, uk_ref, uv_ref, q_ref, k_ref, v_ref, mk_ref, mv_ref):
    x, y = x_ref[0], y_ref[0]
    q_ref[...] = (dot(x, wq_ref[...]) + vec_ref[V_QB : V_QB + 1, :]).astype(BF)
    k_ref[...] = dot(x, wk_ref[...]).astype(BF)
    v_ref[...] = (dot(x, wv_ref[...]) + vec_ref[V_VB : V_VB + 1, :]).astype(BF)
    mk_ref[...] = dot(y, uk_ref[...]).astype(BF)
    mv_ref[...] = (dot(y, uv_ref[...]) + vec_ref[V_CVB : V_CVB + 1, :]).astype(BF)


def project_near(order, spots, hidden_in, memory, vec, weights):
    half, D = hidden_in.shape[1:]
    x = pl.BlockSpec((1, half, D), lambda i, p: (p[4], 0, 0))
    return order.call(
        near_kernel, spots, hidden_in, memory, vec, *weights, scalars=1, name="project_near", us=8, grid=(1,),
        in_specs=[x, x, full(vec.shape)] + [full((D, D))] * 5,
        out_specs=[still((half, D))] * 5, out_shape=[shaped(half, D)] * 5)


class Loads:
    def __init__(self, sem):
        self.sem = sem
        self.copies = []

    def add(self, src, dst):
        self.copies.append(pltpu.make_async_copy(src, dst, self.sem.at[len(self.copies)]))
        return self.copies[-1]


def columns(p, width=128):
    return pl.ds(pl.multiple_of(p * width, width), width)


def self_kernel(spot_ref, vec_ref, oh_ref, mk_ref, hin_ref, hgot_ref, qn_ref, kn_ref, vn_ref, wq_ref, wk_ref, wv_ref, wo_ref, wc_ref,
                l_ref, n_ref, r_ref, low_ref, cq_ref, h_out, q_out, k_out, v_out, m_out,
                h_s, q_s, k_s, v_s, m_s, wq_s, wk_s, wv_s, wo_s, wc_s, sem, *, pairs, bq):
    v = lambda i: vec_ref[i : i + 1, :]
    at = pl.program_id(0)
    half = hgot_ref.shape[0]
    s = spot_ref[4]
    near = pl.ds(pl.multiple_of(s * half, half), half)
    far = pl.ds(pl.multiple_of((1 - s) * half, half), half)
    loads = Loads(sem)
    got = loads.add(hgot_ref, h_s.at[far])
    in_q, in_k, in_v = loads.add(wq_ref, wq_s), loads.add(wk_ref, wk_s), loads.add(wv_ref, wv_s)
    own = [loads.add(hin_ref.at[s], h_s.at[near])]
    own += [loads.add(a, b.at[near]) for a, b in ((qn_ref, q_s), (kn_ref, k_s), (vn_ref, v_s))]
    later = [loads.add(wo_ref, wo_s), loads.add(wc_ref, wc_s)]
    outs = [loads.add(a, b) for a, b in ((h_s, h_out), (q_s, q_out), (k_s, k_out), (v_s, v_out))]
    mixed_out = loads.add(m_s, m_out)

    @pl.when(at == 0)
    def _():
        for c in (got, in_q, in_k, in_v, *own, *later):
            c.start()
        got.wait()
        x = h_s[far, :]
        in_q.wait()
        q_s[far, :] = (dot(x, wq_s[...]) + v(V_QB)).astype(BF)
        in_k.wait()
        k_s[far, :] = dot(x, wk_s[...]).astype(BF)
        in_v.wait()
        v_s[far, :] = (dot(x, wv_s[...]) + v(V_VB)).astype(BF)
        for c in own:
            c.wait()
        for c in outs:
            c.start()

    @pl.when((at > 0) & (at <= pairs))
    def _():
        cols = columns(at - 1)

        def put_total(h, i, row):
            l_ref[0, h : h + 1, i * bq : (i + 1) * bq] = row

        blocks = attend_pair(q_s[:, cols], k_s[:, cols], v_s[:, cols], oh_ref[...], mk_ref[...], put_total, bq, True)
        for i, b in enumerate(blocks):
            m_s[i * bq : (i + 1) * bq, cols] = b

    @pl.when(at == pairs + 1)
    def _():
        mixed_out.start()
        for c in later:
            c.wait()

    @pl.when(at > pairs)
    def _():
        rows = pl.ds(pl.multiple_of((at - pairs - 1) * half, half), half)
        x = h_s[rows, :].astype(F32) + (dot(m_s[rows, :], wo_s[...]) + v(V_OB))
        n, r = norm_stats(x)
        n_ref[...] = n
        r_ref[...] = r
        low = (n * v(V_G1) + v(V_B1)).astype(BF)
        low_ref[...] = low
        cq_ref[...] = (dot(low, wc_s[...]) + v(V_CQB)).astype(BF)

    @pl.when(at == pairs + 2)
    def _():
        for c in (*outs, mixed_out):
            c.wait()


def self_forward(order, spots, vec, oh, mk, hidden_in, hidden_got, near, weights):
    half, D = hidden_got.shape
    T, pairs = 2 * half, D // 128
    token = lambda width: pl.BlockSpec((half, width), lambda i, p: (jnp.maximum(i - pairs - 1, 0), 0))
    hbm = pl.BlockSpec(memory_space=pl.ANY)
    return order.call(
        functools.partial(self_kernel, pairs=pairs, bq=512), spots, vec, oh, mk, hidden_in, hidden_got, *near, *weights,
        scalars=1, name="self_forward", us=25, grid=(pairs + 3,),
        in_specs=[full(a.shape) for a in (vec, oh, mk)] + [hbm] * 10,
        out_specs=[pl.BlockSpec((1, 8, T), lambda i, p: (jnp.clip(i - 1, 0, pairs - 1), 0, 0)),
                   token(D), token(1), token(D), token(D)] + [hbm] * 5,
        out_shape=[shaped(pairs, 8, T, dtype=F32), shaped(T, D, dtype=F32), shaped(T, 1, dtype=F32), shaped(T, D), shaped(T, D)]
        + [shaped(T, D)] * 5,
        scratch_shapes=[pltpu.VMEM((T, D), BF)] * 5 + [pltpu.VMEM((D, D), BF)] * 5 + [pltpu.SemaphoreType.DMA((15,))])


def cross_kernel(spot_ref, vec_ref, oh_ref, mask_ref, cq_ref, min_ref, mgot_ref, kn_ref, vn_ref, uk_ref, uv_ref,
                 l_ref, m_out, k_out, v_out, c_out, m_s, k_s, v_s, q_s, c_s, uk_s, uv_s, sem, *, pairs, bq):
    at = pl.program_id(0)
    half = mgot_ref.shape[0]
    s = spot_ref[4]
    near = pl.ds(pl.multiple_of(s * half, half), half)
    far = pl.ds(pl.multiple_of((1 - s) * half, half), half)
    loads = Loads(sem)
    got = loads.add(mgot_ref, m_s.at[far])
    in_k, in_v = loads.add(uk_ref, uk_s), loads.add(uv_ref, uv_s)
    own = [loads.add(min_ref.at[s], m_s.at[near]), loads.add(cq_ref, q_s)]
    own += [loads.add(kn_ref, k_s.at[near]), loads.add(vn_ref, v_s.at[near])]
    outs = [loads.add(a, b) for a, b in ((m_s, m_out), (k_s, k_out), (v_s, v_out))]

    @pl.when(at == 0)
    def _():
        for c in (got, in_k, in_v, *own):
            c.start()
        got.wait()
        x = m_s[far, :]
        in_k.wait()
        k_s[far, :] = dot(x, uk_s[...]).astype(BF)
        in_v.wait()
        v_s[far, :] = (dot(x, uv_s[...]) + vec_ref[V_CVB : V_CVB + 1, :]).astype(BF)
        for c in own:
            c.wait()
        for c in outs:
            c.start()

    @pl.when(at > 0)
    def _():
        cols = columns(at - 1)

        def put_total(h, i, row):
            l_ref[0, h : h + 1, i * bq : (i + 1) * bq] = row

        blocks = attend_pair(q_s[:, cols], k_s[:, cols], v_s[:, cols], oh_ref[...], mask_ref[...], put_total, bq, False)
        for i, b in enumerate(blocks):
            c_out[i * bq : (i + 1) * bq, :] = b

    @pl.when(at == pairs)
    def _():
        for c in outs:
            c.wait()


def cross_forward(order, spots, vec, oh, mask, cq, memory, memory_got, near, weights):
    half, D = memory_got.shape
    T, pairs = 2 * half, D // 128
    hbm = pl.BlockSpec(memory_space=pl.ANY)
    pair = lambda i: jnp.maximum(i - 1, 0)
    return order.call(
        functools.partial(cross_kernel, pairs=pairs, bq=512), spots, vec, oh, mask, cq, memory, memory_got, *near, *weights,
        scalars=1, name="cross_forward", us=23, grid=(pairs + 1,),
        in_specs=[full(a.shape) for a in (vec, oh, mask)] + [hbm] * 7,
        out_specs=[pl.BlockSpec((1, 8, T), lambda i, p: (pair(i), 0, 0))] + [hbm] * 3
        + [pl.BlockSpec((T, 128), lambda i, p: (0, pair(i)))],
        out_shape=[shaped(pairs, 8, T, dtype=F32)] + [shaped(T, D)] * 4,
        scratch_shapes=[pltpu.VMEM((T, D), BF)] * 4 + [pltpu.VMEM((16, 128), BF)] + [pltpu.VMEM((D, D), BF)] * 2
        + [pltpu.SemaphoreType.DMA((10,))])


def ffn_kernel(spot_ref, vec_ref, bin_ref, n1_ref, cm_ref, og_ref, oggot_ref, wco_ref, win_ref, wout_ref,
               own_ref, other_ref, sb_ref, cmb_ref, vo_ref, vi_ref, all_ref,
               act_s, ib_s, cm_s, og_s, wco_s, win_s, wout_s, fb_s, low_s, cb_s, stage_s, stage_sem, sem, *, parts):
    v = lambda i: vec_ref[i : i + 1, :]
    t = pl.program_id(0)
    half, D = oggot_ref.shape
    s = spot_ref[4]
    loads = Loads(sem)
    in_cm, in_co = loads.add(cm_ref, cm_s), loads.add(wco_ref, wco_s)
    in_up, in_down = loads.add(win_ref, win_s), loads.add(wout_ref, wout_s)
    in_og = [loads.add(og_ref.at[s], og_s.at[s]), loads.add(oggot_ref, og_s.at[1 - s])]

    def need(*copies):
        @pl.when(t == 0)
        def _():
            for c in copies:
                c.wait()

    @pl.when(t == 0)
    def _():
        for c in loads.copies:
            c.start()
        vo_ref[...] = jnp.zeros_like(vo_ref)
        vi_ref[...] = jnp.zeros_like(vi_ref)

    @pl.when(t < 2)
    def _():
        need(in_cm, in_co)
        rows = pl.ds(pl.multiple_of(t * half, half), half)
        first = n1_ref[...] * v(V_G1) + v(V_B1)
        n2, r2 = norm_stats(first + (dot(cm_s[rows, :], wco_s[...]) + v(V_COB)))
        second = n2 * v(V_G2) + v(V_B2)
        low = second.astype(BF)
        low_s[rows, :] = low
        need(in_up, in_down, *in_og)
        width = win_s.shape[1] // parts
        branch = None
        for c in range(parts):
            cols = slice(c * width, (c + 1) * width)
            act, slope = gelu_pair(dot(low, win_s[:, cols]) + bin_ref[:, cols])
            ib_s[rows, cols] = slope.astype(BF)
            act = act.astype(BF)
            act_s[rows, cols] = act
            term = dot(act, wout_s[cols, :])
            branch = term if branch is None else branch + term
        n3, r3 = norm_stats(second + (branch + v(V_FOB)))
        ho = (n3 * v(V_G3) + v(V_B3)).astype(BF)

        @pl.when(t == s)
        def _():
            own_ref[...] = ho

        @pl.when(t != s)
        def _():
            other_ref[...] = ho

        e = og_s[t].astype(F32)
        third = norm_back(e, n3, r3, v(V_G3))
        fb = third.astype(BF)
        fb_s[rows, :] = fb
        vo_ref[0:1, :] += sums(e * n3)
        vo_ref[1:2, :] += sums(e)
        vo_ref[2:3, :] += sums(fb.astype(F32))
        e = third
        for c in range(parts):
            cols = slice(c * width, (c + 1) * width)
            ib = (nt(fb, wout_s[cols, :]) * ib_s[rows, cols].astype(F32)).astype(BF)
            ib_s[rows, cols] = ib
            vi_ref[:, cols] += sums(ib.astype(F32))
            e = e + nt(ib, win_s[:, cols])
        back = norm_back(e, n2, r2, v(V_G2))
        sb_ref[...] = back
        cb = back.astype(BF)
        cb_s[rows, :] = cb
        vo_ref[3:4, :] += sums(e * n2)
        vo_ref[4:5, :] += sums(e)
        vo_ref[5:6, :] += sums(cb.astype(F32))
        cmb_ref[...] = nt(cb, wco_s[...]).astype(BF)

    t = t - 2
    slot = t % 2

    def tall(b, slot):
        return pltpu.make_async_copy(stage_s.at[slot], all_ref.at[b, :, pl.ds(0, 4)], stage_sem.at[slot])

    def flat(b, slot):
        return pltpu.make_async_copy(stage_s.at[slot], all_ref.at[:, :, 4 + b], stage_sem.at[slot])

    @pl.when((t >= 2) & (t < 6))
    def _():
        tall(t - 2, slot).wait()

    @pl.when(t >= 6)
    def _():
        flat(t - 6, slot).wait()

    def put(x, g):
        stage_s[slot] = tn(x, g).astype(BF).reshape(4, 4, 48, D)

    @pl.when((t >= 0) & (t < 4))
    def _():
        put(act_s[:, columns(t, D)], fb_s[...])
        tall(t, slot).start()

    @pl.when((t >= 4) & (t < 8))
    def _():
        put(low_s[...], ib_s[:, columns(t - 4, D)])
        flat(t - 4, slot).start()

    @pl.when(t == 8)
    def _():
        put(cm_s[...], cb_s[...])
        flat(4, 0).start()
        flat(3, 1).wait()
        flat(4, 0).wait()


def ffn_both(order, spots, vec, bin_, n1, cm, out_grad, out_grad_got, weights):
    half, D = out_grad_got.shape
    T, FF = 2 * half, bin_.shape[1]
    token = lambda width: pl.BlockSpec((half, width), lambda i, p: (jnp.minimum(i, 1), 0))
    hbm = pl.BlockSpec(memory_space=pl.ANY)
    big = lambda *shape: pltpu.VMEM(shape, BF)
    return order.call(
        functools.partial(ffn_kernel, parts=4), spots, vec, bin_, n1, cm, out_grad, out_grad_got, *weights,
        scalars=1, name="ffn_both", us=60, grid=(11,),
        in_specs=[full(vec.shape), full(bin_.shape), token(D)] + [hbm] * 6,
        out_specs=[still((half, D)), still((half, D)), token(D), token(D), still((8, D)), still((1, FF)), hbm],
        out_shape=[shaped(half, D), shaped(half, D), shaped(T, D, dtype=F32), shaped(T, D),
                   shaped(8, D, dtype=F32), shaped(1, FF, dtype=F32), shaped(4, 4, 9, 48, D)],
        scratch_shapes=[big(T, FF), big(T, FF), big(T, D), big(2, half, D), big(D, D), big(D, FF), big(FF, D), big(T, D), big(T, D),
                        big(T, D), big(2, 4, 4, 48, D), pltpu.SemaphoreType.DMA((2,)), pltpu.SemaphoreType.DMA((6,))])


def middle_kernel(spot_ref, vec_ref, q_ref, n_ref, r_ref, sb_ref,
                  k_in, v_in, low_in, src_in, mix_in, wq_in, wk_in, wv_in, wo_in,
                  fb_ref, mb_ref, own_ref, other_ref, vo_ref, send_ref, keep_ref,
                  dq_s, dk_s, dv_s, back_s, low_s, src_s, mix_s, wq_s, wk_s, wv_s, wo_s, sem):
    v = lambda i: vec_ref[i : i + 1, :]
    t = pl.program_id(0)
    half, D = own_ref.shape
    loads = Loads(sem)
    first = [loads.add(wq_in, wq_s), loads.add(wo_in, wo_s)]
    more = [loads.add(a, b) for a, b in ((wk_in, wk_s), (wv_in, wv_s), (k_in, dk_s), (v_in, dv_s))]
    last = [loads.add(a, b) for a, b in ((low_in, low_s), (src_in, src_s), (mix_in, mix_s))]

    @pl.when(t == 0)
    def _():
        for c in loads.copies:
            c.start()
        vo_ref[...] = jnp.zeros_like(vo_ref)
        for c in first:
            c.wait()

    @pl.when(t < 2)
    def _():
        rows = pl.ds(pl.multiple_of(t * half, half), half)
        dq = q_ref[...]
        dq_s[rows, :] = dq
        n = n_ref[...]
        e = sb_ref[...] + nt(dq, wq_s[...])
        back = norm_back(e, n, r_ref[...], v(V_G1))
        fb_ref[...] = back
        low = back.astype(BF)
        back_s[rows, :] = low
        vo_ref[0:1, :] += sums(e * n)
        vo_ref[1:2, :] += sums(e)
        vo_ref[2:3, :] += sums(low.astype(F32))
        vo_ref[3:4, :] += sums(dq.astype(F32))
        mb_ref[...] = nt(low, wo_s[...]).astype(BF)

        @pl.when(t == 0)
        def _():
            for c in more:
                c.wait()

        dv = dv_s[rows, :]
        vo_ref[4:5, :] += sums(dv.astype(F32))
        mg = (nt(dk_s[rows, :], wk_s[...]) + nt(dv, wv_s[...])).astype(BF)

        @pl.when(t == spot_ref[4])
        def _():
            own_ref[...] = mg

        @pl.when(t != spot_ref[4])
        def _():
            other_ref[...] = mg

    @pl.when(t == 2)
    def _():
        for c in last:
            c.wait()

    for i, (x, g) in enumerate(((low_s, dq_s), (src_s, dk_s), (src_s, dv_s), (mix_s, back_s))):
        @pl.when(t == 2 + i)
        def _():
            total = tn(x[...], g[...]).astype(BF)
            def put_piece(which, x, zl, zh, rows):
                for k in range(2):
                    (send_ref, keep_ref)[which][at_of(ORDERS["cross"], x=x, y=k, zl=zl, zh=zh) + (0,)] = rows[:, D // 2 * k : D // 2 * (k + 1)]

            place_rows(spot_ref[0], total, 48, put_piece)


def middle(order, spots, vec, dq, dk, dv, n1, r1, sb, low, source, mixed, weights):
    T, D = n1.shape
    half = T // 2
    token = lambda width: pl.BlockSpec((half, width), lambda i, p: (jnp.minimum(i, 1), 0))
    out = pl.BlockSpec((2, 2, 2, 2, 1, 48, D // 2), lambda i, p: (0, 0, 0, 0, jnp.maximum(i - 2, 0), 0, 0))
    hbm = pl.BlockSpec(memory_space=pl.ANY)
    square, rect = pltpu.VMEM((D, D), BF), pltpu.VMEM((T, D), BF)
    return order.call(
        middle_kernel, spots, vec, dq, n1, r1, sb, dk, dv, low, source, mixed, *weights, scalars=1, name="middle", us=18,
        grid=(6,),
        in_specs=[full(vec.shape)] + [token(D), token(D), token(1), token(D)] + [hbm] * 9,
        out_specs=[token(D), token(D), still((half, D)), still((half, D)), still((8, D)), out, out],
        out_shape=[shaped(T, D, dtype=F32), shaped(T, D), shaped(half, D), shaped(half, D), shaped(8, D, dtype=F32)]
        + [shaped(2, 2, 2, 2, 4, 48, D // 2)] * 2,
        scratch_shapes=[rect] * 7 + [square] * 4 + [pltpu.SemaphoreType.DMA((9,))])


def back_kernel(spot_ref, *refs, counts):
    n = len(counts)
    g, rest = refs[: sum(counts)], refs[sum(counts) :]
    w, (plain_ref, own_ref, other_ref) = rest[:n], rest[n:]
    total = plain_ref[...]
    for i, count in enumerate(counts):
        total = total + nt(joined(g[:count]), w[i][...])
        g = g[count:]
    total = total.astype(BF)

    @pl.when(pl.program_id(0) == spot_ref[4])
    def _():
        own_ref[...] = total

    @pl.when(pl.program_id(0) != spot_ref[4])
    def _():
        other_ref[...] = total


def back_rows(order, spots, grads, weights, plain, moves):
    parts = [p for g in grads for p in g]
    T, D = plain.shape
    half = T // 2
    r = lambda width: pl.BlockSpec((half, width), lambda i, p: (i, 0))
    return order.call(
        functools.partial(back_kernel, counts=[len(g) for g in grads]), spots, *parts, *weights, plain,
        scalars=1, name="back_rows", us=9, grid=(2,), moves=moves,
        in_specs=[r(p.shape[1]) for p in parts] + [full((D, D))] * len(weights) + [r(D)],
        out_specs=[still((half, D))] * 2, out_shape=[shaped(half, D)] * 2)


def place_rows(core, total, height, put):
    for j in range(total.shape[0] // (2 * height)):
        even = total[2 * j * height : (2 * j + 1) * height]
        odd = total[(2 * j + 1) * height : (2 * j + 2) * height]
        put(1, j % 2, (j // 2) % 2, j // 4, jnp.where(core == 0, even, odd))
        put(0, j % 2, (j // 2) % 2, j // 4, jnp.where(core == 0, odd, even))


ORDERS = {"cross": ("y", "zl", "x", "zh"), "square": ("x", "zl", "zh")}


def at_of(order, **place):
    return tuple(place[name] for name in order)


def joined(refs):
    return refs[0][...] if len(refs) == 1 else jnp.concatenate([r[...] for r in refs], 1)


def self_back_kernel(spot_ref, q_ref, k_ref, v_ref, do_ref, o_ref, l_ref, oh_ref, mk_ref, vf_ref, v1_ref, vi_ref, h_in,
                     dq_ref, dk_ref, dv_ref, send_ref, keep_ref, keep_v_ref, acc_s, g_s, h_s, sem, *, pairs, bk):
    at = pl.program_id(0)
    hidden = pltpu.make_async_copy(h_in, h_s, sem)
    D = 128 * pairs
    wide = D // 2

    @pl.when(at == 0)
    def _():
        hidden.start()

    @pl.when(at < pairs)
    def _():
        out = {"q": (dq_ref, 0), "k": (dk_ref, 1), "v": (dv_ref, 2)}

        def put(name, rows, block):
            ref, i = out[name]
            ref[rows, :] = block
            g_s[i, rows, columns(at)] = block

        attend_pair_back(q_ref[...], k_ref[...], v_ref[...], do_ref[...], o_ref[...], [l_ref[0, h : h + 1, :] for h in (0, 1)],
                         oh_ref[...], mk_ref[...], acc_s, put, bk, True)

    core = spot_ref[0]
    tail = keep_ref.shape[0]

    for i in range(3):
        @pl.when(at == pairs + i)
        def _():
            if i == 0:
                hidden.wait()

            def put_piece(which, x, zl, zh, rows):
                j = 4 * x + 2 * zl + zh
                for k in range(2):
                    part = rows[:, wide * k : wide * (k + 1)]
                    if i < 2:
                        at_row = 96 * (2 * j + i) + 48 * k
                        (send_ref, keep_ref)[which][at_row : at_row + 48, :] = part
                    elif which:
                        keep_v_ref[128 * j + 64 * k : 128 * j + 64 * k + 48, :] = part
                    else:
                        send_ref[tail + 128 * j + 64 * k : tail + 128 * j + 64 * k + 48, :] = part

            place_rows(core, tn(h_s[...], g_s[i]).astype(BF), 48, put_piece)

    @pl.when(at == pairs + 2)
    def _():
        row_of = lambda i: sums(g_s[i].astype(F32))
        rows = jnp.concatenate([vf_ref[0:6, :], v1_ref[0:5, :], row_of(0), row_of(2), jnp.zeros((3, D), F32)], 0)
        spread = jnp.broadcast_to(vi_ref[...], (16, vi_ref.shape[1]))
        for first, part, w in ((0, rows, 48), (128, spread, 192)):
            for j in range(8):
                x, zl, zh = j % 2, (j // 2) % 2, j // 4
                even = part[:, 2 * j * w : (2 * j + 1) * w].astype(BF)
                odd = part[:, (2 * j + 1) * w : (2 * j + 2) * w].astype(BF)
                at_row = 128 * (4 * x + 2 * zl + zh) + 48
                keep_v_ref[at_row : at_row + 16, first : first + w] = jnp.where(core == 0, even, odd)
                send_ref[tail + at_row : tail + at_row + 16, first : first + w] = jnp.where(core == 0, odd, even)


def self_back(order, spots, q, k, v, do, o, totals, oh, mk, vectors, hidden, moves):
    T, D = q.shape
    pairs = D // 128
    p_in = lambda i: jnp.minimum(i, pairs - 1)
    pair = pl.BlockSpec((T, 128), lambda i, p: (0, p_in(i)))
    rows = 16 * 2 * 48, 16 * 64
    return order.call(
        functools.partial(self_back_kernel, pairs=pairs, bk=256), spots, q, k, v, do, o, totals, oh, mk, *vectors, hidden,
        scalars=1, name="self_back", us=30, grid=(pairs + 3,), moves=moves,
        in_specs=[pair] * 5 + [pl.BlockSpec((1, 8, T), lambda i, p: (p_in(i), 0, 0))]
        + [full(a.shape) for a in (oh, mk, *vectors)] + [pl.BlockSpec(memory_space=pl.ANY)],
        out_specs=[pair] * 3 + [still((r, D // 2)) for r in (sum(rows), *rows)],
        out_shape=[shaped(T, D)] * 3 + [shaped(r, D // 2) for r in (sum(rows), *rows)],
        scratch_shapes=[pltpu.VMEM((128, T), F32), pltpu.VMEM((3, T, D), BF), pltpu.VMEM((T, D), BF), pltpu.SemaphoreType.DMA])


def fold_kernel(spot_ref, *refs, kinds):
    n_in = sum(4 if k else 2 for k in kinds)
    ins, outs = refs[:n_in], refs[n_in:]
    for splits in kinds:
        if splits:
            keep, keep_other, got, got_other = ins[:4]
            ins = ins[4:]
            outs[0][...] = keep[0] + got[0]
            outs[1][...] = keep_other[0] + got_other[0]
            outs = outs[2:]
        else:
            outs[0][...] = ins[0][...] + ins[1][...]
            ins, outs = ins[2:], outs[1:]


def small_fold_kernel(spot_ref, *refs, items, keeps, gots):
    keep_refs, got_refs, outs = refs[:keeps], refs[keeps : keeps + gots], refs[keeps + gots :]
    for i, (g, at, which, message, first) in enumerate(items):
        keep, got, out = keep_refs[i], got_refs[g], outs[i]
        rows = out.shape[0]
        if which is None:
            total = keep[...] + got[at : at + rows, :]
            out[...] = total
        else:
            mine = spot_ref[which]
            part = lambda p: pl.ds(pl.multiple_of(p * rows, 16), rows)
            there = lambda p: pl.ds(pl.multiple_of(at + p * rows, 16), rows)
            out[...] = keep[part(mine), :] + got[there(mine), :]
            total = keep[part(1 - mine), :] + got[there(1 - mine), :]
        if message is not None:
            outs[keeps + message][first : first + rows, :] = total


LINKS = {"core": ("dp", 1, 16, 0), "x": ("dp", 2, 16, 1), "zl": ("dp", 4, 16, 2), "zh": ("dp", 8, 16, 3),
         "y": ("seq", 1, 2, 4), "sum": ("seq", 1, 2, None), "gather": ("seq", 1, 2, None)}


class Sum:
    def __init__(self, keep, got, at, *links):
        self.keep, self.got, self.at = keep, got, at
        self.links, self.step = links, 0

    def link(self):
        return self.links[self.step] if self.step < len(self.links) else None


def first_swap(send, keep, after=None):
    if after is not None:
        send, _ = lax.optimization_barrier((send, after))
    flat = lambda a: a.reshape(-1, a.shape[-1])
    return flat(keep), swap(flat(send), *LINKS["core"][:3])


def advance(order, spots, *groups):
    groups = [g for g in groups if g.link() is not None]
    whichs = [LINKS[g.link()][3] for g in groups]
    rows = [g.keep.shape[0] // (1 if w is None else 2) for g, w in zip(groups, whichs)]
    shared = {}
    for i, g in enumerate(groups):
        shared.setdefault((LINKS[g.link()][:3], g.keep.shape[1]), []).append(i)
    steps = next(s for s in (4, 2, 1) if all(r % (16 * s) == 0 for r in rows))
    simple = all(len(s) == 1 for s in shared.values()) and all(g.got.shape == g.keep.shape for g in groups)
    if simple and steps > 1:
        args, in_specs, out_specs, out_shape = [], [], [], []
        for g, w, r in zip(groups, whichs, rows):
            width, bt = g.keep.shape[1], r // steps
            flat = pl.BlockSpec((bt, width), lambda i, p: (i, 0))
            if w is None:
                args += [g.keep, g.got]
                in_specs += [flat, flat]
            else:
                keep, got = g.keep.reshape(2, r, width), g.got.reshape(2, r, width)
                mine = pl.BlockSpec((1, bt, width), lambda i, p, w=w: (p[w], i, 0))
                other = pl.BlockSpec((1, bt, width), lambda i, p, w=w: (1 - p[w], i, 0))
                args += [keep, keep, got, got]
                in_specs += [mine, other, mine, other]
            n = 1 if w is None else 2
            out_specs += [flat] * n
            out_shape += [shaped(r, width)] * n
        out = list(order.call(
            functools.partial(fold_kernel, kinds=[w is not None for w in whichs]), spots, *args, scalars=1, name="fold", us=3,
            grid=(steps,), in_specs=in_specs, out_specs=out_specs, out_shape=out_shape))
        for g, w in zip(groups, whichs):
            g.keep = out.pop(0)
            g.got, g.at = swap(g.keep if w is None else out.pop(0), *LINKS[g.link()][:3]), 0
            g.step += 1
        return
    gots, items, messages = [], [], []
    for g in groups:
        if not any(a is g.got for a in gots):
            gots.append(g.got)
    place = {}
    for key, members in shared.items():
        if len(members) == 1 and whichs[members[0]] is None:
            continue
        first = 0
        for i in members:
            place[i] = (len(messages), first)
            first += rows[i]
        messages.append((first, key[1]))
    for i, (g, w) in enumerate(zip(groups, whichs)):
        items.append((next(n for n, a in enumerate(gots) if a is g.got), g.at, w, *place.get(i, (None, 0))))
    shapes = [(r, g.keep.shape[1]) for r, g in zip(rows, groups)] + messages
    arrays = [g.keep for g in groups] + gots
    out = order.call(
        functools.partial(small_fold_kernel, items=items, keeps=len(groups), gots=len(gots)), spots, *arrays, scalars=1,
        name="fold", us=3, grid=(1,), in_specs=[full(a.shape) for a in arrays],
        out_specs=[still(s) for s in shapes], out_shape=[shaped(*s) for s in shapes])
    came = {}
    for i, g in enumerate(groups):
        g.keep = out[i]
        links = LINKS[g.link()][:3]
        if i not in place:
            g.got, g.at = swap(g.keep, *links), 0
        else:
            message, first = place[i]
            if message not in came:
                came[message] = swap(out[len(groups) + message], *links)
            g.got, g.at = came[message], first
        g.step += 1


def finish_kernel(spot_ref, *refs, items, keeps, gots):
    ffn_ref, *refs = refs
    keep_refs, got_refs, outs = refs[:keeps], refs[keeps : keeps + gots], list(refs[keeps + gots :])
    values = []
    for i, (g, at, join) in enumerate(items):
        own = keep_refs[i][...]
        got = got_refs[g][at : at + own.shape[0], :]
        if join:
            first = spot_ref[4] == 0
            values.append((jnp.where(first, own, got), jnp.where(first, got, own)))
        else:
            values.append(own + got)
    cross, self_qk, self_v = values
    (sq, sk, sv, so, cq, ck, cv, co, fi, fo, *vectors) = outs
    f32 = lambda v: v.astype(F32)
    D = ffn_ref.shape[1]
    w = D // 2
    unit = lambda v, u: f32(v[48 * u : 48 * u + 48])
    fo[...] = f32(ffn_ref[0:192, :])
    for b in range(4):
        fi[:, D * b : D * (b + 1)] = f32(ffn_ref[192 + 48 * b : 240 + 48 * b, :])
    co[...] = f32(ffn_ref[384:432, :])
    for k in range(2):
        cols = slice(k * w, (k + 1) * w)
        for i, o in enumerate((cq, ck, cv, so)):
            o[:, cols] = unit(cross[k], i)
        for i, o in enumerate((sq, sk)):
            o[:, cols] = unit(self_qk, 2 * i + k)
        sv[:, cols] = f32(self_v[64 * k : 64 * k + 48])
    rows = f32(self_v[48:64])
    for i, o in enumerate(vectors[:13]):
        o[...] = rows[i : i + 1, :48]
    vectors[13][...] = rows[0:1, 128:320]


def finish(order, spots, ffn, *groups):
    D = ffn.shape[1]
    gots = []
    for g in groups:
        if not any(a is g.got for a in gots):
            gots.append(g.got)
    items = [(next(n for n, a in enumerate(gots) if a is g.got), g.at, g.links[-1] == "gather") for g in groups]
    arrays = [ffn] + [g.keep for g in groups] + gots
    shapes = [(48, D)] * 8 + [(48, 4 * D), (192, D)] + [(1, 48)] * 13 + [(1, 192)]
    return order.call(
        functools.partial(finish_kernel, items=items, keeps=len(groups), gots=len(gots)), spots, *arrays, scalars=1,
        name="finish", us=3, grid=(1,), in_specs=[full(a.shape) for a in arrays], out_specs=[still(s) for s in shapes],
        out_shape=[shaped(*s, dtype=F32) for s in shapes])


def swap(block, ax, bit, size):
    return lax.ppermute(block, ax, [(i, i ^ bit) for i in range(size)])


def two(s, first, second):
    return jnp.where(s == 0, jnp.concatenate([first, second], 0), jnp.concatenate([second, first], 0))


def pick(array, index, axis):
    return lax.dynamic_index_in_dim(array, index, axis, keepdims=False)


def row_in(array, s):
    own = pick(array, s, 0)
    other = swap(pick(array, 1 - s, 0), "seq", 1, 2)
    return two(s, own, other)


def whole_rows(
    hidden_in, memory, tgt_segment, src_segment, out_grad,
    self_query, query_bias, self_key, self_value, value_bias, self_output, output_bias,
    first_gain, first_shift,
    cross_query, cross_query_bias, cross_key, cross_value, cross_value_bias, cross_output,
    cross_output_bias, second_gain, second_shift,
    ffn_in, ffn_in_bias, ffn_out, ffn_out_bias, third_gain, third_shift,
):
    f32 = lambda v: v.astype(F32)
    s = lax.axis_index("seq")
    dp = lax.axis_index("dp")
    place = dp % 2, (dp // 2) % 2, (dp // 4) % 2, dp // 8, s
    spots = jnp.stack(place).astype(jnp.int32)
    order = Order()
    far_half = lambda array: pick(array, 1 - s, 0)
    segs = row_in(jnp.stack([tgt_segment, src_segment], -1), s)
    hidden_got = swap(far_half(hidden_in), "seq", 1, 2)
    vec = jnp.stack([query_bias, value_bias, output_bias, first_gain, first_shift, cross_query_bias, cross_value_bias,
                     cross_output_bias, second_gain, second_shift, ffn_out_bias, third_gain, third_shift]).astype(F32)
    bin_ = f32(ffn_in_bias).reshape(1, -1)
    tgt, src = segs[:, 0], segs[:, 1]
    self_oh, self_mk = masks(tgt, tgt)
    _, cross_mk = masks(tgt, src)
    *near_self, near_key, near_value = project_near(
        order, spots, hidden_in, memory, vec, [self_query, self_key, self_value, cross_key, cross_value])
    next_half, hidden_got, near_self[0] = lax.optimization_barrier((far_half(memory), hidden_got, near_self[0]))
    memory_got = swap(next_half, "seq", 1, 2)
    self_totals, n1, r1, first_low, cross_queries, hidden, queries, key_rows, value_rows, self_mixed = self_forward(
        order, spots, vec, self_oh, self_mk, hidden_in, hidden_got, near_self,
        [self_query, self_key, self_value, self_output, cross_query])
    next_half, memory_got, r1 = lax.optimization_barrier((far_half(out_grad), memory_got, r1))
    out_grad_got = swap(next_half, "seq", 1, 2)
    cross_totals, source, memory_keys, memory_values, cross_mixed = cross_forward(
        order, spots, vec, self_oh, cross_mk, cross_queries, memory, memory_got, [near_key, near_value], [cross_key, cross_value])
    ho, ho_far, second_back, cross_mixed_back, v_ffn, v_in, ffn_all = ffn_both(
        order, spots, vec, bin_, n1, cross_mixed, out_grad, out_grad_got, [cross_output, ffn_in, ffn_out])
    ho_got = swap(ho_far, "seq", 1, 2)
    ffn_sum = lax.psum(lax.psum_scatter(ffn_all.reshape(16, 432, -1), "dp", scatter_dimension=0, tiled=False), "seq")
    cross_parts = attend_bwd(order, spots, cross_queries, memory_keys, memory_values, cross_mixed_back, cross_mixed, cross_totals,
                             self_oh, cross_mk, False, 512)
    order.last.append(ho_got)
    first_back, self_mixed_back, mg, mg_far, v_first, *pairs = middle(
        order, spots, vec, *cross_parts, n1, r1, second_back, first_low, source, self_mixed,
        [cross_query, cross_key, cross_value, self_output])
    cross_sum = Sum(*first_swap(*pairs), 0, *ORDERS["cross"], "gather")
    advance(order, spots, cross_sum)
    query_back, key_back, value_back, send, keep_qk, keep_v, hidden_out = self_back(
        order, spots, queries, key_rows, value_rows, self_mixed_back, self_mixed, self_totals, self_oh, self_mk,
        [v_ffn, v_first, v_in], hidden, [(ho, ho_got)])
    advance(order, spots, cross_sum)
    keep_qk, got = first_swap(send, keep_qk, cross_sum.keep)
    qk_sum = Sum(keep_qk, got, 0, *ORDERS["square"], "sum")
    v_sum = Sum(keep_v, got, keep_qk.shape[0], "sum", *ORDERS["square"])
    advance(order, spots, qk_sum, v_sum)
    hg, hg_far = back_rows(
        order, spots, [[query_back], [key_back], [value_back]], [self_query, self_key, self_value], first_back, [])
    mg_far, _ = lax.optimization_barrier((mg_far, keep_v))
    mg_got = swap(mg_far, "seq", 1, 2)
    hg_got = swap(hg_far, "seq", 1, 2)
    for _ in range(3):
        advance(order, spots, cross_sum, qk_sum, v_sum)
    memory_grad = two(s, mg[None], mg_got[None])
    hidden_grad = two(s, hg[None], hg_got[None])
    (g_sq, g_sk, g_sv, g_so, g_cq, g_ck, g_cv, g_co, g_fi, g_fo, *v, v_fi) = finish(
        order, spots, ffn_sum, cross_sum, qk_sum, v_sum)
    (g3, b3, fob, g2, b2, cob, g1, b1, ob, cqb, cvb, qb, vb) = [a.reshape(-1) for a in v]
    return (
        hidden_out, hidden_grad, memory_grad,
        g_sq, qb, g_sk, g_sv, vb, g_so, ob, g1, b1, g_cq, cqb, g_ck, g_cv, cvb, g_co, cob, g2, b2,
        g_fi, v_fi.reshape(-1), g_fo, fob, g3, b3,
    )


def solution(mesh):
    in_specs = (
        P("dp", "seq", None),
        P("dp", "seq", None),
        P("dp", "seq"),
        P("dp", "seq"),
        P("dp", "seq", None),
        P(),
        P(),
        P(),
        P(),
        P(),
        P(),
        P(),
        P(),
        P(),
        P(),
        P(),
        P(),
        P(),
        P(),
        P(),
        P(),
        P(),
        P(),
        P(),
        P(),
        P(),
        P(),
        P(),
        P(),
    )
    out_specs = (
        P("dp", "seq", None),
        P("dp", "seq", None),
        P("dp", "seq", None),
        P("dp", None),
        P("dp"),
        P("dp", None),
        P("dp", None),
        P("dp"),
        P("dp", None),
        P("dp"),
        P("dp"),
        P("dp"),
        P("dp", None),
        P("dp"),
        P("dp", None),
        P("dp", None),
        P("dp"),
        P("dp", None),
        P("dp"),
        P("dp"),
        P("dp"),
        P("dp", None),
        P("dp"),
        P("dp", None),
        P("dp"),
        P("dp"),
        P("dp"),
    )
    rows_form = mesh.shape["seq"] == 2 and mesh.shape["dp"] == 16

    def on_device(*arrays):
        if rows_form and arrays[0].shape[0] == 2:
            return whole_rows(*arrays)
        return split_rows(*arrays)

    return jax.shard_map(
        on_device, mesh=mesh, in_specs=in_specs, out_specs=out_specs, check_vma=False
    )
```

```python
import functools
import math

import jax
import jax.numpy as jnp
from jax import lax
from jax.experimental import pallas as pl
from jax.experimental.pallas import tpu as pltpu
from jax.sharding import PartitionSpec as P

HEADS = 12
BF=jnp.bfloat16; F32=jnp.float32
BIG=-1e30
def dot(a,b): return jnp.dot(a,b,preferred_element_type=F32)

def lane_low(shape): return lax.broadcasted_iota(jnp.int32, shape, 1) < 64

def prepare(q,k,v,oh,mk):
    low=lane_low(k.shape)
    qT=(q*BF(0.125)).T
    vT=v.T
    ones=jnp.ones((16,k.shape[0]),BF)
    kas=[jnp.where(low,k,mk),jnp.where(low,mk,k)]
    vas=[jnp.concatenate([vT[64*h:64*h+64],ones],0) for h in (0,1)]
    qas=[jnp.concatenate([qT[:64],oh],0),jnp.concatenate([oh,qT[64:]],0)]
    return kas,vas,qas

def causal_block(n):
    return lax.broadcasted_iota(jnp.int32,(n,n),0)<=lax.broadcasted_iota(jnp.int32,(n,n),1)

def attend_near(q,k,v,oh,mk):
    kas,vas,qas=prepare(q,k,v,oh,mk)
    dm=causal_block(q.shape[0])
    ss=[jnp.where(dm,dot(kas[h],qas[h]),BIG) for h in (0,1)]
    out=[]
    for h in (0,1):
        m=jnp.max(ss[h],axis=0,keepdims=True)
        o=dot(vas[h],jnp.exp(ss[h]-m).astype(BF))
        out.append((o[:64],m,o[64:65]))
    return out

def attend_rest(first,near,far_args,off_args):
    far=prepare(*far_args); off=prepare(*off_args)
    dm=causal_block(far_args[0].shape[0])
    fs=[jnp.where(dm,dot(far[0][h],far[2][h]),BIG) for h in (0,1)]
    os=[]; result=[]
    for h in (0,1):
        os.append(dot(off[0][h],off[2][h]))
        m=jnp.max(fs[h],axis=0,keepdims=True)
        p=jnp.exp(fs[h]-m).astype(BF)
        o=dot(far[1][h],p)
        here=(o[:64],m,o[64:65])
        result.append(([jnp.where(first,a,b) for a,b in zip(near[h],here)],[jnp.where(first,b,a) for a,b in zip(near[h],here)]))
    out=[]
    for h in (0,1):
        (o0,m0,l0),(o1,m1,l1)=result[h]
        m=jnp.maximum(m1,jnp.max(os[h],axis=0,keepdims=True))
        p=jnp.exp(os[h]-m).astype(BF)
        w=jnp.exp(m1-m)
        o=dot(off[1][h],p)
        l=o[64:65]+w*l1
        out.append(((o0/l0,m0+jnp.log(l0)),((o[:64]+w*o1)/l,m+jnp.log(l))))
    return out

def attend_pair(q,k,v,oh,mk,put_total,bq):
    T=q.shape[0]
    kas,vas,qas=prepare(q,k,v,oh,mk)
    def scores(i,h):
        return dot(kas[h],qas[h][:,i*bq:(i+1)*bq])
    def weigh(s):
        m=jnp.max(s,axis=0,keepdims=True)
        return m,jnp.exp(s-m).astype(BF)
    def mix(i,h,m,p):
        o=dot(vas[h],p)
        l=o[64:65]
        put_total(h,i,m+jnp.log(l))
        return o[:64]/l
    units=[(i,h) for i in range(T//bq) for h in (0,1)]
    os=[]
    s=scores(*units[0]); late=None
    for n,u in enumerate(units):
        coming=scores(*units[n+1]) if n+1<len(units) else None
        m,p=weigh(s)
        if late is not None: os.append(mix(*late))
        late=(*u,m,p)
        s=coming
    os.append(mix(*late))
    return [jnp.concatenate(os[2*i:2*i+2],0).T.astype(BF) for i in range(T//bq)]

def split3(x):
    a=x.astype(BF); r=x-a.astype(F32); b=r.astype(BF); c=(r-b.astype(F32)).astype(BF)
    return a,b,c

def attend_pair_back(q,k,v,do,o,totals,oh,mk,acc_ref,put,bk,causal):
    T=q.shape[0]; K=k.shape[0]
    low=lane_low((K,128))
    q=q*BF(0.125)
    qT=q.T; doT=do.T
    kT=k.T
    prodT=(do.astype(F32)*o.astype(F32)).T
    rowi=lax.broadcasted_iota(jnp.int32,(64,T),0)
    one=jnp.full((K,128),-1.0,BF)
    if causal:
        dm=lax.broadcasted_iota(jnp.int32,(bk,bk),0)<=lax.broadcasted_iota(jnp.int32,(bk,bk),1)
    qas=[];das=[]
    for h in (0,1):
        a,b,c=split3(totals[h])
        ohl=jnp.where(rowi==4,a,jnp.where(rowi==5,b,jnp.where(rowi==6,c,oh)))
        D=jnp.sum(prodT[64*h:64*h+64],axis=0,keepdims=True)
        a,b,c=split3(D)
        z=jnp.zeros((64,T),BF)
        dd=jnp.where(rowi==0,a,jnp.where(rowi==1,b,jnp.where(rowi==2,c,z)))
        if h==0:
            qas.append(jnp.concatenate([qT[:64],ohl],0)); das.append(jnp.concatenate([doT[:64],dd],0))
        else:
            qas.append(jnp.concatenate([ohl,qT[64:]],0)); das.append(jnp.concatenate([dd,doT[64:]],0))
    kas=[jnp.where(low,k,mk),jnp.where(low,mk,k)]
    vas=[jnp.where(low,v,one),jnp.where(low,one,v)]
    def ahead(j,h):
        q0=j*bk if causal else 0
        ks=slice(j*bk,(j+1)*bk)
        return dot(kas[h][ks],qas[h][:,q0:]),dot(vas[h][ks],das[h][:,q0:])
    def weigh(j,s,dp):
        q0=j*bk if causal else 0
        if causal:
            sd=jnp.where(dm,s[:,:bk],BIG)
            s=jnp.concatenate([sd,s[:,bk:]],1) if q0+bk<T else sd
        p=jnp.exp(s)
        return p.astype(BF),(p*dp).astype(BF)
    done={}
    def behind(j,h,p,ds):
        q0=j*bk if causal else 0
        ks=slice(j*bk,(j+1)*bk)
        done[h]=dot(ds,q[q0:]),dot(p,do[q0:])
        dqt=dot(kT[64*h:64*h+64,ks],ds)
        if j==0: acc_ref[64*h:64*h+64,:]=dqt
        else: acc_ref[64*h:64*h+64,q0:]+=dqt
        if h:
            lw=low[:bk]
            put("k",ks,jnp.where(lw,done[0][0],done[1][0]).astype(BF))
            put("v",ks,jnp.where(lw,done[0][1],done[1][1]).astype(BF))
    units=[(j,h) for j in range(K//bk) for h in (0,1)]
    now=ahead(*units[0]); late=None
    for n,u in enumerate(units):
        coming=ahead(*units[n+1]) if n+1<len(units) else None
        pd=weigh(u[0],*now)
        if late is not None: behind(*late)
        late=(*u,*pd)
        now=coming
    behind(*late)
    put("q",slice(0,T),(acc_ref[...]*0.125).T.astype(BF))


def project(values, weight):
    return jnp.dot(values, weight, preferred_element_type=jnp.float32)


def project_back(gradient, weight):
    return jnp.einsum("rte,de->rtd", gradient, weight, preferred_element_type=jnp.float32)


def weight_grad(values, gradient):
    return jnp.einsum("rtd,rte->de", values, gradient, preferred_element_type=jnp.float32)


def token_sum(gradient):
    return jnp.sum(gradient.astype(jnp.float32), axis=(0, 1))


def layer_norm(values, norm_gain, norm_shift):
    center = values - jnp.mean(values, axis=-1, keepdims=True)
    spread = jnp.mean(center * center, axis=-1, keepdims=True)
    return center * lax.rsqrt(spread + 1e-05) * norm_gain + norm_shift


def exact_gelu(values):
    return jax.nn.gelu(values, approximate=False)


def split_heads(values):
    return values.reshape(values.shape[0], values.shape[1], HEADS, values.shape[2] // HEADS)


def merge_heads(values):
    return values.reshape(values.shape[0], values.shape[1], values.shape[2] * values.shape[3])


def masked_scores(queries, key_rows, allowed):
    raw_scores = jnp.einsum(
        "rqhd,rkhd->rhqk",
        split_heads(queries),
        split_heads(key_rows),
        preferred_element_type=jnp.float32,
    )
    factor = 1.0 / math.sqrt(queries.shape[2] // HEADS)
    return jnp.where(allowed[:, None], raw_scores * factor, -1e30)


def attend_forward(queries, key_rows, value_rows, allowed):
    scores = masked_scores(queries, key_rows, allowed)
    highest = jnp.max(scores, axis=-1, keepdims=True)
    powers = jnp.exp(scores - highest)
    totals = jnp.sum(powers, axis=-1, keepdims=True)
    weights = (powers / totals).astype(jnp.bfloat16)
    mixed_heads = jnp.einsum(
        "rhqk,rkhd->rqhd", weights, split_heads(value_rows), preferred_element_type=jnp.float32
    )
    return (merge_heads(mixed_heads).astype(jnp.bfloat16), highest + jnp.log(totals))


def attend_backward(queries, key_rows, value_rows, allowed, log_totals, mixed_grad):
    scores = masked_scores(queries, key_rows, allowed)
    weights = jnp.exp(scores - log_totals)
    grad_heads = split_heads(mixed_grad)
    value_terms = jnp.einsum(
        "rhqk,rqhd->rkhd",
        weights.astype(jnp.bfloat16),
        grad_heads,
        preferred_element_type=jnp.float32,
    )
    weight_grads = jnp.einsum(
        "rqhd,rkhd->rhqk", grad_heads, split_heads(value_rows), preferred_element_type=jnp.float32
    )
    inner_sum = jnp.sum(weights * weight_grads, axis=-1, keepdims=True)
    factor = 1.0 / math.sqrt(queries.shape[2] // HEADS)
    score_grads = (weights * (weight_grads - inner_sum) * factor).astype(jnp.bfloat16)
    query_grads = jnp.einsum(
        "rhqk,rkhd->rqhd", score_grads, split_heads(key_rows), preferred_element_type=jnp.float32
    )
    key_terms = jnp.einsum(
        "rhqk,rqhd->rkhd", score_grads, split_heads(queries), preferred_element_type=jnp.float32
    )
    return (merge_heads(query_grads), merge_heads(key_terms), merge_heads(value_terms))


def split_rows(
    hidden_in,
    memory,
    tgt_segment,
    src_segment,
    out_grad,
    self_query,
    query_bias,
    self_key,
    self_value,
    value_bias,
    self_output,
    output_bias,
    first_gain,
    first_shift,
    cross_query,
    cross_query_bias,
    cross_key,
    cross_value,
    cross_value_bias,
    cross_output,
    cross_output_bias,
    second_gain,
    second_shift,
    ffn_in,
    ffn_in_bias,
    ffn_out,
    ffn_out_bias,
    third_gain,
    third_shift,
):
    tokens = hidden_in.shape[1]
    queries = (project(hidden_in, self_query) + query_bias.astype(jnp.float32)).astype(jnp.bfloat16)
    key_rows = project(hidden_in, self_key).astype(jnp.bfloat16)
    value_rows = (project(hidden_in, self_value) + value_bias.astype(jnp.float32)).astype(
        jnp.bfloat16
    )
    target_ids = tgt_segment.astype(jnp.bfloat16)
    all_keys, all_values, all_target = (
        lax.all_gather(key_rows, "seq", axis=1, tiled=True),
        lax.all_gather(value_rows, "seq", axis=1, tiled=True),
        lax.all_gather(target_ids, "seq", axis=1, tiled=True),
    )
    memory_keys = project(memory, cross_key).astype(jnp.bfloat16)
    memory_values = (project(memory, cross_value) + cross_value_bias.astype(jnp.float32)).astype(
        jnp.bfloat16
    )
    all_memkeys, all_memvalues, all_source = (
        lax.all_gather(memory_keys, "seq", axis=1, tiled=True),
        lax.all_gather(memory_values, "seq", axis=1, tiled=True),
        lax.all_gather(src_segment.astype(jnp.bfloat16), "seq", axis=1, tiled=True),
    )
    offset = lax.axis_index("seq") * tokens
    query_places = offset + jnp.arange(tokens, dtype=jnp.int32)
    key_places = jnp.arange(all_keys.shape[1], dtype=jnp.int32)
    self_allowed = (target_ids[:, :, None] == all_target[:, None, :]) & (
        query_places[:, None] >= key_places[None, :]
    )[None]
    cross_allowed = target_ids[:, :, None] == all_source[:, None, :]
    self_mixed, self_totals = attend_forward(queries, all_keys, all_values, self_allowed)
    self_branch = project(self_mixed, self_output) + output_bias.astype(jnp.float32)
    first_norm, first_pull = jax.vjp(
        layer_norm,
        hidden_in.astype(jnp.float32) + self_branch,
        first_gain.astype(jnp.float32),
        first_shift.astype(jnp.float32),
    )
    first_low = first_norm.astype(jnp.bfloat16)
    cross_queries = (project(first_low, cross_query) + cross_query_bias.astype(jnp.float32)).astype(
        jnp.bfloat16
    )
    cross_mixed, cross_totals = attend_forward(
        cross_queries, all_memkeys, all_memvalues, cross_allowed
    )
    cross_branch = project(cross_mixed, cross_output) + cross_output_bias.astype(jnp.float32)
    second_norm, second_pull = jax.vjp(
        layer_norm,
        first_norm + cross_branch,
        second_gain.astype(jnp.float32),
        second_shift.astype(jnp.float32),
    )
    second_low = second_norm.astype(jnp.bfloat16)
    inner_rows = project(second_low, ffn_in) + ffn_in_bias.astype(jnp.float32)
    activation_full, gelu_pull = jax.vjp(exact_gelu, inner_rows)
    activation = activation_full.astype(jnp.bfloat16)
    ffn_branch = project(activation, ffn_out) + ffn_out_bias.astype(jnp.float32)
    final_norm, third_pull = jax.vjp(
        layer_norm,
        second_norm + ffn_branch,
        third_gain.astype(jnp.float32),
        third_shift.astype(jnp.float32),
    )
    hidden_out = final_norm.astype(jnp.bfloat16)
    third_back, grad_third_gain, grad_third_shift = third_pull(out_grad.astype(jnp.float32))
    ffn_back = third_back.astype(jnp.bfloat16)
    grad_ffn_out = weight_grad(activation, ffn_back)
    grad_ffn_out_bias = token_sum(ffn_back)
    activation_back = project_back(ffn_back, ffn_out)
    inner_back = gelu_pull(activation_back)[0].astype(jnp.bfloat16)
    grad_ffn_in = weight_grad(second_low, inner_back)
    grad_ffn_in_bias = token_sum(inner_back)
    second_back, grad_second_gain, grad_second_shift = second_pull(
        third_back + project_back(inner_back, ffn_in)
    )
    cross_back = second_back.astype(jnp.bfloat16)
    grad_cross_output = weight_grad(cross_mixed, cross_back)
    grad_cross_output_bias = token_sum(cross_back)
    cross_mixed_back = project_back(cross_back, cross_output).astype(jnp.bfloat16)
    cross_query_grad, memkey_terms, memvalue_terms = attend_backward(
        cross_queries, all_memkeys, all_memvalues, cross_allowed, cross_totals, cross_mixed_back
    )
    memkey_sum, memvalue_sum = (
        lax.psum_scatter(
            memkey_terms.astype(jnp.bfloat16), "seq", scatter_dimension=1, tiled=True
        ).astype(jnp.float32),
        lax.psum_scatter(
            memvalue_terms.astype(jnp.bfloat16), "seq", scatter_dimension=1, tiled=True
        ).astype(jnp.float32),
    )
    memory_key_back = memkey_sum.astype(jnp.bfloat16)
    memory_value_back = memvalue_sum.astype(jnp.bfloat16)
    cross_query_back = cross_query_grad.astype(jnp.bfloat16)
    grad_cross_query = weight_grad(first_low, cross_query_back)
    grad_cross_query_bias = token_sum(cross_query_back)
    grad_cross_key = weight_grad(memory, memory_key_back)
    grad_cross_value = weight_grad(memory, memory_value_back)
    grad_cross_value_bias = token_sum(memory_value_back)
    memory_grad = (
        project_back(memory_key_back, cross_key) + project_back(memory_value_back, cross_value)
    ).astype(jnp.bfloat16)
    first_back, grad_first_gain, grad_first_shift = first_pull(
        second_back + project_back(cross_query_back, cross_query)
    )
    self_back = first_back.astype(jnp.bfloat16)
    grad_self_output = weight_grad(self_mixed, self_back)
    grad_output_bias = token_sum(self_back)
    self_mixed_back = project_back(self_back, self_output).astype(jnp.bfloat16)
    query_grad, key_terms, value_terms = attend_backward(
        queries, all_keys, all_values, self_allowed, self_totals, self_mixed_back
    )
    key_sum, value_sum = (
        lax.psum_scatter(
            key_terms.astype(jnp.bfloat16), "seq", scatter_dimension=1, tiled=True
        ).astype(jnp.float32),
        lax.psum_scatter(
            value_terms.astype(jnp.bfloat16), "seq", scatter_dimension=1, tiled=True
        ).astype(jnp.float32),
    )
    key_back = key_sum.astype(jnp.bfloat16)
    value_back = value_sum.astype(jnp.bfloat16)
    query_back = query_grad.astype(jnp.bfloat16)
    grad_self_query = weight_grad(hidden_in, query_back)
    grad_query_bias = token_sum(query_back)
    grad_self_key = weight_grad(hidden_in, key_back)
    grad_self_value = weight_grad(hidden_in, value_back)
    grad_value_bias = token_sum(value_back)
    hidden_grad = (
        first_back
        + project_back(query_back, self_query)
        + project_back(key_back, self_key)
        + project_back(value_back, self_value)
    ).astype(jnp.bfloat16)
    partial_grads = [
        grad_self_query,
        grad_query_bias,
        grad_self_key,
        grad_self_value,
        grad_value_bias,
        grad_self_output,
        grad_output_bias,
        grad_first_gain,
        grad_first_shift,
        grad_cross_query,
        grad_cross_query_bias,
        grad_cross_key,
        grad_cross_value,
        grad_cross_value_bias,
        grad_cross_output,
        grad_cross_output_bias,
        grad_second_gain,
        grad_second_shift,
        grad_ffn_in,
        grad_ffn_in_bias,
        grad_ffn_out,
        grad_ffn_out_bias,
        grad_third_gain,
        grad_third_shift,
    ]
    summed = (
        lax.psum_scatter(
            partial_grads[0].astype(jnp.bfloat16), "dp", scatter_dimension=0, tiled=True
        ).astype(jnp.float32),
        lax.psum_scatter(
            partial_grads[1].astype(jnp.bfloat16), "dp", scatter_dimension=0, tiled=True
        ).astype(jnp.float32),
        lax.psum_scatter(
            partial_grads[2].astype(jnp.bfloat16), "dp", scatter_dimension=0, tiled=True
        ).astype(jnp.float32),
        lax.psum_scatter(
            partial_grads[3].astype(jnp.bfloat16), "dp", scatter_dimension=0, tiled=True
        ).astype(jnp.float32),
        lax.psum_scatter(
            partial_grads[4].astype(jnp.bfloat16), "dp", scatter_dimension=0, tiled=True
        ).astype(jnp.float32),
        lax.psum_scatter(
            partial_grads[5].astype(jnp.bfloat16), "dp", scatter_dimension=0, tiled=True
        ).astype(jnp.float32),
        lax.psum_scatter(
            partial_grads[6].astype(jnp.bfloat16), "dp", scatter_dimension=0, tiled=True
        ).astype(jnp.float32),
        lax.psum_scatter(
            partial_grads[7].astype(jnp.bfloat16), "dp", scatter_dimension=0, tiled=True
        ).astype(jnp.float32),
        lax.psum_scatter(
            partial_grads[8].astype(jnp.bfloat16), "dp", scatter_dimension=0, tiled=True
        ).astype(jnp.float32),
        lax.psum_scatter(
            partial_grads[9].astype(jnp.bfloat16), "dp", scatter_dimension=0, tiled=True
        ).astype(jnp.float32),
        lax.psum_scatter(
            partial_grads[10].astype(jnp.bfloat16), "dp", scatter_dimension=0, tiled=True
        ).astype(jnp.float32),
        lax.psum_scatter(
            partial_grads[11].astype(jnp.bfloat16), "dp", scatter_dimension=0, tiled=True
        ).astype(jnp.float32),
        lax.psum_scatter(
            partial_grads[12].astype(jnp.bfloat16), "dp", scatter_dimension=0, tiled=True
        ).astype(jnp.float32),
        lax.psum_scatter(
            partial_grads[13].astype(jnp.bfloat16), "dp", scatter_dimension=0, tiled=True
        ).astype(jnp.float32),
        lax.psum_scatter(
            partial_grads[14].astype(jnp.bfloat16), "dp", scatter_dimension=0, tiled=True
        ).astype(jnp.float32),
        lax.psum_scatter(
            partial_grads[15].astype(jnp.bfloat16), "dp", scatter_dimension=0, tiled=True
        ).astype(jnp.float32),
        lax.psum_scatter(
            partial_grads[16].astype(jnp.bfloat16), "dp", scatter_dimension=0, tiled=True
        ).astype(jnp.float32),
        lax.psum_scatter(
            partial_grads[17].astype(jnp.bfloat16), "dp", scatter_dimension=0, tiled=True
        ).astype(jnp.float32),
        lax.psum_scatter(
            partial_grads[18].astype(jnp.bfloat16), "dp", scatter_dimension=0, tiled=True
        ).astype(jnp.float32),
        lax.psum_scatter(
            partial_grads[19].astype(jnp.bfloat16), "dp", scatter_dimension=0, tiled=True
        ).astype(jnp.float32),
        lax.psum_scatter(
            partial_grads[20].astype(jnp.bfloat16), "dp", scatter_dimension=0, tiled=True
        ).astype(jnp.float32),
        lax.psum_scatter(
            partial_grads[21].astype(jnp.bfloat16), "dp", scatter_dimension=0, tiled=True
        ).astype(jnp.float32),
        lax.psum_scatter(
            partial_grads[22].astype(jnp.bfloat16), "dp", scatter_dimension=0, tiled=True
        ).astype(jnp.float32),
        lax.psum_scatter(
            partial_grads[23].astype(jnp.bfloat16), "dp", scatter_dimension=0, tiled=True
        ).astype(jnp.float32),
    )
    finished = (
        lax.psum(summed[0].astype(jnp.bfloat16), "seq").astype(jnp.float32),
        lax.psum(summed[1].astype(jnp.bfloat16), "seq").astype(jnp.float32),
        lax.psum(summed[2].astype(jnp.bfloat16), "seq").astype(jnp.float32),
        lax.psum(summed[3].astype(jnp.bfloat16), "seq").astype(jnp.float32),
        lax.psum(summed[4].astype(jnp.bfloat16), "seq").astype(jnp.float32),
        lax.psum(summed[5].astype(jnp.bfloat16), "seq").astype(jnp.float32),
        lax.psum(summed[6].astype(jnp.bfloat16), "seq").astype(jnp.float32),
        lax.psum(summed[7].astype(jnp.bfloat16), "seq").astype(jnp.float32),
        lax.psum(summed[8].astype(jnp.bfloat16), "seq").astype(jnp.float32),
        lax.psum(summed[9].astype(jnp.bfloat16), "seq").astype(jnp.float32),
        lax.psum(summed[10].astype(jnp.bfloat16), "seq").astype(jnp.float32),
        lax.psum(summed[11].astype(jnp.bfloat16), "seq").astype(jnp.float32),
        lax.psum(summed[12].astype(jnp.bfloat16), "seq").astype(jnp.float32),
        lax.psum(summed[13].astype(jnp.bfloat16), "seq").astype(jnp.float32),
        lax.psum(summed[14].astype(jnp.bfloat16), "seq").astype(jnp.float32),
        lax.psum(summed[15].astype(jnp.bfloat16), "seq").astype(jnp.float32),
        lax.psum(summed[16].astype(jnp.bfloat16), "seq").astype(jnp.float32),
        lax.psum(summed[17].astype(jnp.bfloat16), "seq").astype(jnp.float32),
        lax.psum(summed[18].astype(jnp.bfloat16), "seq").astype(jnp.float32),
        lax.psum(summed[19].astype(jnp.bfloat16), "seq").astype(jnp.float32),
        lax.psum(summed[20].astype(jnp.bfloat16), "seq").astype(jnp.float32),
        lax.psum(summed[21].astype(jnp.bfloat16), "seq").astype(jnp.float32),
        lax.psum(summed[22].astype(jnp.bfloat16), "seq").astype(jnp.float32),
        lax.psum(summed[23].astype(jnp.bfloat16), "seq").astype(jnp.float32),
    )
    finished = list(finished)
    return (hidden_out, hidden_grad, memory_grad) + tuple(finished)


def nt(a, b):
    return lax.dot_general(a, b, (((1,), (1,)), ((), ())), preferred_element_type=F32)


def tn(a, b):
    return lax.dot_general(a, b, (((0,), (0,)), ((), ())), preferred_element_type=F32)


def mean(v):
    return jnp.mean(v, axis=-1, keepdims=True)


def norm_stats(v):
    center = v - mean(v)
    r = lax.rsqrt(mean(center * center) + 1e-05)
    return center * r, r


def norm_back(e, n, r, gain):
    u = e * gain
    return r * (u - mean(u) - n * mean(u * n))


def sums(v):
    return jnp.sum(v, axis=0, keepdims=True)


TAIL = (0.24251982196758853, 0.24429374300098905, 0.2054730204591465, 0.24507896666845616,
        -0.08230106829392796, 0.3798837300580386, -0.30809352249830146, 0.07314529579847638)


def gelu_pair(x):
    d = 1.0 + (0.43 * math.sqrt(0.5)) * jnp.abs(x)
    t = pl.reciprocal(d, approx=True)
    t = t * (2.0 - d * t)
    tail = 0.5 * TAIL[-1]
    for c in TAIL[-2::-1]:
        tail = tail * t + 0.5 * c
    bell = jnp.exp(-0.5 * x * x)
    tail = tail * t * bell
    phi = jnp.where(x >= 0, 1.0 - tail, tail)
    return x * phi, phi + x * bell * (1.0 / math.sqrt(2.0 * math.pi))


def full(shape):
    return pl.BlockSpec(shape, lambda *_: (0,) * len(shape), pipeline_mode=pl.Buffered(1))


def still(shape):
    return pl.BlockSpec(shape, lambda *_: (0,) * len(shape))


def rows_of(bt, width):
    return pl.BlockSpec((bt, width), lambda i: (i, 0))


class Order:
    def __init__(self):
        self.last = []

    def call(self, kernel, *args, name, us, grid, in_specs, out_specs, out_shape, scalars=0, scratch_shapes=(), moves=()):
        at, after, n, n_out = len(args), len(self.last), len(moves), len(out_specs)
        flat = [array for pair in moves for array in pair]
        hbm = pl.BlockSpec(memory_space=pl.ANY)

        def run(*refs):
            outs = at + 2 * n + after
            plain = refs[:at] + refs[outs : outs + n_out]
            if not n:
                return kernel(*plain, *refs[outs + n_out :])
            s = refs[0][4]
            buffer, sem = refs[-2:]
            reads, writes = [], []
            for i in range(n):
                target = refs[outs + n_out + i]
                for j, place in enumerate((s, 1 - s)):
                    slot = 2 * i + j
                    reads.append(pltpu.make_async_copy(refs[at + slot], buffer.at[slot], sem.at[0, slot]))
                    writes.append(pltpu.make_async_copy(buffer.at[slot], target.at[place], sem.at[1, slot]))

            @pl.when(pl.program_id(0) == 0)
            def _():
                for c in reads:
                    c.start()

            @pl.when(pl.program_id(0) == 1)
            def _():
                for r, w in zip(reads, writes):
                    r.wait()
                    w.start()

            kernel(*plain, *refs[outs + n_out + n : -2])

            @pl.when(pl.program_id(0) == grid[0] - 1)
            def _():
                for c in writes:
                    c.wait()

        more = [pltpu.VMEM((2 * n, *flat[0].shape), BF), pltpu.SemaphoreType.DMA((2, 2 * n))] if n else []
        out = pl.pallas_call(
            run, name=name, out_shape=list(out_shape) + [shaped(2, *pair[0].shape) for pair in moves],
            grid_spec=pltpu.PrefetchScalarGridSpec(
                num_scalar_prefetch=scalars, grid=grid, in_specs=list(in_specs) + [hbm] * (2 * n + after),
                out_specs=list(out_specs) + [hbm] * n, scratch_shapes=list(scratch_shapes) + more),
            cost_estimate=pl.CostEstimate(flops=0, bytes_accessed=int(us * 7.2e6), transcendentals=0),
            compiler_params=pltpu.CompilerParams(vmem_limit_bytes=127 * 2**19),
        )(*args, *flat, *self.last)
        self.last = [out[n_out - 1]]
        return out


def shaped(*shape, dtype=BF):
    return jax.ShapeDtypeStruct(shape, dtype)


(V_QB, V_VB, V_OB, V_G1, V_B1, V_CQB, V_CVB, V_COB, V_G2, V_B2, V_FOB, V_G3, V_B3) = range(13)


def mask_of(ids, ref):
    row = lax.broadcasted_iota(jnp.int32, (128, ids.shape[1]), 0) % 64
    ref[...] = jnp.where(row < 4, jnp.where(row == ids, 0.0, BIG), jnp.where(row < 7, -1.0, 0.0)).T.astype(BF)


def one_hot(ids, ref):
    row = lax.broadcasted_iota(jnp.int32, (64, ids.shape[1]), 0)
    ref[...] = jnp.where(row == ids, 1.0, 0.0).astype(BF)


def near_kernel(spot_ref, seg_ref, x_ref, y_ref, far_ref, grad_ref, vec_ref, wq_ref, wk_ref, wv_ref, uk_ref, uv_ref,
                q_ref, k_ref, v_ref, mk_ref, mv_ref, far_out, grad_out, mix_ref, stat_ref, q_s, k_s, v_s, oh_s, mask_s):
    at = pl.program_id(0)

    @pl.when(at == 0)
    def _():
        far_out[...] = far_ref[0]
        grad_out[...] = grad_ref[0]
        ids = seg_ref[pl.ds(spot_ref[4], 1), :]
        one_hot(ids, oh_s)
        mask_of(ids, mask_s)
        x, y = x_ref[0], y_ref[0]
        q_s[...] = (dot(x, wq_ref[...]) + vec_ref[V_QB : V_QB + 1, :]).astype(BF)
        k_s[...] = dot(x, wk_ref[...]).astype(BF)
        v_s[...] = (dot(x, wv_ref[...]) + vec_ref[V_VB : V_VB + 1, :]).astype(BF)
        mk_ref[...] = dot(y, uk_ref[...]).astype(BF)
        mv_ref[...] = (dot(y, uv_ref[...]) + vec_ref[V_CVB : V_CVB + 1, :]).astype(BF)
        q_ref[...], k_ref[...], v_ref[...] = q_s[...], k_s[...], v_s[...]

    @pl.when(at > 0)
    def _():
        cols = columns(at - 1)
        for h, (o, m, l) in enumerate(attend_near(q_s[:, cols], k_s[:, cols], v_s[:, cols], oh_s[...], mask_s[...])):
            mix_ref[64 * h : 64 * h + 64, :] = o
            stat_ref[0, h : h + 1, :] = m
            stat_ref[0, 2 + h : 3 + h, :] = l


def project_near(order, spots, tgt, hidden_in, memory, out_grad, vec, weights):
    half, D = hidden_in.shape[1:]
    pairs = D // 128
    x = pl.BlockSpec((1, half, D), lambda i, p: (p[4], 0, 0))
    other = pl.BlockSpec((1, half, D), lambda i, p: (1 - p[4], 0, 0))
    pair = lambda i: jnp.maximum(i - 1, 0)
    big = pltpu.VMEM((half, D), BF)
    return order.call(
        near_kernel, spots, tgt, hidden_in, memory, memory, out_grad, vec, *weights, scalars=1, name="project_near", us=14,
        grid=(1 + pairs,), in_specs=[full(tgt.shape), x, x, other, other, full(vec.shape)] + [full((D, D))] * 5,
        out_specs=[still((half, D))] * 7 + [pl.BlockSpec((128, half), lambda i, p: (pair(i), 0)),
                                            pl.BlockSpec((1, 8, half), lambda i, p: (pair(i), 0, 0))],
        out_shape=[shaped(half, D)] * 7 + [shaped(D, half, dtype=F32), shaped(pairs, 8, half, dtype=F32)],
        scratch_shapes=[big] * 3 + [pltpu.VMEM((64, half), BF), pltpu.VMEM((half, 128), BF)])


class Loads:
    def __init__(self, sem):
        self.sem = sem
        self.copies = []

    def add(self, src, dst):
        self.copies.append(pltpu.make_async_copy(src, dst, self.sem.at[len(self.copies)]))
        return self.copies[-1]


def columns(p, width=128):
    return pl.ds(pl.multiple_of(p * width, width), width)


def self_kernel(spot_ref, vec_ref, seg_ref, mix_ref, stat_ref, hin_ref, hgot_ref, qn_ref, kn_ref, vn_ref, wq_ref, wk_ref, wv_ref, wo_ref, wc_ref,
                l_ref, n_ref, r_ref, low_ref, cq_ref, oh_ref, mk_ref, cross_mk_ref, h_out, q_out, k_out, v_out, m_out,
                h_s, q_s, k_s, v_s, m_s, wq_s, wk_s, wv_s, wo_s, wc_s, sem, *, pairs):
    v = lambda i: vec_ref[i : i + 1, :]
    at = pl.program_id(0)
    half = hgot_ref.shape[0]
    s = spot_ref[4]
    near = pl.ds(pl.multiple_of(s * half, half), half)
    far = pl.ds(pl.multiple_of((1 - s) * half, half), half)
    loads = Loads(sem)
    got = loads.add(hgot_ref, h_s.at[far])
    in_q, in_k, in_v = loads.add(wq_ref, wq_s), loads.add(wk_ref, wk_s), loads.add(wv_ref, wv_s)
    own = [loads.add(hin_ref.at[s], h_s.at[near])]
    own += [loads.add(a, b.at[near]) for a, b in ((qn_ref, q_s), (kn_ref, k_s), (vn_ref, v_s))]
    later = [loads.add(wo_ref, wo_s), loads.add(wc_ref, wc_s)]
    outs = [loads.add(a, b) for a, b in ((h_s, h_out), (q_s, q_out), (k_s, k_out), (v_s, v_out))]
    mixed_out = loads.add(m_s, m_out)

    @pl.when(at == 0)
    def _():
        for c in (got, in_q, in_k, in_v, *own, *later):
            c.start()
        one_hot(seg_ref[0:1, :], oh_ref)
        mask_of(seg_ref[0:1, :], mk_ref)
        mask_of(seg_ref[1:2, :], cross_mk_ref)
        got.wait()
        x = h_s[far, :]
        in_q.wait()
        q_s[far, :] = (dot(x, wq_s[...]) + v(V_QB)).astype(BF)
        in_k.wait()
        k_s[far, :] = dot(x, wk_s[...]).astype(BF)
        in_v.wait()
        v_s[far, :] = (dot(x, wv_s[...]) + v(V_VB)).astype(BF)
        for c in own:
            c.wait()
        for c in outs:
            c.start()

    @pl.when((at > 0) & (at <= pairs))
    def _():
        cols = columns(at - 1)

        args = lambda q, k: (q_s[q, cols], k_s[k, cols], v_s[k, cols], oh_ref[:, q], mk_ref[k, :])
        lo, hi = pl.ds(0, half), pl.ds(half, half)
        near_sums = [(mix_ref[64 * h : 64 * h + 64, :], stat_ref[0, h : h + 1, :], stat_ref[0, 2 + h : 3 + h, :]) for h in (0, 1)]
        heads = attend_rest(s == 0, near_sums, args(far, far), args(hi, lo))
        for i, rows in enumerate((lo, hi)):
            for h in (0, 1):
                l_ref[0, h : h + 1, rows] = heads[h][i][1]
            m_s[rows, cols] = jnp.concatenate([heads[h][i][0] for h in (0, 1)], 0).T.astype(BF)

    @pl.when(at == pairs + 1)
    def _():
        mixed_out.start()
        for c in later:
            c.wait()

    @pl.when(at > pairs)
    def _():
        rows = pl.ds(pl.multiple_of((at - pairs - 1) * half, half), half)
        x = h_s[rows, :].astype(F32) + (dot(m_s[rows, :], wo_s[...]) + v(V_OB))
        n, r = norm_stats(x)
        n_ref[...] = n
        r_ref[...] = r
        low = (n * v(V_G1) + v(V_B1)).astype(BF)
        low_ref[...] = low
        cq_ref[...] = (dot(low, wc_s[...]) + v(V_CQB)).astype(BF)

    @pl.when(at == pairs + 2)
    def _():
        for c in (*outs, mixed_out):
            c.wait()


def self_forward(order, spots, vec, segs, near_mix, near_stats, hidden_in, hidden_got, near, weights):
    half, D = hidden_got.shape
    T, pairs = 2 * half, D // 128
    token = lambda width: pl.BlockSpec((half, width), lambda i, p: (jnp.maximum(i - pairs - 1, 0), 0))
    hbm = pl.BlockSpec(memory_space=pl.ANY)
    masks = [(64, T), (T, 128), (T, 128)]
    pair = lambda i: jnp.clip(i - 1, 0, pairs - 1)
    return order.call(
        functools.partial(self_kernel, pairs=pairs), spots, vec, segs, near_mix, near_stats, hidden_in, hidden_got, *near, *weights,
        scalars=1, name="self_forward", us=25, grid=(pairs + 3,),
        in_specs=[full(vec.shape), full(segs.shape), pl.BlockSpec((128, half), lambda i, p: (pair(i), 0)),
                  pl.BlockSpec((1, 8, half), lambda i, p: (pair(i), 0, 0))] + [hbm] * 10,
        out_specs=[pl.BlockSpec((1, 8, T), lambda i, p: (pair(i), 0, 0)),
                   token(D), token(1), token(D), token(D)] + [still(s) for s in masks] + [hbm] * 5,
        out_shape=[shaped(pairs, 8, T, dtype=F32), shaped(T, D, dtype=F32), shaped(T, 1, dtype=F32), shaped(T, D), shaped(T, D)]
        + [shaped(*s) for s in masks] + [shaped(T, D)] * 5,
        scratch_shapes=[pltpu.VMEM((T, D), BF)] * 5 + [pltpu.VMEM((D, D), BF)] * 5 + [pltpu.SemaphoreType.DMA((15,))])


def cross_kernel(spot_ref, vec_ref, oh_ref, mask_ref, cq_ref, min_ref, mgot_ref, kn_ref, vn_ref, uk_ref, uv_ref,
                 l_ref, m_out, k_out, v_out, c_out, m_s, k_s, v_s, q_s, c_s, uk_s, uv_s, sem, *, pairs, bq):
    at = pl.program_id(0)
    half = mgot_ref.shape[0]
    s = spot_ref[4]
    near = pl.ds(pl.multiple_of(s * half, half), half)
    far = pl.ds(pl.multiple_of((1 - s) * half, half), half)
    loads = Loads(sem)
    got = loads.add(mgot_ref, m_s.at[far])
    in_k, in_v = loads.add(uk_ref, uk_s), loads.add(uv_ref, uv_s)
    own = [loads.add(min_ref.at[s], m_s.at[near]), loads.add(cq_ref, q_s)]
    own += [loads.add(kn_ref, k_s.at[near]), loads.add(vn_ref, v_s.at[near])]
    outs = [loads.add(a, b) for a, b in ((m_s, m_out), (k_s, k_out), (v_s, v_out))]

    @pl.when(at == 0)
    def _():
        for c in (got, in_k, in_v, *own):
            c.start()
        got.wait()
        x = m_s[far, :]
        in_k.wait()
        k_s[far, :] = dot(x, uk_s[...]).astype(BF)
        in_v.wait()
        v_s[far, :] = (dot(x, uv_s[...]) + vec_ref[V_CVB : V_CVB + 1, :]).astype(BF)
        for c in own:
            c.wait()
        for c in outs:
            c.start()

    @pl.when(at > 0)
    def _():
        cols = columns(at - 1)

        def put_total(h, i, row):
            l_ref[0, h : h + 1, i * bq : (i + 1) * bq] = row

        blocks = attend_pair(q_s[:, cols], k_s[:, cols], v_s[:, cols], oh_ref[...], mask_ref[...], put_total, bq)
        for i, b in enumerate(blocks):
            c_out[i * bq : (i + 1) * bq, :] = b

    @pl.when(at == pairs)
    def _():
        for c in outs:
            c.wait()


def cross_forward(order, spots, vec, oh, mask, cq, memory, memory_got, near, weights):
    half, D = memory_got.shape
    T, pairs = 2 * half, D // 128
    hbm = pl.BlockSpec(memory_space=pl.ANY)
    pair = lambda i: jnp.maximum(i - 1, 0)
    return order.call(
        functools.partial(cross_kernel, pairs=pairs, bq=512), spots, vec, oh, mask, cq, memory, memory_got, *near, *weights,
        scalars=1, name="cross_forward", us=23, grid=(pairs + 1,),
        in_specs=[full(a.shape) for a in (vec, oh, mask)] + [hbm] * 7,
        out_specs=[pl.BlockSpec((1, 8, T), lambda i, p: (pair(i), 0, 0))] + [hbm] * 3
        + [pl.BlockSpec((T, 128), lambda i, p: (0, pair(i)))],
        out_shape=[shaped(pairs, 8, T, dtype=F32)] + [shaped(T, D)] * 4,
        scratch_shapes=[pltpu.VMEM((T, D), BF)] * 4 + [pltpu.VMEM((16, 128), BF)] + [pltpu.VMEM((D, D), BF)] * 2
        + [pltpu.SemaphoreType.DMA((10,))])


def ffn_kernel(spot_ref, vec_ref, bin_ref, n1_ref, cm_ref, og_ref, oggot_ref, wco_ref, win_ref, wout_ref,
               own_ref, other_ref, sb_ref, cmb_ref, vo_ref, vi_ref, all_ref,
               act_s, ib_s, cm_s, og_s, wco_s, win_s, wout_s, fb_s, low_s, cb_s, stage_s, stage_sem, sem, *, parts):
    v = lambda i: vec_ref[i : i + 1, :]
    t = pl.program_id(0)
    half, D = oggot_ref.shape
    s = spot_ref[4]
    loads = Loads(sem)
    in_cm, in_co = loads.add(cm_ref, cm_s), loads.add(wco_ref, wco_s)
    in_up, in_down = loads.add(win_ref, win_s), loads.add(wout_ref, wout_s)
    in_og = [loads.add(og_ref.at[s], og_s.at[s]), loads.add(oggot_ref, og_s.at[1 - s])]

    def need(*copies):
        @pl.when(t == 0)
        def _():
            for c in copies:
                c.wait()

    @pl.when(t == 0)
    def _():
        for c in loads.copies:
            c.start()
        vo_ref[...] = jnp.zeros_like(vo_ref)
        vi_ref[...] = jnp.zeros_like(vi_ref)

    @pl.when(t < 2)
    def _():
        need(in_cm, in_co)
        rows = pl.ds(pl.multiple_of(t * half, half), half)
        first = n1_ref[...] * v(V_G1) + v(V_B1)
        n2, r2 = norm_stats(first + (dot(cm_s[rows, :], wco_s[...]) + v(V_COB)))
        second = n2 * v(V_G2) + v(V_B2)
        low = second.astype(BF)
        low_s[rows, :] = low
        need(in_up, in_down, *in_og)
        width = win_s.shape[1] // parts
        branch = None
        up = lambda c: dot(low, win_s[:, c * width : (c + 1) * width]) + bin_ref[:, c * width : (c + 1) * width]
        x = up(0)
        late = None
        for c in range(parts):
            cols = slice(c * width, (c + 1) * width)
            coming = up(c + 1) if c + 1 < parts else None
            act, slope = gelu_pair(x)
            ib_s[rows, cols] = slope.astype(BF)
            act = act.astype(BF)
            act_s[rows, cols] = act
            if late is not None:
                term = dot(late[1], wout_s[late[0], :])
                branch = term if branch is None else branch + term
            late = cols, act
            x = coming
        term = dot(late[1], wout_s[late[0], :])
        branch = term if branch is None else branch + term
        n3, r3 = norm_stats(second + (branch + v(V_FOB)))
        ho = (n3 * v(V_G3) + v(V_B3)).astype(BF)

        @pl.when(t == s)
        def _():
            own_ref[...] = ho

        @pl.when(t != s)
        def _():
            other_ref[...] = ho

        e = og_s[t].astype(F32)
        third = norm_back(e, n3, r3, v(V_G3))
        fb = third.astype(BF)
        fb_s[rows, :] = fb
        vo_ref[0:1, :] += sums(e * n3)
        vo_ref[1:2, :] += sums(e)
        vo_ref[2:3, :] += sums(fb.astype(F32))
        e = third
        up = lambda c: nt(fb, wout_s[c * width : (c + 1) * width, :])
        x = up(0)
        late = None
        for c in range(parts):
            cols = slice(c * width, (c + 1) * width)
            coming = up(c + 1) if c + 1 < parts else None
            ib = (x * ib_s[rows, cols].astype(F32)).astype(BF)
            ib_s[rows, cols] = ib
            vi_ref[:, cols] += sums(ib.astype(F32))
            if late is not None:
                e = e + nt(late[1], win_s[:, late[0]])
            late = cols, ib
            x = coming
        e = e + nt(late[1], win_s[:, late[0]])
        back = norm_back(e, n2, r2, v(V_G2))
        sb_ref[...] = back
        cb = back.astype(BF)
        cb_s[rows, :] = cb
        vo_ref[3:4, :] += sums(e * n2)
        vo_ref[4:5, :] += sums(e)
        vo_ref[5:6, :] += sums(cb.astype(F32))
        cmb_ref[...] = nt(cb, wco_s[...]).astype(BF)

    t = t - 2
    slot = t % 2

    def tall(b, slot):
        return pltpu.make_async_copy(stage_s.at[slot], all_ref.at[b, :, pl.ds(0, 4)], stage_sem.at[slot])

    def flat(b, slot):
        return pltpu.make_async_copy(stage_s.at[slot], all_ref.at[:, :, 4 + b], stage_sem.at[slot])

    @pl.when((t >= 2) & (t < 6))
    def _():
        tall(t - 2, slot).wait()

    @pl.when(t >= 6)
    def _():
        flat(t - 6, slot).wait()

    def put(x, g):
        stage_s[slot] = tn(x, g).astype(BF).reshape(4, 4, 48, D)

    @pl.when((t >= 0) & (t < 4))
    def _():
        put(act_s[:, columns(t, D)], fb_s[...])
        tall(t, slot).start()

    @pl.when((t >= 4) & (t < 8))
    def _():
        put(low_s[...], ib_s[:, columns(t - 4, D)])
        flat(t - 4, slot).start()

    @pl.when(t == 8)
    def _():
        put(cm_s[...], cb_s[...])
        flat(4, 0).start()
        flat(3, 1).wait()
        flat(4, 0).wait()


def ffn_both(order, spots, vec, bin_, n1, cm, out_grad, out_grad_got, weights):
    half, D = out_grad_got.shape
    T, FF = 2 * half, bin_.shape[1]
    token = lambda width: pl.BlockSpec((half, width), lambda i, p: (jnp.minimum(i, 1), 0))
    hbm = pl.BlockSpec(memory_space=pl.ANY)
    big = lambda *shape: pltpu.VMEM(shape, BF)
    return order.call(
        functools.partial(ffn_kernel, parts=6), spots, vec, bin_, n1, cm, out_grad, out_grad_got, *weights,
        scalars=1, name="ffn_both", us=60, grid=(11,),
        in_specs=[full(vec.shape), full(bin_.shape), token(D)] + [hbm] * 6,
        out_specs=[still((half, D)), still((half, D)), token(D), token(D), still((8, D)), still((1, FF)), hbm],
        out_shape=[shaped(half, D), shaped(half, D), shaped(T, D, dtype=F32), shaped(T, D),
                   shaped(8, D, dtype=F32), shaped(1, FF, dtype=F32), shaped(4, 4, 9, 48, D)],
        scratch_shapes=[big(T, FF), big(T, FF), big(T, D), big(2, half, D), big(D, D), big(D, FF), big(FF, D), big(T, D), big(T, D),
                        big(T, D), big(2, 4, 4, 48, D), pltpu.SemaphoreType.DMA((2,)), pltpu.SemaphoreType.DMA((6,))])


def cross_back_kernel(spot_ref, q_ref, k_ref, v_ref, do_ref, o_ref, l_ref, oh_ref, mask_ref, wk_in, wv_in,
                      dq_ref, dk_ref, dv_ref, own_ref, other_ref, acc_s, dk_s, dv_s, wk_s, wv_s, sem, *, pairs, bk):
    at = pl.program_id(0)
    half = own_ref.shape[0]
    loads = Loads(sem)
    loads.add(wk_in, wk_s), loads.add(wv_in, wv_s)

    @pl.when(at == 0)
    def _():
        for c in loads.copies:
            c.start()

    @pl.when(at < pairs)
    def _():
        out = {"q": dq_ref, "k": dk_ref, "v": dv_ref}

        def put(name, rows, block):
            out[name][rows, :] = block
            if name != "q":
                {"k": dk_s, "v": dv_s}[name][rows, columns(at)] = block

        attend_pair_back(q_ref[...], k_ref[...], v_ref[...], do_ref[...], o_ref[...], [l_ref[0, h : h + 1, :] for h in (0, 1)],
                         oh_ref[...], mask_ref[...], acc_s, put, bk, False)

    @pl.when(at == pairs)
    def _():
        for c in loads.copies:
            c.wait()

    t = at - pairs

    @pl.when(t >= 0)
    def _():
        rows = pl.ds(pl.multiple_of(t * half, half), half)
        mg = (nt(dk_s[rows, :], wk_s[...]) + nt(dv_s[rows, :], wv_s[...])).astype(BF)

        @pl.when(t == spot_ref[4])
        def _():
            own_ref[...] = mg

        @pl.when(t != spot_ref[4])
        def _():
            other_ref[...] = mg


def cross_back(order, spots, q, k, v, do, o, totals, oh, mask, weights):
    T, D = q.shape
    pairs, half = D // 128, T // 2
    p_in = lambda i: jnp.minimum(i, pairs - 1)
    pair = pl.BlockSpec((T, 128), lambda i, p: (0, p_in(i)))
    hbm = pl.BlockSpec(memory_space=pl.ANY)
    return order.call(
        functools.partial(cross_back_kernel, pairs=pairs, bk=512), spots, q, k, v, do, o, totals, oh, mask, *weights,
        scalars=1, name="cross_back", us=38, grid=(pairs + 2,),
        in_specs=[pair] * 5 + [pl.BlockSpec((1, 8, T), lambda i, p: (p_in(i), 0, 0)), full(oh.shape), full(mask.shape), hbm, hbm],
        out_specs=[pair] * 3 + [still((half, D))] * 2, out_shape=[shaped(T, D)] * 3 + [shaped(half, D)] * 2,
        scratch_shapes=[pltpu.VMEM((128, T), F32)] + [pltpu.VMEM((T, D), BF)] * 2 + [pltpu.VMEM((D, D), BF)] * 2
        + [pltpu.SemaphoreType.DMA((2,))])


def middle_kernel(spot_ref, vec_ref, q_ref, n_ref, r_ref, sb_ref,
                  k_in, v_in, low_in, src_in, mix_in, wq_in, wo_in,
                  fb_ref, mb_ref, vo_ref, send_ref, keep_ref,
                  dq_s, dk_s, dv_s, back_s, low_s, src_s, mix_s, wq_s, wo_s, sem):
    v = lambda i: vec_ref[i : i + 1, :]
    t = pl.program_id(0)
    half, D = mb_ref.shape
    loads = Loads(sem)
    first = [loads.add(wq_in, wq_s), loads.add(wo_in, wo_s)]
    last = [loads.add(a, b) for a, b in ((low_in, low_s), (src_in, src_s), (mix_in, mix_s), (k_in, dk_s), (v_in, dv_s))]

    @pl.when(t == 0)
    def _():
        for c in loads.copies:
            c.start()
        vo_ref[...] = jnp.zeros_like(vo_ref)
        for c in first:
            c.wait()

    @pl.when(t < 2)
    def _():
        rows = pl.ds(pl.multiple_of(t * half, half), half)
        dq = q_ref[...]
        dq_s[rows, :] = dq
        n = n_ref[...]
        e = sb_ref[...] + nt(dq, wq_s[...])
        back = norm_back(e, n, r_ref[...], v(V_G1))
        fb_ref[...] = back
        low = back.astype(BF)
        back_s[rows, :] = low
        vo_ref[0:1, :] += sums(e * n)
        vo_ref[1:2, :] += sums(e)
        vo_ref[2:3, :] += sums(low.astype(F32))
        vo_ref[3:4, :] += sums(dq.astype(F32))
        mb_ref[...] = nt(low, wo_s[...]).astype(BF)

    @pl.when(t == 2)
    def _():
        for c in last:
            c.wait()
        vo_ref[4:5, :] = sums(dv_s[...].astype(F32))

    for i, (x, g) in enumerate(((low_s, dq_s), (src_s, dk_s), (src_s, dv_s), (mix_s, back_s))):
        @pl.when(t == 2 + i)
        def _():
            total = tn(x[...], g[...]).astype(BF)
            def put_piece(which, x, zl, zh, rows):
                for k in range(2):
                    (send_ref, keep_ref)[which][at_of(CROSS, x=x, y=k, zl=zl, zh=zh) + (0,)] = rows[:, D // 2 * k : D // 2 * (k + 1)]

            place_rows(spot_ref[0], total, 48, put_piece)


def middle(order, spots, vec, dq, dk, dv, n1, r1, sb, low, source, mixed, weights):
    T, D = n1.shape
    half = T // 2
    token = lambda width: pl.BlockSpec((half, width), lambda i, p: (jnp.minimum(i, 1), 0))
    out = pl.BlockSpec((2, 2, 2, 2, 1, 48, D // 2), lambda i, p: (0, 0, 0, 0, jnp.maximum(i - 2, 0), 0, 0))
    hbm = pl.BlockSpec(memory_space=pl.ANY)
    square, rect = pltpu.VMEM((D, D), BF), pltpu.VMEM((T, D), BF)
    return order.call(
        middle_kernel, spots, vec, dq, n1, r1, sb, dk, dv, low, source, mixed, *weights, scalars=1, name="middle", us=18,
        grid=(6,),
        in_specs=[full(vec.shape)] + [token(D), token(D), token(1), token(D)] + [hbm] * 7,
        out_specs=[token(D), token(D), still((8, D)), out, out],
        out_shape=[shaped(T, D, dtype=F32), shaped(T, D), shaped(8, D, dtype=F32)]
        + [shaped(2, 2, 2, 2, 4, 48, D // 2)] * 2,
        scratch_shapes=[rect] * 7 + [square] * 2 + [pltpu.SemaphoreType.DMA((7,))])


def back_kernel(spot_ref, *refs, counts):
    n = len(counts)
    g, rest = refs[: sum(counts)], refs[sum(counts) :]
    w, (plain_ref, own_ref, other_ref) = rest[:n], rest[n:]
    total = plain_ref[...]
    for i, count in enumerate(counts):
        total = total + nt(joined(g[:count]), w[i][...])
        g = g[count:]
    total = total.astype(BF)

    @pl.when(pl.program_id(0) == spot_ref[4])
    def _():
        own_ref[...] = total

    @pl.when(pl.program_id(0) != spot_ref[4])
    def _():
        other_ref[...] = total


def back_rows(order, spots, grads, weights, plain, moves):
    parts = [p for g in grads for p in g]
    T, D = plain.shape
    half = T // 2
    r = lambda width: pl.BlockSpec((half, width), lambda i, p: (i, 0))
    return order.call(
        functools.partial(back_kernel, counts=[len(g) for g in grads]), spots, *parts, *weights, plain,
        scalars=1, name="back_rows", us=9, grid=(2,), moves=moves,
        in_specs=[r(p.shape[1]) for p in parts] + [full((D, D))] * len(weights) + [r(D)],
        out_specs=[still((half, D))] * 2, out_shape=[shaped(half, D)] * 2)


def place_rows(core, total, height, put):
    for j in range(total.shape[0] // (2 * height)):
        even = total[2 * j * height : (2 * j + 1) * height]
        odd = total[(2 * j + 1) * height : (2 * j + 2) * height]
        put(1, j % 2, (j // 2) % 2, j // 4, jnp.where(core == 0, even, odd))
        put(0, j % 2, (j // 2) % 2, j // 4, jnp.where(core == 0, odd, even))


CROSS = "y", "zl", "x", "zh"
CROSS_LINKS = *CROSS, "gather"
SELF_LINKS = "x", "zl", "zh", "sum"


def at_of(order, **place):
    return tuple(place[name] for name in order)


def joined(refs):
    return refs[0][...] if len(refs) == 1 else jnp.concatenate([r[...] for r in refs], 1)


def self_back_kernel(spot_ref, q_ref, k_ref, v_ref, do_ref, o_ref, l_ref, oh_ref, mk_ref, vf_ref, v1_ref, vi_ref, h_in,
                     dq_ref, dk_ref, dv_ref, send_ref, keep_ref, acc_s, g_s, h_s, sem, *, pairs, bk):
    at = pl.program_id(0)
    hidden = pltpu.make_async_copy(h_in, h_s, sem)
    D = 128 * pairs
    wide = D // 2

    @pl.when(at == 0)
    def _():
        hidden.start()

    @pl.when(at < pairs)
    def _():
        out = {"q": (dq_ref, 0), "k": (dk_ref, 1), "v": (dv_ref, 2)}

        def put(name, rows, block):
            ref, i = out[name]
            ref[rows, :] = block
            g_s[i, rows, columns(at)] = block

        attend_pair_back(q_ref[...], k_ref[...], v_ref[...], do_ref[...], o_ref[...], [l_ref[0, h : h + 1, :] for h in (0, 1)],
                         oh_ref[...], mk_ref[...], acc_s, put, bk, True)

    core = spot_ref[0]
    height = 6 * 48 + 16

    for i in range(3):
        @pl.when(at == pairs + i)
        def _():
            if i == 0:
                hidden.wait()

            def put_piece(which, x, zl, zh, rows):
                for k in range(2):
                    at_row = height * (4 * x + 2 * zl + zh) + 96 * i + 48 * k
                    (send_ref, keep_ref)[which][at_row : at_row + 48, :] = rows[:, wide * k : wide * (k + 1)]

            place_rows(core, tn(h_s[...], g_s[i]).astype(BF), 48, put_piece)

    @pl.when(at == pairs + 2)
    def _():
        row_of = lambda i: sums(g_s[i].astype(F32))
        rows = jnp.concatenate([vf_ref[0:6, :], v1_ref[0:5, :], row_of(0), row_of(2), jnp.zeros((3, D), F32)], 0)
        spread = jnp.broadcast_to(vi_ref[...], (16, vi_ref.shape[1]))
        for first, part, w in ((0, rows, 48), (128, spread, 192)):
            for j in range(8):
                even = part[:, 2 * j * w : (2 * j + 1) * w].astype(BF)
                odd = part[:, (2 * j + 1) * w : (2 * j + 2) * w].astype(BF)
                at_row = height * (4 * (j % 2) + 2 * ((j // 2) % 2) + j // 4) + 288
                keep_ref[at_row : at_row + 16, first : first + w] = jnp.where(core == 0, even, odd)
                send_ref[at_row : at_row + 16, first : first + w] = jnp.where(core == 0, odd, even)


def self_back(order, spots, q, k, v, do, o, totals, oh, mk, vectors, hidden, moves):
    T, D = q.shape
    pairs = D // 128
    p_in = lambda i: jnp.minimum(i, pairs - 1)
    pair = pl.BlockSpec((T, 128), lambda i, p: (0, p_in(i)))
    rows = 8 * (6 * 48 + 16)
    return order.call(
        functools.partial(self_back_kernel, pairs=pairs, bk=256), spots, q, k, v, do, o, totals, oh, mk, *vectors, hidden,
        scalars=1, name="self_back", us=30, grid=(pairs + 3,), moves=moves,
        in_specs=[pair] * 5 + [pl.BlockSpec((1, 8, T), lambda i, p: (p_in(i), 0, 0))]
        + [full(a.shape) for a in (oh, mk, *vectors)] + [pl.BlockSpec(memory_space=pl.ANY)],
        out_specs=[pair] * 3 + [still((rows, D // 2))] * 2, out_shape=[shaped(T, D)] * 3 + [shaped(rows, D // 2)] * 2,
        scratch_shapes=[pltpu.VMEM((128, T), F32), pltpu.VMEM((3, T, D), BF), pltpu.VMEM((T, D), BF), pltpu.SemaphoreType.DMA])


def fold_kernel(spot_ref, keep_ref, keep_other_ref, got_ref, got_other_ref, sum_ref, send_ref):
    sum_ref[...] = keep_ref[0] + got_ref[0]
    send_ref[...] = keep_other_ref[0] + got_other_ref[0]


def small_fold_kernel(spot_ref, *refs, items, keeps, gots):
    keep_refs, got_refs, outs = refs[:keeps], refs[keeps : keeps + gots], refs[keeps + gots :]
    for i, (came, spots, messages) in enumerate(items):
        keep, out = keep_refs[i], outs[i]
        rows = out.shape[0]

        def piece(p):
            part = lambda first: pl.ds(pl.multiple_of(first + p * rows, 16), rows)
            total = keep[part(0), :]
            for g, at in came:
                total = total + got_refs[g][part(at), :]
            return total

        mine = 0
        for s in spots:
            mine = 2 * mine + spot_ref[s]
        out[...] = piece(mine)
        for n, (m, first) in enumerate(messages):
            outs[keeps + m][first : first + rows, :] = out[...] if not spots else piece(mine ^ (n + 1))


LINKS = {"core": ([("dp", 1, 16)], (0,)), "x": ([("dp", 2, 16)], (1,)), "zl": ([("dp", 4, 16)], (2,)), "zh": ([("dp", 8, 16)], (3,)),
         "z": ([("dp", 8, 16), ("dp", 4, 16), ("dp", 12, 16)], (2, 3)), "y": ([("seq", 1, 2)], (4,)),
         "sum": ([("seq", 1, 2)], ()), "gather": ([("seq", 1, 2)], ())}


class Sum:
    def __init__(self, keep, got, *links):
        self.keep, self.gots = keep, [(got, 0)]
        self.links, self.step = links, 0

    def link(self):
        return self.links[self.step] if self.step < len(self.links) else None


def first_swap(send, keep, after=None):
    if after is not None:
        send, _ = lax.optimization_barrier((send, after))
    flat = lambda a: a.reshape(-1, a.shape[-1])
    return flat(keep), swap(flat(send), *LINKS["core"][0][0])


def advance(order, spots, *groups):
    groups = [g for g in groups if g.link() is not None]
    links = [LINKS[g.link()] for g in groups]
    rows = [g.keep.shape[0] >> len(places) for g, (_, places) in zip(groups, links)]
    if len(groups) == 1 and len(links[0][1]) == 1 and len(groups[0].gots) == 1:
        (g,), ((to,), (which,)), (r,) = groups, links[0], rows
        width = g.keep.shape[1]
        steps = next(s for s in (4, 2, 1) if r % (16 * s) == 0)
        keep, got = g.keep.reshape(2, r, width), g.gots[0][0].reshape(2, r, width)
        mine = pl.BlockSpec((1, r // steps, width), lambda i, p: (p[which], i, 0))
        other = pl.BlockSpec((1, r // steps, width), lambda i, p: (1 - p[which], i, 0))
        g.keep, send = order.call(
            fold_kernel, spots, keep, keep, got, got, scalars=1, name="fold", us=3, grid=(steps,),
            in_specs=[mine, other, mine, other], out_specs=[pl.BlockSpec((r // steps, width), lambda i, p: (i, 0))] * 2,
            out_shape=[shaped(r, width)] * 2)
        g.gots = [(swap(send, *to), 0)]
        g.step += 1
        return
    gots = []
    for g in groups:
        for a, _ in g.gots:
            if not any(a is b for b in gots):
                gots.append(a)
    messages, heights, items = [], [], []
    for g, (tos, places), r in zip(groups, links, rows):
        sent = []
        for to in tos:
            key = to, g.keep.shape[1]
            if key not in messages:
                messages.append(key)
                heights.append(0)
            m = messages.index(key)
            sent.append((m, heights[m]))
            heights[m] += r
        items.append(([(next(n for n, b in enumerate(gots) if a is b), at) for a, at in g.gots], places, sent))
    shapes = [(r, g.keep.shape[1]) for r, g in zip(rows, groups)] + [(h, w) for h, (_, w) in zip(heights, messages)]
    arrays = [g.keep for g in groups] + gots
    out = order.call(
        functools.partial(small_fold_kernel, items=items, keeps=len(groups), gots=len(gots)), spots, *arrays, scalars=1,
        name="fold", us=3, grid=(1,), in_specs=[full(a.shape) for a in arrays],
        out_specs=[still(s) for s in shapes], out_shape=[shaped(*s) for s in shapes])
    came = [swap(out[len(groups) + m], *to) for m, (to, _) in enumerate(messages)]
    for i, g in enumerate(groups):
        g.keep = out[i]
        g.gots = [(came[m], first) for m, first in items[i][2]]
        g.step += 1


def finish_kernel(spot_ref, ffn_ref, ffn_got_ref, cross_ref, cross_got_ref, self_ref, self_got_ref, *outs, cross_at, self_at):
    (sq, sk, sv, so, cq, ck, cv, co, fi, fo, *vectors) = outs
    f32 = lambda v: v.astype(F32)
    D = ffn_ref.shape[1]
    w = D // 2
    unit = lambda v, u: f32(v[48 * u : 48 * u + 48])
    ffn = ffn_ref[...] + ffn_got_ref[...]
    fo[...] = f32(ffn[0:192, :])
    for b in range(4):
        fi[:, D * b : D * (b + 1)] = unit(ffn, 4 + b)
    co[...] = unit(ffn, 8)
    first = spot_ref[4] == 0
    own, got = cross_ref[...], cross_got_ref[cross_at : cross_at + cross_ref.shape[0], :]
    cross = jnp.where(first, own, got), jnp.where(first, got, own)
    sums_ = self_ref[...] + self_got_ref[self_at : self_at + self_ref.shape[0], :]
    for k in range(2):
        cols = slice(k * w, (k + 1) * w)
        for i, o in enumerate((cq, ck, cv, so)):
            o[:, cols] = unit(cross[k], i)
        for i, o in enumerate((sq, sk, sv)):
            o[:, cols] = unit(sums_, 2 * i + k)
    rows = f32(sums_[288:304])
    for i, o in enumerate(vectors[:13]):
        o[...] = rows[i : i + 1, :48]
    vectors[13][...] = rows[0:1, 128:320]


def finish(order, spots, ffn, ffn_got, cross, own):
    D = ffn.shape[1]
    ((cross_got, cross_at),), ((own_got, own_at),) = cross.gots, own.gots
    arrays = ffn, ffn_got, cross.keep, cross_got, own.keep, own_got
    shapes = [(48, D)] * 8 + [(48, 4 * D), (192, D)] + [(1, 48)] * 13 + [(1, 192)]
    return order.call(
        functools.partial(finish_kernel, cross_at=cross_at, self_at=own_at), spots, *arrays, scalars=1,
        name="finish", us=3, grid=(1,), in_specs=[full(a.shape) for a in arrays], out_specs=[still(s) for s in shapes],
        out_shape=[shaped(*s, dtype=F32) for s in shapes])


def swap(block, ax, bit, size):
    return lax.ppermute(block, ax, [(i, i ^ bit) for i in range(size)])


def two(s, first, second):
    return jnp.where(s == 0, jnp.concatenate([first, second], 0), jnp.concatenate([second, first], 0))


def pick(array, index, axis):
    return lax.dynamic_index_in_dim(array, index, axis, keepdims=False)


def whole_rows(
    hidden_in, memory, tgt_segment, src_segment, out_grad,
    self_query, query_bias, self_key, self_value, value_bias, self_output, output_bias,
    first_gain, first_shift,
    cross_query, cross_query_bias, cross_key, cross_value, cross_value_bias, cross_output,
    cross_output_bias, second_gain, second_shift,
    ffn_in, ffn_in_bias, ffn_out, ffn_out_bias, third_gain, third_shift,
):
    f32 = lambda v: v.astype(F32)
    s = lax.axis_index("seq")
    dp = lax.axis_index("dp")
    place = dp % 2, (dp // 2) % 2, (dp // 4) % 2, dp // 8, s
    spots = jnp.stack(place).astype(jnp.int32)
    order = Order()
    segs = jnp.stack([tgt_segment, src_segment])
    segs_own, segs_got = pick(segs, s, 1), swap(pick(segs, 1 - s, 1), "seq", 1, 2)
    segs = jnp.where(s == 0, jnp.concatenate([segs_own, segs_got], 1), jnp.concatenate([segs_got, segs_own], 1))
    hidden_got = swap(pick(hidden_in, 1 - s, 0), "seq", 1, 2)
    vec = jnp.stack([query_bias, value_bias, output_bias, first_gain, first_shift, cross_query_bias, cross_value_bias,
                     cross_output_bias, second_gain, second_shift, ffn_out_bias, third_gain, third_shift]).astype(F32)
    bin_ = f32(ffn_in_bias).reshape(1, -1)
    *near_self, near_key, near_value, memory_far, out_grad_far, near_mix, near_stats = project_near(
        order, spots, tgt_segment, hidden_in, memory, out_grad, vec, [self_query, self_key, self_value, cross_key, cross_value])
    memory_far, hidden_got, segs = lax.optimization_barrier((memory_far, hidden_got, segs))
    memory_got = swap(memory_far, "seq", 1, 2)
    (self_totals, n1, r1, first_low, cross_queries, self_oh, self_mk, cross_mk,
     hidden, queries, key_rows, value_rows, self_mixed) = self_forward(
        order, spots, vec, segs, near_mix, near_stats, hidden_in, hidden_got, near_self,
        [self_query, self_key, self_value, self_output, cross_query])
    out_grad_far, memory_got, r1 = lax.optimization_barrier((out_grad_far, memory_got, r1))
    out_grad_got = swap(out_grad_far, "seq", 1, 2)
    cross_totals, source, memory_keys, memory_values, cross_mixed = cross_forward(
        order, spots, vec, self_oh, cross_mk, cross_queries, memory, memory_got, [near_key, near_value], [cross_key, cross_value])
    ho, ho_far, second_back, cross_mixed_back, v_ffn, v_in, ffn_all = ffn_both(
        order, spots, vec, bin_, n1, cross_mixed, out_grad, out_grad_got, [cross_output, ffn_in, ffn_out])
    ho_got = swap(ho_far, "seq", 1, 2)
    ffn_sum = lax.psum_scatter(ffn_all.reshape(16, 432, -1), "dp", scatter_dimension=0, tiled=False)
    cross_query_back, memory_key_back, memory_value_back, mg, mg_far = cross_back(
        order, spots, cross_queries, memory_keys, memory_values, cross_mixed_back, cross_mixed, cross_totals, self_oh, cross_mk,
        [cross_key, cross_value])
    mg_far, ho_got = lax.optimization_barrier((mg_far, ho_got))
    mg_got = swap(mg_far, "seq", 1, 2)
    first_back, self_mixed_back, v_first, *pairs = middle(
        order, spots, vec, cross_query_back, memory_key_back, memory_value_back, n1, r1, second_back, first_low, source,
        self_mixed, [cross_query, self_output])
    cross_sum = Sum(*first_swap(*pairs, mg_got), *CROSS_LINKS)
    advance(order, spots, cross_sum)
    query_back, key_back, value_back, send, keep, hidden_out, memory_grad = self_back(
        order, spots, queries, key_rows, value_rows, self_mixed_back, self_mixed, self_totals, self_oh, self_mk,
        [v_ffn, v_first, v_in], hidden, [(ho, ho_got), (mg, mg_got)])
    self_sum = Sum(*first_swap(send, keep, cross_sum.gots[0][0]), *SELF_LINKS)
    advance(order, spots, cross_sum, self_sum)
    hg, hg_far = back_rows(
        order, spots, [[query_back], [key_back], [value_back]], [self_query, self_key, self_value], first_back, [])
    ffn_sum, hg = lax.optimization_barrier((ffn_sum, hg))
    ffn_got = swap(ffn_sum, "seq", 1, 2)
    hg_got = swap(hg_far, "seq", 1, 2)
    advance(order, spots, cross_sum, self_sum)
    advance(order, spots, cross_sum, self_sum)
    order.last += [ffn_got, hg_got]
    advance(order, spots, cross_sum, self_sum)
    hidden_grad = two(s, hg[None], hg_got[None])
    (g_sq, g_sk, g_sv, g_so, g_cq, g_ck, g_cv, g_co, g_fi, g_fo, *v, v_fi) = finish(
        order, spots, ffn_sum, ffn_got, cross_sum, self_sum)
    (g3, b3, fob, g2, b2, cob, g1, b1, ob, cqb, cvb, qb, vb) = [a.reshape(-1) for a in v]
    return (
        hidden_out, hidden_grad, memory_grad,
        g_sq, qb, g_sk, g_sv, vb, g_so, ob, g1, b1, g_cq, cqb, g_ck, g_cv, cvb, g_co, cob, g2, b2,
        g_fi, v_fi.reshape(-1), g_fo, fob, g3, b3,
    )


def solution(mesh):
    in_specs = (
        P("dp", "seq", None),
        P("dp", "seq", None),
        P("dp", "seq"),
        P("dp", "seq"),
        P("dp", "seq", None),
        P(),
        P(),
        P(),
        P(),
        P(),
        P(),
        P(),
        P(),
        P(),
        P(),
        P(),
        P(),
        P(),
        P(),
        P(),
        P(),
        P(),
        P(),
        P(),
        P(),
        P(),
        P(),
        P(),
        P(),
    )
    out_specs = (
        P("dp", "seq", None),
        P("dp", "seq", None),
        P("dp", "seq", None),
        P("dp", None),
        P("dp"),
        P("dp", None),
        P("dp", None),
        P("dp"),
        P("dp", None),
        P("dp"),
        P("dp"),
        P("dp"),
        P("dp", None),
        P("dp"),
        P("dp", None),
        P("dp", None),
        P("dp"),
        P("dp", None),
        P("dp"),
        P("dp"),
        P("dp"),
        P("dp", None),
        P("dp"),
        P("dp", None),
        P("dp"),
        P("dp"),
        P("dp"),
    )
    rows_form = mesh.shape["seq"] == 2 and mesh.shape["dp"] == 16

    def on_device(*arrays):
        if rows_form and arrays[0].shape[0] == 2:
            return whole_rows(*arrays)
        return split_rows(*arrays)

    return jax.shard_map(
        on_device, mesh=mesh, in_specs=in_specs, out_specs=out_specs, check_vma=False
    )
```

```python
import functools
import math

import jax
import jax.numpy as jnp
from jax import lax
from jax.experimental import pallas as pl
from jax.experimental.pallas import tpu as pltpu
from jax.sharding import PartitionSpec as P

HEADS = 12
BF=jnp.bfloat16; F32=jnp.float32
BIG=-1e30
def dot(a,b): return jnp.dot(a,b,preferred_element_type=F32)

def lane_low(shape): return lax.broadcasted_iota(jnp.int32, shape, 1) < 64

def prepare(q,k,v,oh,mk):
    low=lane_low(k.shape)
    qT=(q*BF(0.125)).T
    vT=v.T
    ones=jnp.ones((16,k.shape[0]),BF)
    kas=[jnp.where(low,k,mk),jnp.where(low,mk,k)]
    vas=[jnp.concatenate([vT[64*h:64*h+64],ones],0) for h in (0,1)]
    qas=[jnp.concatenate([qT[:64],oh],0),jnp.concatenate([oh,qT[64:]],0)]
    return kas,vas,qas

def causal_block(n):
    return lax.broadcasted_iota(jnp.int32,(n,n),0)<=lax.broadcasted_iota(jnp.int32,(n,n),1)

def attend_near(q,k,v,oh,mk):
    kas,vas,qas=prepare(q,k,v,oh,mk)
    dm=causal_block(q.shape[0])
    ss=[jnp.where(dm,dot(kas[h],qas[h]),BIG) for h in (0,1)]
    out=[]
    for h in (0,1):
        m=jnp.max(ss[h],axis=0,keepdims=True)
        o=dot(vas[h],jnp.exp(ss[h]-m).astype(BF))
        out.append((o[:64],m,o[64:65]))
    return out

def attend_rest(first,near,far_args,off_args):
    far=prepare(*far_args); off=prepare(*off_args)
    dm=causal_block(far_args[0].shape[0])
    fs=[jnp.where(dm,dot(far[0][h],far[2][h]),BIG) for h in (0,1)]
    os=[]; result=[]
    for h in (0,1):
        os.append(dot(off[0][h],off[2][h]))
        m=jnp.max(fs[h],axis=0,keepdims=True)
        p=jnp.exp(fs[h]-m).astype(BF)
        o=dot(far[1][h],p)
        here=(o[:64],m,o[64:65])
        result.append(([jnp.where(first,a,b) for a,b in zip(near[h],here)],[jnp.where(first,b,a) for a,b in zip(near[h],here)]))
    out=[]
    for h in (0,1):
        (o0,m0,l0),(o1,m1,l1)=result[h]
        m=jnp.maximum(m1,jnp.max(os[h],axis=0,keepdims=True))
        p=jnp.exp(os[h]-m).astype(BF)
        w=jnp.exp(m1-m)
        o=dot(off[1][h],p)
        l=o[64:65]+w*l1
        out.append(((o0/l0,m0+jnp.log(l0)),((o[:64]+w*o1)/l,m+jnp.log(l))))
    return out

def attend_pair(q,k,v,oh,mk,put_total,bq):
    T=q.shape[0]
    kas,vas,qas=prepare(q,k,v,oh,mk)
    def scores(i,h):
        return dot(kas[h],qas[h][:,i*bq:(i+1)*bq])
    def weigh(s):
        m=jnp.max(s,axis=0,keepdims=True)
        return m,jnp.exp(s-m).astype(BF)
    def mix(i,h,m,p):
        o=dot(vas[h],p)
        l=o[64:65]
        put_total(h,i,m+jnp.log(l))
        return o[:64]/l
    units=[(i,h) for i in range(T//bq) for h in (0,1)]
    os=[]
    s=scores(*units[0]); late=None
    for n,u in enumerate(units):
        coming=scores(*units[n+1]) if n+1<len(units) else None
        m,p=weigh(s)
        if late is not None: os.append(mix(*late))
        late=(*u,m,p)
        s=coming
    os.append(mix(*late))
    return [jnp.concatenate(os[2*i:2*i+2],0).T.astype(BF) for i in range(T//bq)]

def split3(x):
    a=x.astype(BF); r=x-a.astype(F32); b=r.astype(BF); c=(r-b.astype(F32)).astype(BF)
    return a,b,c

def attend_pair_back(q,k,v,do,o,totals,oh,mk,acc_ref,put,bk,causal):
    T=q.shape[0]; K=k.shape[0]
    low=lane_low((K,128))
    q=q*BF(0.125)
    qT=q.T; doT=do.T
    kT=k.T
    prodT=(do.astype(F32)*o.astype(F32)).T
    rowi=lax.broadcasted_iota(jnp.int32,(64,T),0)
    one=jnp.full((K,128),-1.0,BF)
    if causal:
        dm=lax.broadcasted_iota(jnp.int32,(bk,bk),0)<=lax.broadcasted_iota(jnp.int32,(bk,bk),1)
    qas=[];das=[]
    for h in (0,1):
        a,b,c=split3(totals[h])
        ohl=jnp.where(rowi==4,a,jnp.where(rowi==5,b,jnp.where(rowi==6,c,oh)))
        D=jnp.sum(prodT[64*h:64*h+64],axis=0,keepdims=True)
        a,b,c=split3(D)
        z=jnp.zeros((64,T),BF)
        dd=jnp.where(rowi==0,a,jnp.where(rowi==1,b,jnp.where(rowi==2,c,z)))
        if h==0:
            qas.append(jnp.concatenate([qT[:64],ohl],0)); das.append(jnp.concatenate([doT[:64],dd],0))
        else:
            qas.append(jnp.concatenate([ohl,qT[64:]],0)); das.append(jnp.concatenate([dd,doT[64:]],0))
    kas=[jnp.where(low,k,mk),jnp.where(low,mk,k)]
    vas=[jnp.where(low,v,one),jnp.where(low,one,v)]
    def ahead(j,h):
        q0=j*bk if causal else 0
        ks=slice(j*bk,(j+1)*bk)
        return dot(kas[h][ks],qas[h][:,q0:]),dot(vas[h][ks],das[h][:,q0:])
    def weigh(j,s,dp):
        q0=j*bk if causal else 0
        if causal:
            sd=jnp.where(dm,s[:,:bk],BIG)
            s=jnp.concatenate([sd,s[:,bk:]],1) if q0+bk<T else sd
        p=jnp.exp(s)
        return p.astype(BF),(p*dp).astype(BF)
    done={}
    def behind(j,h,p,ds):
        q0=j*bk if causal else 0
        ks=slice(j*bk,(j+1)*bk)
        done[h]=dot(ds,q[q0:]),dot(p,do[q0:])
        dqt=dot(kT[64*h:64*h+64,ks],ds)
        if j==0: acc_ref[64*h:64*h+64,:]=dqt
        else: acc_ref[64*h:64*h+64,q0:]+=dqt
        if h:
            lw=low[:bk]
            put("k",ks,jnp.where(lw,done[0][0],done[1][0]).astype(BF))
            put("v",ks,jnp.where(lw,done[0][1],done[1][1]).astype(BF))
    units=[(j,h) for j in range(K//bk) for h in (0,1)]
    now=ahead(*units[0]); late=None
    for n,u in enumerate(units):
        coming=ahead(*units[n+1]) if n+1<len(units) else None
        pd=weigh(u[0],*now)
        if late is not None: behind(*late)
        late=(*u,*pd)
        now=coming
    behind(*late)
    put("q",slice(0,T),(acc_ref[...]*0.125).T.astype(BF))


def project(values, weight):
    return jnp.dot(values, weight, preferred_element_type=jnp.float32)


def project_back(gradient, weight):
    return jnp.einsum("rte,de->rtd", gradient, weight, preferred_element_type=jnp.float32)


def weight_grad(values, gradient):
    return jnp.einsum("rtd,rte->de", values, gradient, preferred_element_type=jnp.float32)


def token_sum(gradient):
    return jnp.sum(gradient.astype(jnp.float32), axis=(0, 1))


def layer_norm(values, norm_gain, norm_shift):
    center = values - jnp.mean(values, axis=-1, keepdims=True)
    spread = jnp.mean(center * center, axis=-1, keepdims=True)
    return center * lax.rsqrt(spread + 1e-05) * norm_gain + norm_shift


def exact_gelu(values):
    return jax.nn.gelu(values, approximate=False)


def split_heads(values):
    return values.reshape(values.shape[0], values.shape[1], HEADS, values.shape[2] // HEADS)


def merge_heads(values):
    return values.reshape(values.shape[0], values.shape[1], values.shape[2] * values.shape[3])


def masked_scores(queries, key_rows, allowed):
    raw_scores = jnp.einsum(
        "rqhd,rkhd->rhqk",
        split_heads(queries),
        split_heads(key_rows),
        preferred_element_type=jnp.float32,
    )
    factor = 1.0 / math.sqrt(queries.shape[2] // HEADS)
    return jnp.where(allowed[:, None], raw_scores * factor, -1e30)


def attend_forward(queries, key_rows, value_rows, allowed):
    scores = masked_scores(queries, key_rows, allowed)
    highest = jnp.max(scores, axis=-1, keepdims=True)
    powers = jnp.exp(scores - highest)
    totals = jnp.sum(powers, axis=-1, keepdims=True)
    weights = (powers / totals).astype(jnp.bfloat16)
    mixed_heads = jnp.einsum(
        "rhqk,rkhd->rqhd", weights, split_heads(value_rows), preferred_element_type=jnp.float32
    )
    return (merge_heads(mixed_heads).astype(jnp.bfloat16), highest + jnp.log(totals))


def attend_backward(queries, key_rows, value_rows, allowed, log_totals, mixed_grad):
    scores = masked_scores(queries, key_rows, allowed)
    weights = jnp.exp(scores - log_totals)
    grad_heads = split_heads(mixed_grad)
    value_terms = jnp.einsum(
        "rhqk,rqhd->rkhd",
        weights.astype(jnp.bfloat16),
        grad_heads,
        preferred_element_type=jnp.float32,
    )
    weight_grads = jnp.einsum(
        "rqhd,rkhd->rhqk", grad_heads, split_heads(value_rows), preferred_element_type=jnp.float32
    )
    inner_sum = jnp.sum(weights * weight_grads, axis=-1, keepdims=True)
    factor = 1.0 / math.sqrt(queries.shape[2] // HEADS)
    score_grads = (weights * (weight_grads - inner_sum) * factor).astype(jnp.bfloat16)
    query_grads = jnp.einsum(
        "rhqk,rkhd->rqhd", score_grads, split_heads(key_rows), preferred_element_type=jnp.float32
    )
    key_terms = jnp.einsum(
        "rhqk,rqhd->rkhd", score_grads, split_heads(queries), preferred_element_type=jnp.float32
    )
    return (merge_heads(query_grads), merge_heads(key_terms), merge_heads(value_terms))


def split_rows(
    hidden_in,
    memory,
    tgt_segment,
    src_segment,
    out_grad,
    self_query,
    query_bias,
    self_key,
    self_value,
    value_bias,
    self_output,
    output_bias,
    first_gain,
    first_shift,
    cross_query,
    cross_query_bias,
    cross_key,
    cross_value,
    cross_value_bias,
    cross_output,
    cross_output_bias,
    second_gain,
    second_shift,
    ffn_in,
    ffn_in_bias,
    ffn_out,
    ffn_out_bias,
    third_gain,
    third_shift,
):
    tokens = hidden_in.shape[1]
    queries = (project(hidden_in, self_query) + query_bias.astype(jnp.float32)).astype(jnp.bfloat16)
    key_rows = project(hidden_in, self_key).astype(jnp.bfloat16)
    value_rows = (project(hidden_in, self_value) + value_bias.astype(jnp.float32)).astype(
        jnp.bfloat16
    )
    target_ids = tgt_segment.astype(jnp.bfloat16)
    all_keys, all_values, all_target = (
        lax.all_gather(key_rows, "seq", axis=1, tiled=True),
        lax.all_gather(value_rows, "seq", axis=1, tiled=True),
        lax.all_gather(target_ids, "seq", axis=1, tiled=True),
    )
    memory_keys = project(memory, cross_key).astype(jnp.bfloat16)
    memory_values = (project(memory, cross_value) + cross_value_bias.astype(jnp.float32)).astype(
        jnp.bfloat16
    )
    all_memkeys, all_memvalues, all_source = (
        lax.all_gather(memory_keys, "seq", axis=1, tiled=True),
        lax.all_gather(memory_values, "seq", axis=1, tiled=True),
        lax.all_gather(src_segment.astype(jnp.bfloat16), "seq", axis=1, tiled=True),
    )
    offset = lax.axis_index("seq") * tokens
    query_places = offset + jnp.arange(tokens, dtype=jnp.int32)
    key_places = jnp.arange(all_keys.shape[1], dtype=jnp.int32)
    self_allowed = (target_ids[:, :, None] == all_target[:, None, :]) & (
        query_places[:, None] >= key_places[None, :]
    )[None]
    cross_allowed = target_ids[:, :, None] == all_source[:, None, :]
    self_mixed, self_totals = attend_forward(queries, all_keys, all_values, self_allowed)
    self_branch = project(self_mixed, self_output) + output_bias.astype(jnp.float32)
    first_norm, first_pull = jax.vjp(
        layer_norm,
        hidden_in.astype(jnp.float32) + self_branch,
        first_gain.astype(jnp.float32),
        first_shift.astype(jnp.float32),
    )
    first_low = first_norm.astype(jnp.bfloat16)
    cross_queries = (project(first_low, cross_query) + cross_query_bias.astype(jnp.float32)).astype(
        jnp.bfloat16
    )
    cross_mixed, cross_totals = attend_forward(
        cross_queries, all_memkeys, all_memvalues, cross_allowed
    )
    cross_branch = project(cross_mixed, cross_output) + cross_output_bias.astype(jnp.float32)
    second_norm, second_pull = jax.vjp(
        layer_norm,
        first_norm + cross_branch,
        second_gain.astype(jnp.float32),
        second_shift.astype(jnp.float32),
    )
    second_low = second_norm.astype(jnp.bfloat16)
    inner_rows = project(second_low, ffn_in) + ffn_in_bias.astype(jnp.float32)
    activation_full, gelu_pull = jax.vjp(exact_gelu, inner_rows)
    activation = activation_full.astype(jnp.bfloat16)
    ffn_branch = project(activation, ffn_out) + ffn_out_bias.astype(jnp.float32)
    final_norm, third_pull = jax.vjp(
        layer_norm,
        second_norm + ffn_branch,
        third_gain.astype(jnp.float32),
        third_shift.astype(jnp.float32),
    )
    hidden_out = final_norm.astype(jnp.bfloat16)
    third_back, grad_third_gain, grad_third_shift = third_pull(out_grad.astype(jnp.float32))
    ffn_back = third_back.astype(jnp.bfloat16)
    grad_ffn_out = weight_grad(activation, ffn_back)
    grad_ffn_out_bias = token_sum(ffn_back)
    activation_back = project_back(ffn_back, ffn_out)
    inner_back = gelu_pull(activation_back)[0].astype(jnp.bfloat16)
    grad_ffn_in = weight_grad(second_low, inner_back)
    grad_ffn_in_bias = token_sum(inner_back)
    second_back, grad_second_gain, grad_second_shift = second_pull(
        third_back + project_back(inner_back, ffn_in)
    )
    cross_back = second_back.astype(jnp.bfloat16)
    grad_cross_output = weight_grad(cross_mixed, cross_back)
    grad_cross_output_bias = token_sum(cross_back)
    cross_mixed_back = project_back(cross_back, cross_output).astype(jnp.bfloat16)
    cross_query_grad, memkey_terms, memvalue_terms = attend_backward(
        cross_queries, all_memkeys, all_memvalues, cross_allowed, cross_totals, cross_mixed_back
    )
    memkey_sum, memvalue_sum = (
        lax.psum_scatter(
            memkey_terms.astype(jnp.bfloat16), "seq", scatter_dimension=1, tiled=True
        ).astype(jnp.float32),
        lax.psum_scatter(
            memvalue_terms.astype(jnp.bfloat16), "seq", scatter_dimension=1, tiled=True
        ).astype(jnp.float32),
    )
    memory_key_back = memkey_sum.astype(jnp.bfloat16)
    memory_value_back = memvalue_sum.astype(jnp.bfloat16)
    cross_query_back = cross_query_grad.astype(jnp.bfloat16)
    grad_cross_query = weight_grad(first_low, cross_query_back)
    grad_cross_query_bias = token_sum(cross_query_back)
    grad_cross_key = weight_grad(memory, memory_key_back)
    grad_cross_value = weight_grad(memory, memory_value_back)
    grad_cross_value_bias = token_sum(memory_value_back)
    memory_grad = (
        project_back(memory_key_back, cross_key) + project_back(memory_value_back, cross_value)
    ).astype(jnp.bfloat16)
    first_back, grad_first_gain, grad_first_shift = first_pull(
        second_back + project_back(cross_query_back, cross_query)
    )
    self_back = first_back.astype(jnp.bfloat16)
    grad_self_output = weight_grad(self_mixed, self_back)
    grad_output_bias = token_sum(self_back)
    self_mixed_back = project_back(self_back, self_output).astype(jnp.bfloat16)
    query_grad, key_terms, value_terms = attend_backward(
        queries, all_keys, all_values, self_allowed, self_totals, self_mixed_back
    )
    key_sum, value_sum = (
        lax.psum_scatter(
            key_terms.astype(jnp.bfloat16), "seq", scatter_dimension=1, tiled=True
        ).astype(jnp.float32),
        lax.psum_scatter(
            value_terms.astype(jnp.bfloat16), "seq", scatter_dimension=1, tiled=True
        ).astype(jnp.float32),
    )
    key_back = key_sum.astype(jnp.bfloat16)
    value_back = value_sum.astype(jnp.bfloat16)
    query_back = query_grad.astype(jnp.bfloat16)
    grad_self_query = weight_grad(hidden_in, query_back)
    grad_query_bias = token_sum(query_back)
    grad_self_key = weight_grad(hidden_in, key_back)
    grad_self_value = weight_grad(hidden_in, value_back)
    grad_value_bias = token_sum(value_back)
    hidden_grad = (
        first_back
        + project_back(query_back, self_query)
        + project_back(key_back, self_key)
        + project_back(value_back, self_value)
    ).astype(jnp.bfloat16)
    partial_grads = [
        grad_self_query,
        grad_query_bias,
        grad_self_key,
        grad_self_value,
        grad_value_bias,
        grad_self_output,
        grad_output_bias,
        grad_first_gain,
        grad_first_shift,
        grad_cross_query,
        grad_cross_query_bias,
        grad_cross_key,
        grad_cross_value,
        grad_cross_value_bias,
        grad_cross_output,
        grad_cross_output_bias,
        grad_second_gain,
        grad_second_shift,
        grad_ffn_in,
        grad_ffn_in_bias,
        grad_ffn_out,
        grad_ffn_out_bias,
        grad_third_gain,
        grad_third_shift,
    ]
    summed = (
        lax.psum_scatter(
            partial_grads[0].astype(jnp.bfloat16), "dp", scatter_dimension=0, tiled=True
        ).astype(jnp.float32),
        lax.psum_scatter(
            partial_grads[1].astype(jnp.bfloat16), "dp", scatter_dimension=0, tiled=True
        ).astype(jnp.float32),
        lax.psum_scatter(
            partial_grads[2].astype(jnp.bfloat16), "dp", scatter_dimension=0, tiled=True
        ).astype(jnp.float32),
        lax.psum_scatter(
            partial_grads[3].astype(jnp.bfloat16), "dp", scatter_dimension=0, tiled=True
        ).astype(jnp.float32),
        lax.psum_scatter(
            partial_grads[4].astype(jnp.bfloat16), "dp", scatter_dimension=0, tiled=True
        ).astype(jnp.float32),
        lax.psum_scatter(
            partial_grads[5].astype(jnp.bfloat16), "dp", scatter_dimension=0, tiled=True
        ).astype(jnp.float32),
        lax.psum_scatter(
            partial_grads[6].astype(jnp.bfloat16), "dp", scatter_dimension=0, tiled=True
        ).astype(jnp.float32),
        lax.psum_scatter(
            partial_grads[7].astype(jnp.bfloat16), "dp", scatter_dimension=0, tiled=True
        ).astype(jnp.float32),
        lax.psum_scatter(
            partial_grads[8].astype(jnp.bfloat16), "dp", scatter_dimension=0, tiled=True
        ).astype(jnp.float32),
        lax.psum_scatter(
            partial_grads[9].astype(jnp.bfloat16), "dp", scatter_dimension=0, tiled=True
        ).astype(jnp.float32),
        lax.psum_scatter(
            partial_grads[10].astype(jnp.bfloat16), "dp", scatter_dimension=0, tiled=True
        ).astype(jnp.float32),
        lax.psum_scatter(
            partial_grads[11].astype(jnp.bfloat16), "dp", scatter_dimension=0, tiled=True
        ).astype(jnp.float32),
        lax.psum_scatter(
            partial_grads[12].astype(jnp.bfloat16), "dp", scatter_dimension=0, tiled=True
        ).astype(jnp.float32),
        lax.psum_scatter(
            partial_grads[13].astype(jnp.bfloat16), "dp", scatter_dimension=0, tiled=True
        ).astype(jnp.float32),
        lax.psum_scatter(
            partial_grads[14].astype(jnp.bfloat16), "dp", scatter_dimension=0, tiled=True
        ).astype(jnp.float32),
        lax.psum_scatter(
            partial_grads[15].astype(jnp.bfloat16), "dp", scatter_dimension=0, tiled=True
        ).astype(jnp.float32),
        lax.psum_scatter(
            partial_grads[16].astype(jnp.bfloat16), "dp", scatter_dimension=0, tiled=True
        ).astype(jnp.float32),
        lax.psum_scatter(
            partial_grads[17].astype(jnp.bfloat16), "dp", scatter_dimension=0, tiled=True
        ).astype(jnp.float32),
        lax.psum_scatter(
            partial_grads[18].astype(jnp.bfloat16), "dp", scatter_dimension=0, tiled=True
        ).astype(jnp.float32),
        lax.psum_scatter(
            partial_grads[19].astype(jnp.bfloat16), "dp", scatter_dimension=0, tiled=True
        ).astype(jnp.float32),
        lax.psum_scatter(
            partial_grads[20].astype(jnp.bfloat16), "dp", scatter_dimension=0, tiled=True
        ).astype(jnp.float32),
        lax.psum_scatter(
            partial_grads[21].astype(jnp.bfloat16), "dp", scatter_dimension=0, tiled=True
        ).astype(jnp.float32),
        lax.psum_scatter(
            partial_grads[22].astype(jnp.bfloat16), "dp", scatter_dimension=0, tiled=True
        ).astype(jnp.float32),
        lax.psum_scatter(
            partial_grads[23].astype(jnp.bfloat16), "dp", scatter_dimension=0, tiled=True
        ).astype(jnp.float32),
    )
    finished = (
        lax.psum(summed[0].astype(jnp.bfloat16), "seq").astype(jnp.float32),
        lax.psum(summed[1].astype(jnp.bfloat16), "seq").astype(jnp.float32),
        lax.psum(summed[2].astype(jnp.bfloat16), "seq").astype(jnp.float32),
        lax.psum(summed[3].astype(jnp.bfloat16), "seq").astype(jnp.float32),
        lax.psum(summed[4].astype(jnp.bfloat16), "seq").astype(jnp.float32),
        lax.psum(summed[5].astype(jnp.bfloat16), "seq").astype(jnp.float32),
        lax.psum(summed[6].astype(jnp.bfloat16), "seq").astype(jnp.float32),
        lax.psum(summed[7].astype(jnp.bfloat16), "seq").astype(jnp.float32),
        lax.psum(summed[8].astype(jnp.bfloat16), "seq").astype(jnp.float32),
        lax.psum(summed[9].astype(jnp.bfloat16), "seq").astype(jnp.float32),
        lax.psum(summed[10].astype(jnp.bfloat16), "seq").astype(jnp.float32),
        lax.psum(summed[11].astype(jnp.bfloat16), "seq").astype(jnp.float32),
        lax.psum(summed[12].astype(jnp.bfloat16), "seq").astype(jnp.float32),
        lax.psum(summed[13].astype(jnp.bfloat16), "seq").astype(jnp.float32),
        lax.psum(summed[14].astype(jnp.bfloat16), "seq").astype(jnp.float32),
        lax.psum(summed[15].astype(jnp.bfloat16), "seq").astype(jnp.float32),
        lax.psum(summed[16].astype(jnp.bfloat16), "seq").astype(jnp.float32),
        lax.psum(summed[17].astype(jnp.bfloat16), "seq").astype(jnp.float32),
        lax.psum(summed[18].astype(jnp.bfloat16), "seq").astype(jnp.float32),
        lax.psum(summed[19].astype(jnp.bfloat16), "seq").astype(jnp.float32),
        lax.psum(summed[20].astype(jnp.bfloat16), "seq").astype(jnp.float32),
        lax.psum(summed[21].astype(jnp.bfloat16), "seq").astype(jnp.float32),
        lax.psum(summed[22].astype(jnp.bfloat16), "seq").astype(jnp.float32),
        lax.psum(summed[23].astype(jnp.bfloat16), "seq").astype(jnp.float32),
    )
    finished = list(finished)
    return (hidden_out, hidden_grad, memory_grad) + tuple(finished)


def nt(a, b):
    return lax.dot_general(a, b, (((1,), (1,)), ((), ())), preferred_element_type=F32)


def tn(a, b):
    return lax.dot_general(a, b, (((0,), (0,)), ((), ())), preferred_element_type=F32)


def mean(v):
    return jnp.mean(v, axis=-1, keepdims=True)


def norm_stats(v):
    center = v - mean(v)
    r = lax.rsqrt(mean(center * center) + 1e-05)
    return center * r, r


def norm_back(e, n, r, gain):
    u = e * gain
    return r * (u - mean(u) - n * mean(u * n))


def sums(v):
    return jnp.sum(v, axis=0, keepdims=True)


TAIL = (0.24251982196758853, 0.24429374300098905, 0.2054730204591465, 0.24507896666845616,
        -0.08230106829392796, 0.3798837300580386, -0.30809352249830146, 0.07314529579847638)


def gelu_pair(x):
    d = 1.0 + (0.43 * math.sqrt(0.5)) * jnp.abs(x)
    t = pl.reciprocal(d, approx=True)
    t = t * (2.0 - d * t)
    tail = 0.5 * TAIL[-1]
    for c in TAIL[-2::-1]:
        tail = tail * t + 0.5 * c
    bell = jnp.exp(-0.5 * x * x)
    tail = tail * t * bell
    phi = jnp.where(x >= 0, 1.0 - tail, tail)
    return x * phi, phi + x * bell * (1.0 / math.sqrt(2.0 * math.pi))


def full(shape):
    return pl.BlockSpec(shape, lambda *_: (0,) * len(shape), pipeline_mode=pl.Buffered(1))


def still(shape):
    return pl.BlockSpec(shape, lambda *_: (0,) * len(shape))


def rows_of(bt, width):
    return pl.BlockSpec((bt, width), lambda i: (i, 0))


class Order:
    def __init__(self):
        self.last = []

    def call(self, kernel, *args, name, us, grid, in_specs, out_specs, out_shape, scalars=0, scratch_shapes=(), moves=()):
        at, after, n, n_out = len(args), len(self.last), len(moves), len(out_specs)
        flat = [array for pair in moves for array in pair]
        hbm = pl.BlockSpec(memory_space=pl.ANY)

        def run(*refs):
            outs = at + 2 * n + after
            plain = refs[:at] + refs[outs : outs + n_out]
            if not n:
                return kernel(*plain, *refs[outs + n_out :])
            s = refs[0][4]
            buffer, sem = refs[-2:]
            reads, writes = [], []
            for i in range(n):
                target = refs[outs + n_out + i]
                for j, place in enumerate((s, 1 - s)):
                    slot = 2 * i + j
                    reads.append(pltpu.make_async_copy(refs[at + slot], buffer.at[slot], sem.at[0, slot]))
                    writes.append(pltpu.make_async_copy(buffer.at[slot], target.at[place], sem.at[1, slot]))

            @pl.when(pl.program_id(0) == 0)
            def _():
                for c in reads:
                    c.start()

            @pl.when(pl.program_id(0) == 1)
            def _():
                for r, w in zip(reads, writes):
                    r.wait()
                    w.start()

            kernel(*plain, *refs[outs + n_out + n : -2])

            @pl.when(pl.program_id(0) == grid[0] - 1)
            def _():
                for c in writes:
                    c.wait()

        more = [pltpu.VMEM((2 * n, *flat[0].shape), BF), pltpu.SemaphoreType.DMA((2, 2 * n))] if n else []
        out = pl.pallas_call(
            run, name=name, out_shape=list(out_shape) + [shaped(2, *pair[0].shape) for pair in moves],
            grid_spec=pltpu.PrefetchScalarGridSpec(
                num_scalar_prefetch=scalars, grid=grid, in_specs=list(in_specs) + [hbm] * (2 * n + after),
                out_specs=list(out_specs) + [hbm] * n, scratch_shapes=list(scratch_shapes) + more),
            cost_estimate=pl.CostEstimate(flops=0, bytes_accessed=int(us * 7.2e6), transcendentals=0),
            compiler_params=pltpu.CompilerParams(vmem_limit_bytes=127 * 2**19),
        )(*args, *flat, *self.last)
        self.last = [out[n_out - 1]]
        return out


def shaped(*shape, dtype=BF):
    return jax.ShapeDtypeStruct(shape, dtype)


(V_QB, V_VB, V_OB, V_G1, V_B1, V_CQB, V_CVB, V_COB, V_G2, V_B2, V_FOB, V_G3, V_B3) = range(13)


def mask_of(ids, ref):
    row = lax.broadcasted_iota(jnp.int32, (128, ids.shape[1]), 0) % 64
    ref[...] = jnp.where(row < 4, jnp.where(row == ids, 0.0, BIG), jnp.where(row < 7, -1.0, 0.0)).T.astype(BF)


def one_hot(ids, ref):
    row = lax.broadcasted_iota(jnp.int32, (64, ids.shape[1]), 0)
    ref[...] = jnp.where(row == ids, 1.0, 0.0).astype(BF)


def near_kernel(spot_ref, seg_ref, x_ref, y_ref, far_ref, grad_ref, vec_ref, wq_ref, wk_ref, wv_ref, uk_ref, uv_ref,
                q_ref, k_ref, v_ref, mk_ref, mv_ref, far_out, grad_out, mix_ref, stat_ref, q_s, k_s, v_s, oh_s, mask_s):
    at = pl.program_id(0)

    @pl.when(at == 0)
    def _():
        far_out[...] = far_ref[0]
        grad_out[...] = grad_ref[0]
        ids = seg_ref[pl.ds(spot_ref[4], 1), :]
        one_hot(ids, oh_s)
        mask_of(ids, mask_s)
        x, y = x_ref[0], y_ref[0]
        q_s[...] = (dot(x, wq_ref[...]) + vec_ref[V_QB : V_QB + 1, :]).astype(BF)
        k_s[...] = dot(x, wk_ref[...]).astype(BF)
        v_s[...] = (dot(x, wv_ref[...]) + vec_ref[V_VB : V_VB + 1, :]).astype(BF)
        mk_ref[...] = dot(y, uk_ref[...]).astype(BF)
        mv_ref[...] = (dot(y, uv_ref[...]) + vec_ref[V_CVB : V_CVB + 1, :]).astype(BF)
        q_ref[...], k_ref[...], v_ref[...] = q_s[...], k_s[...], v_s[...]

    @pl.when(at > 0)
    def _():
        cols = columns(at - 1)
        for h, (o, m, l) in enumerate(attend_near(q_s[:, cols], k_s[:, cols], v_s[:, cols], oh_s[...], mask_s[...])):
            mix_ref[64 * h : 64 * h + 64, :] = o
            stat_ref[0, h : h + 1, :] = m
            stat_ref[0, 2 + h : 3 + h, :] = l


def project_near(order, spots, tgt, hidden_in, memory, out_grad, vec, weights):
    half, D = hidden_in.shape[1:]
    pairs = D // 128
    x = pl.BlockSpec((1, half, D), lambda i, p: (p[4], 0, 0))
    other = pl.BlockSpec((1, half, D), lambda i, p: (1 - p[4], 0, 0))
    pair = lambda i: jnp.maximum(i - 1, 0)
    big = pltpu.VMEM((half, D), BF)
    return order.call(
        near_kernel, spots, tgt, hidden_in, memory, memory, out_grad, vec, *weights, scalars=1, name="project_near", us=14,
        grid=(1 + pairs,), in_specs=[full(tgt.shape), x, x, other, other, full(vec.shape)] + [full((D, D))] * 5,
        out_specs=[still((half, D))] * 7 + [pl.BlockSpec((128, half), lambda i, p: (pair(i), 0)),
                                            pl.BlockSpec((1, 8, half), lambda i, p: (pair(i), 0, 0))],
        out_shape=[shaped(half, D)] * 7 + [shaped(D, half, dtype=F32), shaped(pairs, 8, half, dtype=F32)],
        scratch_shapes=[big] * 3 + [pltpu.VMEM((64, half), BF), pltpu.VMEM((half, 128), BF)])


class Loads:
    def __init__(self, sem):
        self.sem = sem
        self.copies = []

    def add(self, src, dst):
        self.copies.append(pltpu.make_async_copy(src, dst, self.sem.at[len(self.copies)]))
        return self.copies[-1]


def columns(p, width=128):
    return pl.ds(pl.multiple_of(p * width, width), width)


def self_kernel(spot_ref, vec_ref, seg_ref, mix_ref, stat_ref, hin_ref, hgot_ref, qn_ref, kn_ref, vn_ref, wq_ref, wk_ref, wv_ref, wo_ref, wc_ref,
                l_ref, n_ref, r_ref, low_ref, cq_ref, oh_ref, mk_ref, cross_mk_ref, h_out, q_out, k_out, v_out, m_out,
                h_s, q_s, k_s, v_s, m_s, wq_s, wk_s, wv_s, wo_s, wc_s, sem, *, pairs):
    v = lambda i: vec_ref[i : i + 1, :]
    at = pl.program_id(0)
    half = hgot_ref.shape[0]
    s = spot_ref[4]
    near = pl.ds(pl.multiple_of(s * half, half), half)
    far = pl.ds(pl.multiple_of((1 - s) * half, half), half)
    loads = Loads(sem)
    got = loads.add(hgot_ref, h_s.at[far])
    in_q, in_k, in_v = loads.add(wq_ref, wq_s), loads.add(wk_ref, wk_s), loads.add(wv_ref, wv_s)
    own = [loads.add(hin_ref.at[s], h_s.at[near])]
    own += [loads.add(a, b.at[near]) for a, b in ((qn_ref, q_s), (kn_ref, k_s), (vn_ref, v_s))]
    later = [loads.add(wo_ref, wo_s), loads.add(wc_ref, wc_s)]
    outs = [loads.add(a, b) for a, b in ((h_s, h_out), (q_s, q_out), (k_s, k_out), (v_s, v_out))]
    mixed_out = loads.add(m_s, m_out)

    @pl.when(at == 0)
    def _():
        for c in (got, in_q, in_k, in_v, *own, *later):
            c.start()
        one_hot(seg_ref[0:1, :], oh_ref)
        mask_of(seg_ref[0:1, :], mk_ref)
        mask_of(seg_ref[1:2, :], cross_mk_ref)
        got.wait()
        x = h_s[far, :]
        in_q.wait()
        q_s[far, :] = (dot(x, wq_s[...]) + v(V_QB)).astype(BF)
        in_k.wait()
        k_s[far, :] = dot(x, wk_s[...]).astype(BF)
        in_v.wait()
        v_s[far, :] = (dot(x, wv_s[...]) + v(V_VB)).astype(BF)
        for c in own:
            c.wait()
        for c in outs:
            c.start()

    @pl.when((at > 0) & (at <= pairs))
    def _():
        cols = columns(at - 1)

        args = lambda q, k: (q_s[q, cols], k_s[k, cols], v_s[k, cols], oh_ref[:, q], mk_ref[k, :])
        lo, hi = pl.ds(0, half), pl.ds(half, half)
        near_sums = [(mix_ref[64 * h : 64 * h + 64, :], stat_ref[0, h : h + 1, :], stat_ref[0, 2 + h : 3 + h, :]) for h in (0, 1)]
        heads = attend_rest(s == 0, near_sums, args(far, far), args(hi, lo))
        for i, rows in enumerate((lo, hi)):
            for h in (0, 1):
                l_ref[0, h : h + 1, rows] = heads[h][i][1]
            m_s[rows, cols] = jnp.concatenate([heads[h][i][0] for h in (0, 1)], 0).T.astype(BF)

    @pl.when(at == pairs + 1)
    def _():
        mixed_out.start()
        for c in later:
            c.wait()

    @pl.when(at > pairs)
    def _():
        rows = pl.ds(pl.multiple_of((at - pairs - 1) * half, half), half)
        x = h_s[rows, :].astype(F32) + (dot(m_s[rows, :], wo_s[...]) + v(V_OB))
        n, r = norm_stats(x)
        n_ref[...] = n
        r_ref[...] = r
        low = (n * v(V_G1) + v(V_B1)).astype(BF)
        low_ref[...] = low
        cq_ref[...] = (dot(low, wc_s[...]) + v(V_CQB)).astype(BF)

    @pl.when(at == pairs + 2)
    def _():
        for c in (*outs, mixed_out):
            c.wait()


def self_forward(order, spots, vec, segs, near_mix, near_stats, hidden_in, hidden_got, near, weights):
    half, D = hidden_got.shape
    T, pairs = 2 * half, D // 128
    token = lambda width: pl.BlockSpec((half, width), lambda i, p: (jnp.maximum(i - pairs - 1, 0), 0))
    hbm = pl.BlockSpec(memory_space=pl.ANY)
    masks = [(64, T), (T, 128), (T, 128)]
    pair = lambda i: jnp.clip(i - 1, 0, pairs - 1)
    return order.call(
        functools.partial(self_kernel, pairs=pairs), spots, vec, segs, near_mix, near_stats, hidden_in, hidden_got, *near, *weights,
        scalars=1, name="self_forward", us=25, grid=(pairs + 3,),
        in_specs=[full(vec.shape), full(segs.shape), pl.BlockSpec((128, half), lambda i, p: (pair(i), 0)),
                  pl.BlockSpec((1, 8, half), lambda i, p: (pair(i), 0, 0))] + [hbm] * 10,
        out_specs=[pl.BlockSpec((1, 8, T), lambda i, p: (pair(i), 0, 0)),
                   token(D), token(1), token(D), token(D)] + [still(s) for s in masks] + [hbm] * 5,
        out_shape=[shaped(pairs, 8, T, dtype=F32), shaped(T, D, dtype=F32), shaped(T, 1, dtype=F32), shaped(T, D), shaped(T, D)]
        + [shaped(*s) for s in masks] + [shaped(T, D)] * 5,
        scratch_shapes=[pltpu.VMEM((T, D), BF)] * 5 + [pltpu.VMEM((D, D), BF)] * 5 + [pltpu.SemaphoreType.DMA((15,))])


def cross_kernel(spot_ref, vec_ref, oh_ref, mask_ref, cq_ref, min_ref, mgot_ref, kn_ref, vn_ref, uk_ref, uv_ref,
                 l_ref, m_out, k_out, v_out, c_out, m_s, k_s, v_s, q_s, c_s, uk_s, uv_s, sem, *, pairs, bq):
    at = pl.program_id(0)
    half = mgot_ref.shape[0]
    s = spot_ref[4]
    near = pl.ds(pl.multiple_of(s * half, half), half)
    far = pl.ds(pl.multiple_of((1 - s) * half, half), half)
    loads = Loads(sem)
    got = loads.add(mgot_ref, m_s.at[far])
    in_k, in_v = loads.add(uk_ref, uk_s), loads.add(uv_ref, uv_s)
    own = [loads.add(min_ref.at[s], m_s.at[near]), loads.add(cq_ref, q_s)]
    own += [loads.add(kn_ref, k_s.at[near]), loads.add(vn_ref, v_s.at[near])]
    outs = [loads.add(a, b) for a, b in ((m_s, m_out), (k_s, k_out), (v_s, v_out))]

    @pl.when(at == 0)
    def _():
        for c in (got, in_k, in_v, *own):
            c.start()
        got.wait()
        x = m_s[far, :]
        in_k.wait()
        k_s[far, :] = dot(x, uk_s[...]).astype(BF)
        in_v.wait()
        v_s[far, :] = (dot(x, uv_s[...]) + vec_ref[V_CVB : V_CVB + 1, :]).astype(BF)
        for c in own:
            c.wait()
        for c in outs:
            c.start()

    @pl.when(at > 0)
    def _():
        cols = columns(at - 1)

        def put_total(h, i, row):
            l_ref[0, h : h + 1, i * bq : (i + 1) * bq] = row

        blocks = attend_pair(q_s[:, cols], k_s[:, cols], v_s[:, cols], oh_ref[...], mask_ref[...], put_total, bq)
        for i, b in enumerate(blocks):
            c_out[i * bq : (i + 1) * bq, :] = b

    @pl.when(at == pairs)
    def _():
        for c in outs:
            c.wait()


def cross_forward(order, spots, vec, oh, mask, cq, memory, memory_got, near, weights):
    half, D = memory_got.shape
    T, pairs = 2 * half, D // 128
    hbm = pl.BlockSpec(memory_space=pl.ANY)
    pair = lambda i: jnp.maximum(i - 1, 0)
    return order.call(
        functools.partial(cross_kernel, pairs=pairs, bq=512), spots, vec, oh, mask, cq, memory, memory_got, *near, *weights,
        scalars=1, name="cross_forward", us=23, grid=(pairs + 1,),
        in_specs=[full(a.shape) for a in (vec, oh, mask)] + [hbm] * 7,
        out_specs=[pl.BlockSpec((1, 8, T), lambda i, p: (pair(i), 0, 0))] + [hbm] * 3
        + [pl.BlockSpec((T, 128), lambda i, p: (0, pair(i)))],
        out_shape=[shaped(pairs, 8, T, dtype=F32)] + [shaped(T, D)] * 4,
        scratch_shapes=[pltpu.VMEM((T, D), BF)] * 4 + [pltpu.VMEM((16, 128), BF)] + [pltpu.VMEM((D, D), BF)] * 2
        + [pltpu.SemaphoreType.DMA((10,))])


def ffn_kernel(spot_ref, vec_ref, bin_ref, n1_ref, cm_ref, og_ref, oggot_ref, wco_ref, win_ref, wout_ref,
               own_ref, other_ref, sb_ref, cmb_ref, vo_ref, vi_ref, all_ref,
               act_s, ib_s, cm_s, og_s, wco_s, win_s, wout_s, fb_s, low_s, cb_s, stage_s, stage_sem, sem, *, parts):
    v = lambda i: vec_ref[i : i + 1, :]
    t = pl.program_id(0)
    half, D = oggot_ref.shape
    s = spot_ref[4]
    loads = Loads(sem)
    in_cm, in_co = loads.add(cm_ref, cm_s), loads.add(wco_ref, wco_s)
    in_up, in_down = loads.add(win_ref, win_s), loads.add(wout_ref, wout_s)
    in_og = [loads.add(og_ref.at[s], og_s.at[s]), loads.add(oggot_ref, og_s.at[1 - s])]

    def need(*copies):
        @pl.when(t == 0)
        def _():
            for c in copies:
                c.wait()

    @pl.when(t == 0)
    def _():
        for c in loads.copies:
            c.start()
        vo_ref[...] = jnp.zeros_like(vo_ref)
        vi_ref[...] = jnp.zeros_like(vi_ref)

    @pl.when(t < 2)
    def _():
        need(in_cm, in_co)
        rows = pl.ds(pl.multiple_of(t * half, half), half)
        first = n1_ref[...] * v(V_G1) + v(V_B1)
        n2, r2 = norm_stats(first + (dot(cm_s[rows, :], wco_s[...]) + v(V_COB)))
        second = n2 * v(V_G2) + v(V_B2)
        low = second.astype(BF)
        low_s[rows, :] = low
        need(in_up, in_down, *in_og)
        width = win_s.shape[1] // parts
        branch = None
        up = lambda c: dot(low, win_s[:, c * width : (c + 1) * width]) + bin_ref[:, c * width : (c + 1) * width]
        x = up(0)
        late = None
        for c in range(parts):
            cols = slice(c * width, (c + 1) * width)
            coming = up(c + 1) if c + 1 < parts else None
            act, slope = gelu_pair(x)
            ib_s[rows, cols] = slope.astype(BF)
            act = act.astype(BF)
            act_s[rows, cols] = act
            if late is not None:
                term = dot(late[1], wout_s[late[0], :])
                branch = term if branch is None else branch + term
            late = cols, act
            x = coming
        term = dot(late[1], wout_s[late[0], :])
        branch = term if branch is None else branch + term
        n3, r3 = norm_stats(second + (branch + v(V_FOB)))
        ho = (n3 * v(V_G3) + v(V_B3)).astype(BF)

        @pl.when(t == s)
        def _():
            own_ref[...] = ho

        @pl.when(t != s)
        def _():
            other_ref[...] = ho

        e = og_s[t].astype(F32)
        third = norm_back(e, n3, r3, v(V_G3))
        fb = third.astype(BF)
        fb_s[rows, :] = fb
        vo_ref[0:1, :] += sums(e * n3)
        vo_ref[1:2, :] += sums(e)
        vo_ref[2:3, :] += sums(fb.astype(F32))
        e = third
        up = lambda c: nt(fb, wout_s[c * width : (c + 1) * width, :])
        x = up(0)
        late = None
        for c in range(parts):
            cols = slice(c * width, (c + 1) * width)
            coming = up(c + 1) if c + 1 < parts else None
            ib = (x * ib_s[rows, cols].astype(F32)).astype(BF)
            ib_s[rows, cols] = ib
            vi_ref[:, cols] += sums(ib.astype(F32))
            if late is not None:
                e = e + nt(late[1], win_s[:, late[0]])
            late = cols, ib
            x = coming
        e = e + nt(late[1], win_s[:, late[0]])
        back = norm_back(e, n2, r2, v(V_G2))
        sb_ref[...] = back
        cb = back.astype(BF)
        cb_s[rows, :] = cb
        vo_ref[3:4, :] += sums(e * n2)
        vo_ref[4:5, :] += sums(e)
        vo_ref[5:6, :] += sums(cb.astype(F32))
        cmb_ref[...] = nt(cb, wco_s[...]).astype(BF)

    t = t - 2
    slot = t % 2

    def tall(b, slot):
        return pltpu.make_async_copy(stage_s.at[slot], all_ref.at[b, :, pl.ds(0, 4)], stage_sem.at[slot])

    def flat(b, slot):
        return pltpu.make_async_copy(stage_s.at[slot], all_ref.at[:, :, 4 + b], stage_sem.at[slot])

    @pl.when((t >= 2) & (t < 6))
    def _():
        tall(t - 2, slot).wait()

    @pl.when(t >= 6)
    def _():
        flat(t - 6, slot).wait()

    def put(x, g):
        stage_s[slot] = tn(x, g).astype(BF).reshape(4, 4, 48, D)

    @pl.when((t >= 0) & (t < 4))
    def _():
        put(act_s[:, columns(t, D)], fb_s[...])
        tall(t, slot).start()

    @pl.when((t >= 4) & (t < 8))
    def _():
        put(low_s[...], ib_s[:, columns(t - 4, D)])
        flat(t - 4, slot).start()

    @pl.when(t == 8)
    def _():
        put(cm_s[...], cb_s[...])
        flat(4, 0).start()
        flat(3, 1).wait()
        flat(4, 0).wait()


def ffn_both(order, spots, vec, bin_, n1, cm, out_grad, out_grad_got, weights):
    half, D = out_grad_got.shape
    T, FF = 2 * half, bin_.shape[1]
    token = lambda width: pl.BlockSpec((half, width), lambda i, p: (jnp.minimum(i, 1), 0))
    hbm = pl.BlockSpec(memory_space=pl.ANY)
    big = lambda *shape: pltpu.VMEM(shape, BF)
    return order.call(
        functools.partial(ffn_kernel, parts=6), spots, vec, bin_, n1, cm, out_grad, out_grad_got, *weights,
        scalars=1, name="ffn_both", us=60, grid=(11,),
        in_specs=[full(vec.shape), full(bin_.shape), token(D)] + [hbm] * 6,
        out_specs=[still((half, D)), still((half, D)), token(D), token(D), still((8, D)), still((1, FF)), hbm],
        out_shape=[shaped(half, D), shaped(half, D), shaped(T, D, dtype=F32), shaped(T, D),
                   shaped(8, D, dtype=F32), shaped(1, FF, dtype=F32), shaped(4, 4, 9, 48, D)],
        scratch_shapes=[big(T, FF), big(T, FF), big(T, D), big(2, half, D), big(D, D), big(D, FF), big(FF, D), big(T, D), big(T, D),
                        big(T, D), big(2, 4, 4, 48, D), pltpu.SemaphoreType.DMA((2,)), pltpu.SemaphoreType.DMA((6,))])


def cross_back_kernel(spot_ref, q_ref, k_ref, v_ref, do_ref, o_ref, l_ref, oh_ref, mask_ref, wk_in, wv_in,
                      dq_ref, dk_ref, dv_ref, own_ref, other_ref, acc_s, dk_s, dv_s, wk_s, wv_s, sem, *, pairs, bk):
    at = pl.program_id(0)
    half = own_ref.shape[0]
    loads = Loads(sem)
    loads.add(wk_in, wk_s), loads.add(wv_in, wv_s)

    @pl.when(at == 0)
    def _():
        for c in loads.copies:
            c.start()

    @pl.when(at < pairs)
    def _():
        out = {"q": dq_ref, "k": dk_ref, "v": dv_ref}

        def put(name, rows, block):
            out[name][rows, :] = block
            if name != "q":
                {"k": dk_s, "v": dv_s}[name][rows, columns(at)] = block

        attend_pair_back(q_ref[...], k_ref[...], v_ref[...], do_ref[...], o_ref[...], [l_ref[0, h : h + 1, :] for h in (0, 1)],
                         oh_ref[...], mask_ref[...], acc_s, put, bk, False)

    @pl.when(at == pairs)
    def _():
        for c in loads.copies:
            c.wait()

    t = at - pairs

    @pl.when(t >= 0)
    def _():
        rows = pl.ds(pl.multiple_of(t * half, half), half)
        mg = (nt(dk_s[rows, :], wk_s[...]) + nt(dv_s[rows, :], wv_s[...])).astype(BF)

        @pl.when(t == spot_ref[4])
        def _():
            own_ref[...] = mg

        @pl.when(t != spot_ref[4])
        def _():
            other_ref[...] = mg


def cross_back(order, spots, q, k, v, do, o, totals, oh, mask, weights):
    T, D = q.shape
    pairs, half = D // 128, T // 2
    p_in = lambda i: jnp.minimum(i, pairs - 1)
    pair = pl.BlockSpec((T, 128), lambda i, p: (0, p_in(i)))
    hbm = pl.BlockSpec(memory_space=pl.ANY)
    return order.call(
        functools.partial(cross_back_kernel, pairs=pairs, bk=512), spots, q, k, v, do, o, totals, oh, mask, *weights,
        scalars=1, name="cross_back", us=38, grid=(pairs + 2,),
        in_specs=[pair] * 5 + [pl.BlockSpec((1, 8, T), lambda i, p: (p_in(i), 0, 0)), full(oh.shape), full(mask.shape), hbm, hbm],
        out_specs=[pair] * 3 + [still((half, D))] * 2, out_shape=[shaped(T, D)] * 3 + [shaped(half, D)] * 2,
        scratch_shapes=[pltpu.VMEM((128, T), F32)] + [pltpu.VMEM((T, D), BF)] * 2 + [pltpu.VMEM((D, D), BF)] * 2
        + [pltpu.SemaphoreType.DMA((2,))])


def middle_kernel(spot_ref, vec_ref, q_ref, n_ref, r_ref, sb_ref,
                  k_in, v_in, low_in, src_in, mix_in, wq_in, wo_in,
                  fb_ref, mb_ref, vo_ref, send_ref, keep_ref,
                  dq_s, dk_s, dv_s, back_s, low_s, src_s, mix_s, wq_s, wo_s, sem):
    v = lambda i: vec_ref[i : i + 1, :]
    t = pl.program_id(0)
    half, D = mb_ref.shape
    loads = Loads(sem)
    first = [loads.add(wq_in, wq_s), loads.add(wo_in, wo_s)]
    last = [loads.add(a, b) for a, b in ((low_in, low_s), (src_in, src_s), (mix_in, mix_s), (k_in, dk_s), (v_in, dv_s))]

    @pl.when(t == 0)
    def _():
        for c in loads.copies:
            c.start()
        vo_ref[...] = jnp.zeros_like(vo_ref)
        for c in first:
            c.wait()

    @pl.when(t < 2)
    def _():
        rows = pl.ds(pl.multiple_of(t * half, half), half)
        dq = q_ref[...]
        dq_s[rows, :] = dq
        n = n_ref[...]
        e = sb_ref[...] + nt(dq, wq_s[...])
        back = norm_back(e, n, r_ref[...], v(V_G1))
        fb_ref[...] = back
        low = back.astype(BF)
        back_s[rows, :] = low
        vo_ref[0:1, :] += sums(e * n)
        vo_ref[1:2, :] += sums(e)
        vo_ref[2:3, :] += sums(low.astype(F32))
        vo_ref[3:4, :] += sums(dq.astype(F32))
        mb_ref[...] = nt(low, wo_s[...]).astype(BF)

    @pl.when(t == 2)
    def _():
        for c in last:
            c.wait()
        vo_ref[4:5, :] = sums(dv_s[...].astype(F32))

    for i, (x, g) in enumerate(((low_s, dq_s), (src_s, dk_s), (src_s, dv_s), (mix_s, back_s))):
        @pl.when(t == 2 + i)
        def _():
            total = tn(x[...], g[...]).astype(BF)
            def put_piece(which, x, zl, zh, rows):
                for k in range(2):
                    (send_ref, keep_ref)[which][at_of(PLACES, x=x, y=k, zl=zl, zh=zh) + (0,)] = rows[:, D // 2 * k : D // 2 * (k + 1)]

            place_rows(spot_ref[0], total, 48, put_piece)


def middle(order, spots, vec, dq, dk, dv, n1, r1, sb, low, source, mixed, weights):
    T, D = n1.shape
    half = T // 2
    token = lambda width: pl.BlockSpec((half, width), lambda i, p: (jnp.minimum(i, 1), 0))
    out = pl.BlockSpec((2, 2, 2, 2, 1, 48, D // 2), lambda i, p: (0, 0, 0, 0, jnp.maximum(i - 2, 0), 0, 0))
    hbm = pl.BlockSpec(memory_space=pl.ANY)
    square, rect = pltpu.VMEM((D, D), BF), pltpu.VMEM((T, D), BF)
    return order.call(
        middle_kernel, spots, vec, dq, n1, r1, sb, dk, dv, low, source, mixed, *weights, scalars=1, name="middle", us=18,
        grid=(6,),
        in_specs=[full(vec.shape)] + [token(D), token(D), token(1), token(D)] + [hbm] * 7,
        out_specs=[token(D), token(D), still((8, D)), out, out],
        out_shape=[shaped(T, D, dtype=F32), shaped(T, D), shaped(8, D, dtype=F32)]
        + [shaped(2, 2, 2, 2, 4, 48, D // 2)] * 2,
        scratch_shapes=[rect] * 7 + [square] * 2 + [pltpu.SemaphoreType.DMA((7,))])


def back_kernel(spot_ref, *refs, n, plain):
    own_ref, other_ref = refs[-2:]
    total = refs[2 * n][...] if plain else None
    for g, w in zip(refs[:n], refs[n : 2 * n]):
        term = nt(g[...], w[...])
        total = term if total is None else total + term
    total = total.astype(BF)

    @pl.when(pl.program_id(0) == spot_ref[4])
    def _():
        own_ref[...] = total

    @pl.when(pl.program_id(0) != spot_ref[4])
    def _():
        other_ref[...] = total


def back_rows(order, spots, grads, weights, plain=None):
    T, D = grads[0].shape
    half, n = T // 2, len(grads)
    more = [] if plain is None else [plain]
    r = pl.BlockSpec((half, D), lambda i, p: (i, 0))
    return order.call(
        functools.partial(back_kernel, n=n, plain=plain is not None), spots, *grads, *weights, *more,
        scalars=1, name="back_rows", us=9, grid=(2,), in_specs=[r] * n + [full((D, D))] * n + [r] * len(more),
        out_specs=[still((half, D))] * 2, out_shape=[shaped(half, D)] * 2)


def place_rows(core, total, height, put):
    for j in range(total.shape[0] // (2 * height)):
        even = total[2 * j * height : (2 * j + 1) * height]
        odd = total[(2 * j + 1) * height : (2 * j + 2) * height]
        put(1, j % 2, (j // 2) % 2, j // 4, jnp.where(core == 0, even, odd))
        put(0, j % 2, (j // 2) % 2, j // 4, jnp.where(core == 0, odd, even))


PLACES = "y", "zl", "x", "zh"
GROUP_LINKS = *PLACES, "gather"


def at_of(order, **place):
    return tuple(place[name] for name in order)


def self_back_kernel(spot_ref, q_ref, k_ref, v_ref, do_ref, o_ref, l_ref, oh_ref, mk_ref, vf_ref, v1_ref, vi_ref, h_in,
                     dq_ref, dk_ref, dv_ref, send_ref, keep_ref, acc_s, g_s, h_s, sem, *, pairs, bk):
    at = pl.program_id(0)
    hidden = pltpu.make_async_copy(h_in, h_s, sem)
    D = 128 * pairs
    wide = D // 2

    @pl.when(at == 0)
    def _():
        hidden.start()

    @pl.when(at < pairs)
    def _():
        out = {"q": (dq_ref, 0), "k": (dk_ref, 1), "v": (dv_ref, 2)}

        def put(name, rows, block):
            ref, i = out[name]
            ref[rows, :] = block
            g_s[i, rows, columns(at)] = block

        attend_pair_back(q_ref[...], k_ref[...], v_ref[...], do_ref[...], o_ref[...], [l_ref[0, h : h + 1, :] for h in (0, 1)],
                         oh_ref[...], mk_ref[...], acc_s, put, bk, True)

    core = spot_ref[0]
    height = 3 * 48 + 16

    def at_row(x, y, zl, zh):
        place = {"x": x, "y": y, "zl": zl, "zh": zh}
        row = 0
        for name in PLACES:
            row = 2 * row + place[name]
        return height * row

    for i in range(3):
        @pl.when(at == pairs + i)
        def _():
            if i == 0:
                hidden.wait()

            def put_piece(which, x, zl, zh, rows):
                for k in range(2):
                    row = at_row(x, k, zl, zh) + 48 * i
                    (send_ref, keep_ref)[which][row : row + 48, :] = rows[:, wide * k : wide * (k + 1)]

            place_rows(core, tn(h_s[...], g_s[i]).astype(BF), 48, put_piece)

    @pl.when(at == pairs + 2)
    def _():
        row_of = lambda i: sums(g_s[i].astype(F32))
        rows = jnp.concatenate([vf_ref[0:6, :], v1_ref[0:5, :], row_of(0), row_of(2), jnp.zeros((3, D), F32)], 0)
        spread = jnp.broadcast_to(vi_ref[...], (16, vi_ref.shape[1]))
        for first, part, w in ((0, rows, 48), (128, spread, 192)):
            for j in range(8):
                even = part[:, 2 * j * w : (2 * j + 1) * w].astype(BF)
                odd = part[:, (2 * j + 1) * w : (2 * j + 2) * w].astype(BF)
                row = at_row(j % 2, 0, (j // 2) % 2, j // 4) + 144
                keep_ref[row : row + 16, first : first + w] = jnp.where(core == 0, even, odd)
                send_ref[row : row + 16, first : first + w] = jnp.where(core == 0, odd, even)


def self_back(order, spots, q, k, v, do, o, totals, oh, mk, vectors, hidden, moves):
    T, D = q.shape
    pairs = D // 128
    p_in = lambda i: jnp.minimum(i, pairs - 1)
    pair = pl.BlockSpec((T, 128), lambda i, p: (0, p_in(i)))
    rows = 16 * (3 * 48 + 16)
    return order.call(
        functools.partial(self_back_kernel, pairs=pairs, bk=256), spots, q, k, v, do, o, totals, oh, mk, *vectors, hidden,
        scalars=1, name="self_back", us=30, grid=(pairs + 3,), moves=moves,
        in_specs=[pair] * 5 + [pl.BlockSpec((1, 8, T), lambda i, p: (p_in(i), 0, 0))]
        + [full(a.shape) for a in (oh, mk, *vectors)] + [pl.BlockSpec(memory_space=pl.ANY)],
        out_specs=[pair] * 3 + [still((rows, D // 2))] * 2, out_shape=[shaped(T, D)] * 3 + [shaped(rows, D // 2)] * 2,
        scratch_shapes=[pltpu.VMEM((128, T), F32), pltpu.VMEM((3, T, D), BF), pltpu.VMEM((T, D), BF), pltpu.SemaphoreType.DMA])


def fold_kernel(spot_ref, keep_ref, keep_other_ref, got_ref, got_other_ref, sum_ref, send_ref):
    sum_ref[...] = keep_ref[0] + got_ref[0]
    send_ref[...] = keep_other_ref[0] + got_other_ref[0]


def small_fold_kernel(spot_ref, *refs, items, keeps, gots):
    keep_refs, got_refs, outs = refs[:keeps], refs[keeps : keeps + gots], refs[keeps + gots :]
    for i, (came, spots, messages) in enumerate(items):
        keep, out = keep_refs[i], outs[i]
        rows = out.shape[0]

        def piece(p):
            part = lambda first: pl.ds(pl.multiple_of(first + p * rows, 16), rows)
            total = keep[part(0), :]
            for g, at in came:
                total = total + got_refs[g][part(at), :]
            return total

        mine = 0
        for s in spots:
            mine = 2 * mine + spot_ref[s]
        out[...] = piece(mine)
        for n, (m, first) in enumerate(messages):
            outs[keeps + m][first : first + rows, :] = out[...] if not spots else piece(mine ^ (n + 1))


LINKS = {"core": ([("dp", 1, 16)], (0,)), "x": ([("dp", 2, 16)], (1,)), "zl": ([("dp", 4, 16)], (2,)), "zh": ([("dp", 8, 16)], (3,)),
         "z": ([("dp", 8, 16), ("dp", 4, 16), ("dp", 12, 16)], (2, 3)), "y": ([("seq", 1, 2)], (4,)),
         "sum": ([("seq", 1, 2)], ()), "gather": ([("seq", 1, 2)], ())}


class Sum:
    def __init__(self, keep, got, *links):
        self.keep, self.gots = keep, [(got, 0)]
        self.links, self.step = links, 0

    def link(self):
        return self.links[self.step] if self.step < len(self.links) else None


def first_swap(send, keep, after=None):
    if after is not None:
        send, _ = lax.optimization_barrier((send, after))
    flat = lambda a: a.reshape(-1, a.shape[-1])
    return flat(keep), swap(flat(send), *LINKS["core"][0][0])


def advance(order, spots, *groups):
    groups = [g for g in groups if g.link() is not None]
    links = [LINKS[g.link()] for g in groups]
    rows = [g.keep.shape[0] >> len(places) for g, (_, places) in zip(groups, links)]
    if len(groups) == 1 and len(links[0][1]) == 1 and len(groups[0].gots) == 1:
        (g,), ((to,), (which,)), (r,) = groups, links[0], rows
        width = g.keep.shape[1]
        steps = next(s for s in (4, 2, 1) if r % (16 * s) == 0)
        keep, got = g.keep.reshape(2, r, width), g.gots[0][0].reshape(2, r, width)
        mine = pl.BlockSpec((1, r // steps, width), lambda i, p: (p[which], i, 0))
        other = pl.BlockSpec((1, r // steps, width), lambda i, p: (1 - p[which], i, 0))
        g.keep, send = order.call(
            fold_kernel, spots, keep, keep, got, got, scalars=1, name="fold", us=3, grid=(steps,),
            in_specs=[mine, other, mine, other], out_specs=[pl.BlockSpec((r // steps, width), lambda i, p: (i, 0))] * 2,
            out_shape=[shaped(r, width)] * 2)
        g.gots = [(swap(send, *to), 0)]
        g.step += 1
        return
    gots = []
    for g in groups:
        for a, _ in g.gots:
            if not any(a is b for b in gots):
                gots.append(a)
    messages, heights, items = [], [], []
    for g, (tos, places), r in zip(groups, links, rows):
        sent = []
        for to in tos:
            key = to, g.keep.shape[1]
            if key not in messages:
                messages.append(key)
                heights.append(0)
            m = messages.index(key)
            sent.append((m, heights[m]))
            heights[m] += r
        items.append(([(next(n for n, b in enumerate(gots) if a is b), at) for a, at in g.gots], places, sent))
    shapes = [(r, g.keep.shape[1]) for r, g in zip(rows, groups)] + [(h, w) for h, (_, w) in zip(heights, messages)]
    arrays = [g.keep for g in groups] + gots
    out = order.call(
        functools.partial(small_fold_kernel, items=items, keeps=len(groups), gots=len(gots)), spots, *arrays, scalars=1,
        name="fold", us=3, grid=(1,), in_specs=[full(a.shape) for a in arrays],
        out_specs=[still(s) for s in shapes], out_shape=[shaped(*s) for s in shapes])
    came = [swap(out[len(groups) + m], *to) for m, (to, _) in enumerate(messages)]
    for i, g in enumerate(groups):
        g.keep = out[i]
        g.gots = [(came[m], first) for m, first in items[i][2]]
        g.step += 1


def finish_ffn_kernel(spot_ref, own_ref, got_ref, fi, fo, co):
    f32 = lambda v: v.astype(F32)
    D = own_ref.shape[1]
    for half in range(2):
        @pl.when(pl.program_id(0) == half)
        def _():
            part = lambda first, rows: f32(own_ref[first : first + rows, :] + got_ref[first : first + rows, :])
            fo[...] = part(96 * half, 96)
            for b in range(2):
                fi[:, D * b : D * (b + 1)] = part(192 + 96 * half + 48 * b, 48)
            if half:
                co[...] = part(384, 48)


def finish_ffn(order, spots, own, got, moves):
    D = own.shape[1]
    shapes = (48, 4 * D), (192, D), (48, D)
    return order.call(
        finish_ffn_kernel, spots, own, got, scalars=1, name="finish_ffn", us=3, grid=(2,), moves=moves,
        in_specs=[full(own.shape), full(got.shape)],
        out_specs=[pl.BlockSpec((48, 2 * D), lambda i, p: (0, i)), pl.BlockSpec((96, D), lambda i, p: (i, 0)), still((48, D))],
        out_shape=[shaped(*s, dtype=F32) for s in shapes])


def finish_kernel(spot_ref, *refs, groups, ats):
    ins, (sq, sk, sv, so, cq, ck, cv, *vectors) = refs[: 2 * groups], refs[2 * groups :]
    f32 = lambda v: v.astype(F32)
    unit = lambda v, u: f32(v[48 * u : 48 * u + 48])
    first = spot_ref[4] == 0
    pairs = []
    for i, at in enumerate(ats):
        own = ins[2 * i][...]
        pairs.append((own, ins[2 * i + 1][at : at + own.shape[0], :]))
    join = lambda own, got: (jnp.where(first, own, got), jnp.where(first, got, own))
    cross, own = join(*pairs[0]), join(*pairs[1])
    w = own[0].shape[1]
    for k in range(2):
        cols = slice(k * w, (k + 1) * w)
        for i, o in enumerate((cq, ck, cv, so)):
            o[:, cols] = unit(cross[k], i)
        for i, o in enumerate((sq, sk, sv)):
            o[:, cols] = unit(own[k], i)
    rows = f32(own[0][144:160])
    for i, o in enumerate(vectors[:13]):
        o[...] = rows[i : i + 1, :48]
    vectors[13][...] = rows[0:1, 128:320]


def finish(order, spots, *groups):
    D = 2 * groups[0].keep.shape[1]
    arrays = [a for g in groups for a in (g.keep, g.gots[0][0])]
    shapes = [(48, D)] * 7 + [(1, 48)] * 13 + [(1, 192)]
    return order.call(
        functools.partial(finish_kernel, groups=len(groups), ats=[g.gots[0][1] for g in groups]), spots, *arrays, scalars=1,
        name="finish", us=3, grid=(1,), in_specs=[full(a.shape) for a in arrays], out_specs=[still(s) for s in shapes],
        out_shape=[shaped(*s, dtype=F32) for s in shapes])


def swap(block, ax, bit, size):
    return lax.ppermute(block, ax, [(i, i ^ bit) for i in range(size)])


def two(s, first, second):
    return jnp.where(s == 0, jnp.concatenate([first, second], 0), jnp.concatenate([second, first], 0))


def pick(array, index, axis):
    return lax.dynamic_index_in_dim(array, index, axis, keepdims=False)


def whole_rows(
    hidden_in, memory, tgt_segment, src_segment, out_grad,
    self_query, query_bias, self_key, self_value, value_bias, self_output, output_bias,
    first_gain, first_shift,
    cross_query, cross_query_bias, cross_key, cross_value, cross_value_bias, cross_output,
    cross_output_bias, second_gain, second_shift,
    ffn_in, ffn_in_bias, ffn_out, ffn_out_bias, third_gain, third_shift,
):
    f32 = lambda v: v.astype(F32)
    s = lax.axis_index("seq")
    dp = lax.axis_index("dp")
    place = dp % 2, (dp // 2) % 2, (dp // 4) % 2, dp // 8, s
    spots = jnp.stack(place).astype(jnp.int32)
    order = Order()
    segs = jnp.stack([tgt_segment, src_segment])
    segs_own, segs_got = pick(segs, s, 1), swap(pick(segs, 1 - s, 1), "seq", 1, 2)
    segs = jnp.where(s == 0, jnp.concatenate([segs_own, segs_got], 1), jnp.concatenate([segs_got, segs_own], 1))
    hidden_got = swap(pick(hidden_in, 1 - s, 0), "seq", 1, 2)
    vec = jnp.stack([query_bias, value_bias, output_bias, first_gain, first_shift, cross_query_bias, cross_value_bias,
                     cross_output_bias, second_gain, second_shift, ffn_out_bias, third_gain, third_shift]).astype(F32)
    bin_ = f32(ffn_in_bias).reshape(1, -1)
    *near_self, near_key, near_value, memory_far, out_grad_far, near_mix, near_stats = project_near(
        order, spots, tgt_segment, hidden_in, memory, out_grad, vec, [self_query, self_key, self_value, cross_key, cross_value])
    memory_far, hidden_got, segs = lax.optimization_barrier((memory_far, hidden_got, segs))
    memory_got = swap(memory_far, "seq", 1, 2)
    (self_totals, n1, r1, first_low, cross_queries, self_oh, self_mk, cross_mk,
     hidden, queries, key_rows, value_rows, self_mixed) = self_forward(
        order, spots, vec, segs, near_mix, near_stats, hidden_in, hidden_got, near_self,
        [self_query, self_key, self_value, self_output, cross_query])
    out_grad_far, memory_got, r1 = lax.optimization_barrier((out_grad_far, memory_got, r1))
    out_grad_got = swap(out_grad_far, "seq", 1, 2)
    cross_totals, source, memory_keys, memory_values, cross_mixed = cross_forward(
        order, spots, vec, self_oh, cross_mk, cross_queries, memory, memory_got, [near_key, near_value], [cross_key, cross_value])
    ho, ho_far, second_back, cross_mixed_back, v_ffn, v_in, ffn_all = ffn_both(
        order, spots, vec, bin_, n1, cross_mixed, out_grad, out_grad_got, [cross_output, ffn_in, ffn_out])
    ho_got = swap(ho_far, "seq", 1, 2)
    ffn_sum = lax.psum_scatter(ffn_all.reshape(16, 432, -1), "dp", scatter_dimension=0, tiled=False)
    cross_query_back, memory_key_back, memory_value_back, mg, mg_far = cross_back(
        order, spots, cross_queries, memory_keys, memory_values, cross_mixed_back, cross_mixed, cross_totals, self_oh, cross_mk,
        [cross_key, cross_value])
    mg_far, ho_got = lax.optimization_barrier((mg_far, ho_got))
    mg_got = swap(mg_far, "seq", 1, 2)
    first_back, self_mixed_back, v_first, *pairs = middle(
        order, spots, vec, cross_query_back, memory_key_back, memory_value_back, n1, r1, second_back, first_low, source,
        self_mixed, [cross_query, self_output])
    cross_sum = Sum(*first_swap(*pairs, mg_got), *GROUP_LINKS)
    advance(order, spots, cross_sum)
    query_back, key_back, value_back, send, keep, hidden_out, memory_grad = self_back(
        order, spots, queries, key_rows, value_rows, self_mixed_back, self_mixed, self_totals, self_oh, self_mk,
        [v_ffn, v_first, v_in], hidden, [(ho, ho_got), (mg, mg_got)])
    self_sum = Sum(*first_swap(send, keep, cross_sum.gots[0][0]), *GROUP_LINKS)
    advance(order, spots, self_sum)
    advance(order, spots, cross_sum)
    hg, hg_far = back_rows(
        order, spots, [query_back, key_back, value_back], [self_query, self_key, self_value], first_back)
    hg_far, came, hg = lax.optimization_barrier((hg_far, self_sum.gots[0][0], hg))
    self_sum.gots = [(came, 0)]
    hg_got = swap(hg_far, "seq", 1, 2)
    ffn_sum, hg = lax.optimization_barrier((ffn_sum, hg))
    ffn_got = swap(ffn_sum, "seq", 1, 2)
    advance(order, spots, cross_sum, self_sum)
    advance(order, spots, cross_sum, self_sum)
    order.last.append(hg_got)
    advance(order, spots, cross_sum, self_sum)
    g_fi, g_fo, g_co, hidden_grad = finish_ffn(order, spots, ffn_sum, ffn_got, [(hg, hg_got)])
    advance(order, spots, cross_sum, self_sum)
    g_sq, g_sk, g_sv, g_so, g_cq, g_ck, g_cv, *v, v_fi = finish(order, spots, cross_sum, self_sum)
    (g3, b3, fob, g2, b2, cob, g1, b1, ob, cqb, cvb, qb, vb) = [a.reshape(-1) for a in v]
    return (
        hidden_out, hidden_grad, memory_grad,
        g_sq, qb, g_sk, g_sv, vb, g_so, ob, g1, b1, g_cq, cqb, g_ck, g_cv, cvb, g_co, cob, g2, b2,
        g_fi, v_fi.reshape(-1), g_fo, fob, g3, b3,
    )


def solution(mesh):
    in_specs = (
        P("dp", "seq", None),
        P("dp", "seq", None),
        P("dp", "seq"),
        P("dp", "seq"),
        P("dp", "seq", None),
        P(),
        P(),
        P(),
        P(),
        P(),
        P(),
        P(),
        P(),
        P(),
        P(),
        P(),
        P(),
        P(),
        P(),
        P(),
        P(),
        P(),
        P(),
        P(),
        P(),
        P(),
        P(),
        P(),
        P(),
    )
    out_specs = (
        P("dp", "seq", None),
        P("dp", "seq", None),
        P("dp", "seq", None),
        P("dp", None),
        P("dp"),
        P("dp", None),
        P("dp", None),
        P("dp"),
        P("dp", None),
        P("dp"),
        P("dp"),
        P("dp"),
        P("dp", None),
        P("dp"),
        P("dp", None),
        P("dp", None),
        P("dp"),
        P("dp", None),
        P("dp"),
        P("dp"),
        P("dp"),
        P("dp", None),
        P("dp"),
        P("dp", None),
        P("dp"),
        P("dp"),
        P("dp"),
    )
    rows_form = mesh.shape["seq"] == 2 and mesh.shape["dp"] == 16

    def on_device(*arrays):
        if rows_form and arrays[0].shape[0] == 2:
            return whole_rows(*arrays)
        return split_rows(*arrays)

    return jax.shard_map(
        on_device, mesh=mesh, in_specs=in_specs, out_specs=out_specs, check_vma=False
    )
```

```python
import functools
import math

import jax
import jax.numpy as jnp
from jax import lax
from jax.experimental import pallas as pl
from jax.experimental.pallas import tpu as pltpu
from jax.sharding import PartitionSpec as P

HEADS = 12
BF=jnp.bfloat16; F32=jnp.float32
BIG=-1e30
def dot(a,b): return jnp.dot(a,b,preferred_element_type=F32)

def lane_low(shape): return lax.broadcasted_iota(jnp.int32, shape, 1) < 64

def prepare(q,k,v,oh,mk):
    low=lane_low(k.shape)
    qT=(q*BF(0.125)).T
    vT=v.T
    ones=jnp.ones((16,k.shape[0]),BF)
    kas=[jnp.where(low,k,mk),jnp.where(low,mk,k)]
    vas=[jnp.concatenate([vT[64*h:64*h+64],ones],0) for h in (0,1)]
    qas=[jnp.concatenate([qT[:64],oh],0),jnp.concatenate([oh,qT[64:]],0)]
    return kas,vas,qas

def causal_block(n):
    return lax.broadcasted_iota(jnp.int32,(n,n),0)<=lax.broadcasted_iota(jnp.int32,(n,n),1)

def attend_near(q,k,v,oh,mk):
    kas,vas,qas=prepare(q,k,v,oh,mk)
    dm=causal_block(q.shape[0])
    ss=[jnp.where(dm,dot(kas[h],qas[h]),BIG) for h in (0,1)]
    out=[]
    for h in (0,1):
        m=jnp.max(ss[h],axis=0,keepdims=True)
        o=dot(vas[h],jnp.exp(ss[h]-m).astype(BF))
        out.append((o[:64],m,o[64:65]))
    return out

def attend_rest(first,near,far_args,off_args):
    far=prepare(*far_args); off=prepare(*off_args)
    dm=causal_block(far_args[0].shape[0])
    fs=[jnp.where(dm,dot(far[0][h],far[2][h]),BIG) for h in (0,1)]
    os=[]; result=[]
    for h in (0,1):
        os.append(dot(off[0][h],off[2][h]))
        m=jnp.max(fs[h],axis=0,keepdims=True)
        p=jnp.exp(fs[h]-m).astype(BF)
        o=dot(far[1][h],p)
        here=(o[:64],m,o[64:65])
        result.append(([jnp.where(first,a,b) for a,b in zip(near[h],here)],[jnp.where(first,b,a) for a,b in zip(near[h],here)]))
    out=[]
    for h in (0,1):
        (o0,m0,l0),(o1,m1,l1)=result[h]
        m=jnp.maximum(m1,jnp.max(os[h],axis=0,keepdims=True))
        p=jnp.exp(os[h]-m).astype(BF)
        w=jnp.exp(m1-m)
        o=dot(off[1][h],p)
        l=o[64:65]+w*l1
        out.append(((o0/l0,m0+jnp.log(l0)),((o[:64]+w*o1)/l,m+jnp.log(l))))
    return out

def attend_pair(q,k,v,oh,mk,put_total,bq):
    T=q.shape[0]
    kas,vas,qas=prepare(q,k,v,oh,mk)
    def scores(i,h):
        return dot(kas[h],qas[h][:,i*bq:(i+1)*bq])
    def weigh(s):
        m=jnp.max(s,axis=0,keepdims=True)
        return m,jnp.exp(s-m).astype(BF)
    def mix(i,h,m,p):
        o=dot(vas[h],p)
        l=o[64:65]
        put_total(h,i,m+jnp.log(l))
        return o[:64]/l
    units=[(i,h) for i in range(T//bq) for h in (0,1)]
    os=[]
    s=scores(*units[0]); late=None
    for n,u in enumerate(units):
        coming=scores(*units[n+1]) if n+1<len(units) else None
        m,p=weigh(s)
        if late is not None: os.append(mix(*late))
        late=(*u,m,p)
        s=coming
    os.append(mix(*late))
    return [jnp.concatenate(os[2*i:2*i+2],0).T.astype(BF) for i in range(T//bq)]

def split3(x):
    a=x.astype(BF); r=x-a.astype(F32); b=r.astype(BF); c=(r-b.astype(F32)).astype(BF)
    return a,b,c

def attend_pair_back(q,k,v,do,o,totals,oh,mk,acc_ref,put,bk,causal):
    T=q.shape[0]; K=k.shape[0]
    low=lane_low((K,128))
    q=q*BF(0.125)
    qT=q.T; doT=do.T
    kT=k.T
    prodT=(do.astype(F32)*o.astype(F32)).T
    rowi=lax.broadcasted_iota(jnp.int32,(64,T),0)
    one=jnp.full((K,128),-1.0,BF)
    if causal:
        dm=lax.broadcasted_iota(jnp.int32,(bk,bk),0)<=lax.broadcasted_iota(jnp.int32,(bk,bk),1)
    qas=[];das=[]
    for h in (0,1):
        a,b,c=split3(totals[h])
        ohl=jnp.where(rowi==4,a,jnp.where(rowi==5,b,jnp.where(rowi==6,c,oh)))
        D=jnp.sum(prodT[64*h:64*h+64],axis=0,keepdims=True)
        a,b,c=split3(D)
        z=jnp.zeros((64,T),BF)
        dd=jnp.where(rowi==0,a,jnp.where(rowi==1,b,jnp.where(rowi==2,c,z)))
        if h==0:
            qas.append(jnp.concatenate([qT[:64],ohl],0)); das.append(jnp.concatenate([doT[:64],dd],0))
        else:
            qas.append(jnp.concatenate([ohl,qT[64:]],0)); das.append(jnp.concatenate([dd,doT[64:]],0))
    kas=[jnp.where(low,k,mk),jnp.where(low,mk,k)]
    vas=[jnp.where(low,v,one),jnp.where(low,one,v)]
    def ahead(j,h):
        q0=j*bk if causal else 0
        ks=slice(j*bk,(j+1)*bk)
        return dot(kas[h][ks],qas[h][:,q0:]),dot(vas[h][ks],das[h][:,q0:])
    def weigh(j,s,dp):
        q0=j*bk if causal else 0
        if causal:
            sd=jnp.where(dm,s[:,:bk],BIG)
            s=jnp.concatenate([sd,s[:,bk:]],1) if q0+bk<T else sd
        p=jnp.exp(s)
        return p.astype(BF),(p*dp).astype(BF)
    done={}
    def behind(j,h,p,ds):
        q0=j*bk if causal else 0
        ks=slice(j*bk,(j+1)*bk)
        done[h]=dot(ds,q[q0:]),dot(p,do[q0:])
        dqt=dot(kT[64*h:64*h+64,ks],ds)
        if j==0: acc_ref[64*h:64*h+64,:]=dqt
        else: acc_ref[64*h:64*h+64,q0:]+=dqt
        if h:
            lw=low[:bk]
            put("k",ks,jnp.where(lw,done[0][0],done[1][0]).astype(BF))
            put("v",ks,jnp.where(lw,done[0][1],done[1][1]).astype(BF))
    units=[(j,h) for j in range(K//bk) for h in (0,1)]
    now=ahead(*units[0]); late=None
    for n,u in enumerate(units):
        coming=ahead(*units[n+1]) if n+1<len(units) else None
        pd=weigh(u[0],*now)
        if late is not None: behind(*late)
        late=(*u,*pd)
        now=coming
    behind(*late)
    put("q",slice(0,T),(acc_ref[...]*0.125).T.astype(BF))


def project(values, weight):
    return jnp.dot(values, weight, preferred_element_type=jnp.float32)


def project_back(gradient, weight):
    return jnp.einsum("rte,de->rtd", gradient, weight, preferred_element_type=jnp.float32)


def weight_grad(values, gradient):
    return jnp.einsum("rtd,rte->de", values, gradient, preferred_element_type=jnp.float32)


def token_sum(gradient):
    return jnp.sum(gradient.astype(jnp.float32), axis=(0, 1))


def layer_norm(values, norm_gain, norm_shift):
    center = values - jnp.mean(values, axis=-1, keepdims=True)
    spread = jnp.mean(center * center, axis=-1, keepdims=True)
    return center * lax.rsqrt(spread + 1e-05) * norm_gain + norm_shift


def exact_gelu(values):
    return jax.nn.gelu(values, approximate=False)


def split_heads(values):
    return values.reshape(values.shape[0], values.shape[1], HEADS, values.shape[2] // HEADS)


def merge_heads(values):
    return values.reshape(values.shape[0], values.shape[1], values.shape[2] * values.shape[3])


def masked_scores(queries, key_rows, allowed):
    raw_scores = jnp.einsum(
        "rqhd,rkhd->rhqk",
        split_heads(queries),
        split_heads(key_rows),
        preferred_element_type=jnp.float32,
    )
    factor = 1.0 / math.sqrt(queries.shape[2] // HEADS)
    return jnp.where(allowed[:, None], raw_scores * factor, -1e30)


def attend_forward(queries, key_rows, value_rows, allowed):
    scores = masked_scores(queries, key_rows, allowed)
    highest = jnp.max(scores, axis=-1, keepdims=True)
    powers = jnp.exp(scores - highest)
    totals = jnp.sum(powers, axis=-1, keepdims=True)
    weights = (powers / totals).astype(jnp.bfloat16)
    mixed_heads = jnp.einsum(
        "rhqk,rkhd->rqhd", weights, split_heads(value_rows), preferred_element_type=jnp.float32
    )
    return (merge_heads(mixed_heads).astype(jnp.bfloat16), highest + jnp.log(totals))


def attend_backward(queries, key_rows, value_rows, allowed, log_totals, mixed_grad):
    scores = masked_scores(queries, key_rows, allowed)
    weights = jnp.exp(scores - log_totals)
    grad_heads = split_heads(mixed_grad)
    value_terms = jnp.einsum(
        "rhqk,rqhd->rkhd",
        weights.astype(jnp.bfloat16),
        grad_heads,
        preferred_element_type=jnp.float32,
    )
    weight_grads = jnp.einsum(
        "rqhd,rkhd->rhqk", grad_heads, split_heads(value_rows), preferred_element_type=jnp.float32
    )
    inner_sum = jnp.sum(weights * weight_grads, axis=-1, keepdims=True)
    factor = 1.0 / math.sqrt(queries.shape[2] // HEADS)
    score_grads = (weights * (weight_grads - inner_sum) * factor).astype(jnp.bfloat16)
    query_grads = jnp.einsum(
        "rhqk,rkhd->rqhd", score_grads, split_heads(key_rows), preferred_element_type=jnp.float32
    )
    key_terms = jnp.einsum(
        "rhqk,rqhd->rkhd", score_grads, split_heads(queries), preferred_element_type=jnp.float32
    )
    return (merge_heads(query_grads), merge_heads(key_terms), merge_heads(value_terms))


def split_rows(
    hidden_in,
    memory,
    tgt_segment,
    src_segment,
    out_grad,
    self_query,
    query_bias,
    self_key,
    self_value,
    value_bias,
    self_output,
    output_bias,
    first_gain,
    first_shift,
    cross_query,
    cross_query_bias,
    cross_key,
    cross_value,
    cross_value_bias,
    cross_output,
    cross_output_bias,
    second_gain,
    second_shift,
    ffn_in,
    ffn_in_bias,
    ffn_out,
    ffn_out_bias,
    third_gain,
    third_shift,
):
    tokens = hidden_in.shape[1]
    queries = (project(hidden_in, self_query) + query_bias.astype(jnp.float32)).astype(jnp.bfloat16)
    key_rows = project(hidden_in, self_key).astype(jnp.bfloat16)
    value_rows = (project(hidden_in, self_value) + value_bias.astype(jnp.float32)).astype(
        jnp.bfloat16
    )
    target_ids = tgt_segment.astype(jnp.bfloat16)
    all_keys, all_values, all_target = (
        lax.all_gather(key_rows, "seq", axis=1, tiled=True),
        lax.all_gather(value_rows, "seq", axis=1, tiled=True),
        lax.all_gather(target_ids, "seq", axis=1, tiled=True),
    )
    memory_keys = project(memory, cross_key).astype(jnp.bfloat16)
    memory_values = (project(memory, cross_value) + cross_value_bias.astype(jnp.float32)).astype(
        jnp.bfloat16
    )
    all_memkeys, all_memvalues, all_source = (
        lax.all_gather(memory_keys, "seq", axis=1, tiled=True),
        lax.all_gather(memory_values, "seq", axis=1, tiled=True),
        lax.all_gather(src_segment.astype(jnp.bfloat16), "seq", axis=1, tiled=True),
    )
    offset = lax.axis_index("seq") * tokens
    query_places = offset + jnp.arange(tokens, dtype=jnp.int32)
    key_places = jnp.arange(all_keys.shape[1], dtype=jnp.int32)
    self_allowed = (target_ids[:, :, None] == all_target[:, None, :]) & (
        query_places[:, None] >= key_places[None, :]
    )[None]
    cross_allowed = target_ids[:, :, None] == all_source[:, None, :]
    self_mixed, self_totals = attend_forward(queries, all_keys, all_values, self_allowed)
    self_branch = project(self_mixed, self_output) + output_bias.astype(jnp.float32)
    first_norm, first_pull = jax.vjp(
        layer_norm,
        hidden_in.astype(jnp.float32) + self_branch,
        first_gain.astype(jnp.float32),
        first_shift.astype(jnp.float32),
    )
    first_low = first_norm.astype(jnp.bfloat16)
    cross_queries = (project(first_low, cross_query) + cross_query_bias.astype(jnp.float32)).astype(
        jnp.bfloat16
    )
    cross_mixed, cross_totals = attend_forward(
        cross_queries, all_memkeys, all_memvalues, cross_allowed
    )
    cross_branch = project(cross_mixed, cross_output) + cross_output_bias.astype(jnp.float32)
    second_norm, second_pull = jax.vjp(
        layer_norm,
        first_norm + cross_branch,
        second_gain.astype(jnp.float32),
        second_shift.astype(jnp.float32),
    )
    second_low = second_norm.astype(jnp.bfloat16)
    inner_rows = project(second_low, ffn_in) + ffn_in_bias.astype(jnp.float32)
    activation_full, gelu_pull = jax.vjp(exact_gelu, inner_rows)
    activation = activation_full.astype(jnp.bfloat16)
    ffn_branch = project(activation, ffn_out) + ffn_out_bias.astype(jnp.float32)
    final_norm, third_pull = jax.vjp(
        layer_norm,
        second_norm + ffn_branch,
        third_gain.astype(jnp.float32),
        third_shift.astype(jnp.float32),
    )
    hidden_out = final_norm.astype(jnp.bfloat16)
    third_back, grad_third_gain, grad_third_shift = third_pull(out_grad.astype(jnp.float32))
    ffn_back = third_back.astype(jnp.bfloat16)
    grad_ffn_out = weight_grad(activation, ffn_back)
    grad_ffn_out_bias = token_sum(ffn_back)
    activation_back = project_back(ffn_back, ffn_out)
    inner_back = gelu_pull(activation_back)[0].astype(jnp.bfloat16)
    grad_ffn_in = weight_grad(second_low, inner_back)
    grad_ffn_in_bias = token_sum(inner_back)
    second_back, grad_second_gain, grad_second_shift = second_pull(
        third_back + project_back(inner_back, ffn_in)
    )
    cross_back = second_back.astype(jnp.bfloat16)
    grad_cross_output = weight_grad(cross_mixed, cross_back)
    grad_cross_output_bias = token_sum(cross_back)
    cross_mixed_back = project_back(cross_back, cross_output).astype(jnp.bfloat16)
    cross_query_grad, memkey_terms, memvalue_terms = attend_backward(
        cross_queries, all_memkeys, all_memvalues, cross_allowed, cross_totals, cross_mixed_back
    )
    memkey_sum, memvalue_sum = (
        lax.psum_scatter(
            memkey_terms.astype(jnp.bfloat16), "seq", scatter_dimension=1, tiled=True
        ).astype(jnp.float32),
        lax.psum_scatter(
            memvalue_terms.astype(jnp.bfloat16), "seq", scatter_dimension=1, tiled=True
        ).astype(jnp.float32),
    )
    memory_key_back = memkey_sum.astype(jnp.bfloat16)
    memory_value_back = memvalue_sum.astype(jnp.bfloat16)
    cross_query_back = cross_query_grad.astype(jnp.bfloat16)
    grad_cross_query = weight_grad(first_low, cross_query_back)
    grad_cross_query_bias = token_sum(cross_query_back)
    grad_cross_key = weight_grad(memory, memory_key_back)
    grad_cross_value = weight_grad(memory, memory_value_back)
    grad_cross_value_bias = token_sum(memory_value_back)
    memory_grad = (
        project_back(memory_key_back, cross_key) + project_back(memory_value_back, cross_value)
    ).astype(jnp.bfloat16)
    first_back, grad_first_gain, grad_first_shift = first_pull(
        second_back + project_back(cross_query_back, cross_query)
    )
    self_back = first_back.astype(jnp.bfloat16)
    grad_self_output = weight_grad(self_mixed, self_back)
    grad_output_bias = token_sum(self_back)
    self_mixed_back = project_back(self_back, self_output).astype(jnp.bfloat16)
    query_grad, key_terms, value_terms = attend_backward(
        queries, all_keys, all_values, self_allowed, self_totals, self_mixed_back
    )
    key_sum, value_sum = (
        lax.psum_scatter(
            key_terms.astype(jnp.bfloat16), "seq", scatter_dimension=1, tiled=True
        ).astype(jnp.float32),
        lax.psum_scatter(
            value_terms.astype(jnp.bfloat16), "seq", scatter_dimension=1, tiled=True
        ).astype(jnp.float32),
    )
    key_back = key_sum.astype(jnp.bfloat16)
    value_back = value_sum.astype(jnp.bfloat16)
    query_back = query_grad.astype(jnp.bfloat16)
    grad_self_query = weight_grad(hidden_in, query_back)
    grad_query_bias = token_sum(query_back)
    grad_self_key = weight_grad(hidden_in, key_back)
    grad_self_value = weight_grad(hidden_in, value_back)
    grad_value_bias = token_sum(value_back)
    hidden_grad = (
        first_back
        + project_back(query_back, self_query)
        + project_back(key_back, self_key)
        + project_back(value_back, self_value)
    ).astype(jnp.bfloat16)
    partial_grads = [
        grad_self_query,
        grad_query_bias,
        grad_self_key,
        grad_self_value,
        grad_value_bias,
        grad_self_output,
        grad_output_bias,
        grad_first_gain,
        grad_first_shift,
        grad_cross_query,
        grad_cross_query_bias,
        grad_cross_key,
        grad_cross_value,
        grad_cross_value_bias,
        grad_cross_output,
        grad_cross_output_bias,
        grad_second_gain,
        grad_second_shift,
        grad_ffn_in,
        grad_ffn_in_bias,
        grad_ffn_out,
        grad_ffn_out_bias,
        grad_third_gain,
        grad_third_shift,
    ]
    summed = (
        lax.psum_scatter(
            partial_grads[0].astype(jnp.bfloat16), "dp", scatter_dimension=0, tiled=True
        ).astype(jnp.float32),
        lax.psum_scatter(
            partial_grads[1].astype(jnp.bfloat16), "dp", scatter_dimension=0, tiled=True
        ).astype(jnp.float32),
        lax.psum_scatter(
            partial_grads[2].astype(jnp.bfloat16), "dp", scatter_dimension=0, tiled=True
        ).astype(jnp.float32),
        lax.psum_scatter(
            partial_grads[3].astype(jnp.bfloat16), "dp", scatter_dimension=0, tiled=True
        ).astype(jnp.float32),
        lax.psum_scatter(
            partial_grads[4].astype(jnp.bfloat16), "dp", scatter_dimension=0, tiled=True
        ).astype(jnp.float32),
        lax.psum_scatter(
            partial_grads[5].astype(jnp.bfloat16), "dp", scatter_dimension=0, tiled=True
        ).astype(jnp.float32),
        lax.psum_scatter(
            partial_grads[6].astype(jnp.bfloat16), "dp", scatter_dimension=0, tiled=True
        ).astype(jnp.float32),
        lax.psum_scatter(
            partial_grads[7].astype(jnp.bfloat16), "dp", scatter_dimension=0, tiled=True
        ).astype(jnp.float32),
        lax.psum_scatter(
            partial_grads[8].astype(jnp.bfloat16), "dp", scatter_dimension=0, tiled=True
        ).astype(jnp.float32),
        lax.psum_scatter(
            partial_grads[9].astype(jnp.bfloat16), "dp", scatter_dimension=0, tiled=True
        ).astype(jnp.float32),
        lax.psum_scatter(
            partial_grads[10].astype(jnp.bfloat16), "dp", scatter_dimension=0, tiled=True
        ).astype(jnp.float32),
        lax.psum_scatter(
            partial_grads[11].astype(jnp.bfloat16), "dp", scatter_dimension=0, tiled=True
        ).astype(jnp.float32),
        lax.psum_scatter(
            partial_grads[12].astype(jnp.bfloat16), "dp", scatter_dimension=0, tiled=True
        ).astype(jnp.float32),
        lax.psum_scatter(
            partial_grads[13].astype(jnp.bfloat16), "dp", scatter_dimension=0, tiled=True
        ).astype(jnp.float32),
        lax.psum_scatter(
            partial_grads[14].astype(jnp.bfloat16), "dp", scatter_dimension=0, tiled=True
        ).astype(jnp.float32),
        lax.psum_scatter(
            partial_grads[15].astype(jnp.bfloat16), "dp", scatter_dimension=0, tiled=True
        ).astype(jnp.float32),
        lax.psum_scatter(
            partial_grads[16].astype(jnp.bfloat16), "dp", scatter_dimension=0, tiled=True
        ).astype(jnp.float32),
        lax.psum_scatter(
            partial_grads[17].astype(jnp.bfloat16), "dp", scatter_dimension=0, tiled=True
        ).astype(jnp.float32),
        lax.psum_scatter(
            partial_grads[18].astype(jnp.bfloat16), "dp", scatter_dimension=0, tiled=True
        ).astype(jnp.float32),
        lax.psum_scatter(
            partial_grads[19].astype(jnp.bfloat16), "dp", scatter_dimension=0, tiled=True
        ).astype(jnp.float32),
        lax.psum_scatter(
            partial_grads[20].astype(jnp.bfloat16), "dp", scatter_dimension=0, tiled=True
        ).astype(jnp.float32),
        lax.psum_scatter(
            partial_grads[21].astype(jnp.bfloat16), "dp", scatter_dimension=0, tiled=True
        ).astype(jnp.float32),
        lax.psum_scatter(
            partial_grads[22].astype(jnp.bfloat16), "dp", scatter_dimension=0, tiled=True
        ).astype(jnp.float32),
        lax.psum_scatter(
            partial_grads[23].astype(jnp.bfloat16), "dp", scatter_dimension=0, tiled=True
        ).astype(jnp.float32),
    )
    finished = (
        lax.psum(summed[0].astype(jnp.bfloat16), "seq").astype(jnp.float32),
        lax.psum(summed[1].astype(jnp.bfloat16), "seq").astype(jnp.float32),
        lax.psum(summed[2].astype(jnp.bfloat16), "seq").astype(jnp.float32),
        lax.psum(summed[3].astype(jnp.bfloat16), "seq").astype(jnp.float32),
        lax.psum(summed[4].astype(jnp.bfloat16), "seq").astype(jnp.float32),
        lax.psum(summed[5].astype(jnp.bfloat16), "seq").astype(jnp.float32),
        lax.psum(summed[6].astype(jnp.bfloat16), "seq").astype(jnp.float32),
        lax.psum(summed[7].astype(jnp.bfloat16), "seq").astype(jnp.float32),
        lax.psum(summed[8].astype(jnp.bfloat16), "seq").astype(jnp.float32),
        lax.psum(summed[9].astype(jnp.bfloat16), "seq").astype(jnp.float32),
        lax.psum(summed[10].astype(jnp.bfloat16), "seq").astype(jnp.float32),
        lax.psum(summed[11].astype(jnp.bfloat16), "seq").astype(jnp.float32),
        lax.psum(summed[12].astype(jnp.bfloat16), "seq").astype(jnp.float32),
        lax.psum(summed[13].astype(jnp.bfloat16), "seq").astype(jnp.float32),
        lax.psum(summed[14].astype(jnp.bfloat16), "seq").astype(jnp.float32),
        lax.psum(summed[15].astype(jnp.bfloat16), "seq").astype(jnp.float32),
        lax.psum(summed[16].astype(jnp.bfloat16), "seq").astype(jnp.float32),
        lax.psum(summed[17].astype(jnp.bfloat16), "seq").astype(jnp.float32),
        lax.psum(summed[18].astype(jnp.bfloat16), "seq").astype(jnp.float32),
        lax.psum(summed[19].astype(jnp.bfloat16), "seq").astype(jnp.float32),
        lax.psum(summed[20].astype(jnp.bfloat16), "seq").astype(jnp.float32),
        lax.psum(summed[21].astype(jnp.bfloat16), "seq").astype(jnp.float32),
        lax.psum(summed[22].astype(jnp.bfloat16), "seq").astype(jnp.float32),
        lax.psum(summed[23].astype(jnp.bfloat16), "seq").astype(jnp.float32),
    )
    finished = list(finished)
    return (hidden_out, hidden_grad, memory_grad) + tuple(finished)


def nt(a, b):
    return lax.dot_general(a, b, (((1,), (1,)), ((), ())), preferred_element_type=F32)


def tn(a, b):
    return lax.dot_general(a, b, (((0,), (0,)), ((), ())), preferred_element_type=F32)


def mean(v):
    return jnp.mean(v, axis=-1, keepdims=True)


def norm_stats(v):
    center = v - mean(v)
    r = lax.rsqrt(mean(center * center) + 1e-05)
    return center * r, r


def norm_back(e, n, r, gain):
    u = e * gain
    return r * (u - mean(u) - n * mean(u * n))


def sums(v):
    return jnp.sum(v, axis=0, keepdims=True)


TAIL = (0.24251982196758853, 0.24429374300098905, 0.2054730204591465, 0.24507896666845616,
        -0.08230106829392796, 0.3798837300580386, -0.30809352249830146, 0.07314529579847638)


def gelu_pair(x):
    d = 1.0 + (0.43 * math.sqrt(0.5)) * jnp.abs(x)
    t = pl.reciprocal(d, approx=True)
    t = t * (2.0 - d * t)
    tail = 0.5 * TAIL[-1]
    for c in TAIL[-2::-1]:
        tail = tail * t + 0.5 * c
    bell = jnp.exp(-0.5 * x * x)
    tail = tail * t * bell
    phi = jnp.where(x >= 0, 1.0 - tail, tail)
    return x * phi, phi + x * bell * (1.0 / math.sqrt(2.0 * math.pi))


def full(shape):
    return pl.BlockSpec(shape, lambda *_: (0,) * len(shape), pipeline_mode=pl.Buffered(1))


def still(shape):
    return pl.BlockSpec(shape, lambda *_: (0,) * len(shape))


def rows_of(bt, width):
    return pl.BlockSpec((bt, width), lambda i: (i, 0))


class Order:
    def __init__(self):
        self.last = []

    def call(self, kernel, *args, name, us, grid, in_specs, out_specs, out_shape, scalars=0, scratch_shapes=(), moves=()):
        at, after, n, n_out = len(args), len(self.last), len(moves), len(out_specs)
        flat = [array for pair in moves for array in pair]
        hbm = pl.BlockSpec(memory_space=pl.ANY)

        def run(*refs):
            outs = at + 2 * n + after
            plain = refs[:at] + refs[outs : outs + n_out]
            if not n:
                return kernel(*plain, *refs[outs + n_out :])
            s = refs[0][4]
            buffer, sem = refs[-2:]
            reads, writes = [], []
            for i in range(n):
                target = refs[outs + n_out + i]
                for j, place in enumerate((s, 1 - s)):
                    slot = 2 * i + j
                    reads.append(pltpu.make_async_copy(refs[at + slot], buffer.at[slot], sem.at[0, slot]))
                    writes.append(pltpu.make_async_copy(buffer.at[slot], target.at[place], sem.at[1, slot]))

            @pl.when(pl.program_id(0) == 0)
            def _():
                for c in reads:
                    c.start()

            @pl.when(pl.program_id(0) == 1)
            def _():
                for r, w in zip(reads, writes):
                    r.wait()
                    w.start()

            kernel(*plain, *refs[outs + n_out + n : -2])

            @pl.when(pl.program_id(0) == grid[0] - 1)
            def _():
                for c in writes:
                    c.wait()

        more = [pltpu.VMEM((2 * n, *flat[0].shape), BF), pltpu.SemaphoreType.DMA((2, 2 * n))] if n else []
        out = pl.pallas_call(
            run, name=name, out_shape=list(out_shape) + [shaped(2, *pair[0].shape) for pair in moves],
            grid_spec=pltpu.PrefetchScalarGridSpec(
                num_scalar_prefetch=scalars, grid=grid, in_specs=list(in_specs) + [hbm] * (2 * n + after),
                out_specs=list(out_specs) + [hbm] * n, scratch_shapes=list(scratch_shapes) + more),
            cost_estimate=pl.CostEstimate(flops=0, bytes_accessed=int(us * 7.2e6), transcendentals=0),
            compiler_params=pltpu.CompilerParams(vmem_limit_bytes=127 * 2**19),
        )(*args, *flat, *self.last)
        self.last = [out[n_out - 1]]
        return out


def shaped(*shape, dtype=BF):
    return jax.ShapeDtypeStruct(shape, dtype)


(V_QB, V_VB, V_OB, V_G1, V_B1, V_CQB, V_CVB, V_COB, V_G2, V_B2, V_FOB, V_G3, V_B3) = range(13)


def mask_of(ids, ref):
    row = lax.broadcasted_iota(jnp.int32, (128, ids.shape[1]), 0) % 64
    ref[...] = jnp.where(row < 4, jnp.where(row == ids, 0.0, BIG), jnp.where(row < 7, -1.0, 0.0)).T.astype(BF)


def one_hot(ids, ref):
    row = lax.broadcasted_iota(jnp.int32, (64, ids.shape[1]), 0)
    ref[...] = jnp.where(row == ids, 1.0, 0.0).astype(BF)


def near_kernel(spot_ref, seg_ref, x_ref, y_ref, far_ref, grad_ref, vec_ref, wq_ref, wk_ref, wv_ref, uk_ref, uv_ref,
                q_ref, k_ref, v_ref, mk_ref, mv_ref, far_out, grad_out, mix_ref, stat_ref, q_s, k_s, v_s, oh_s, mask_s):
    at = pl.program_id(0)

    @pl.when(at == 0)
    def _():
        far_out[...] = far_ref[0]
        grad_out[...] = grad_ref[0]
        ids = seg_ref[pl.ds(spot_ref[4], 1), :]
        one_hot(ids, oh_s)
        mask_of(ids, mask_s)
        x, y = x_ref[0], y_ref[0]
        q_s[...] = (dot(x, wq_ref[...]) + vec_ref[V_QB : V_QB + 1, :]).astype(BF)
        k_s[...] = dot(x, wk_ref[...]).astype(BF)
        v_s[...] = (dot(x, wv_ref[...]) + vec_ref[V_VB : V_VB + 1, :]).astype(BF)
        mk_ref[...] = dot(y, uk_ref[...]).astype(BF)
        mv_ref[...] = (dot(y, uv_ref[...]) + vec_ref[V_CVB : V_CVB + 1, :]).astype(BF)
        q_ref[...], k_ref[...], v_ref[...] = q_s[...], k_s[...], v_s[...]

    @pl.when(at > 0)
    def _():
        cols = columns(at - 1)
        for h, (o, m, l) in enumerate(attend_near(q_s[:, cols], k_s[:, cols], v_s[:, cols], oh_s[...], mask_s[...])):
            mix_ref[64 * h : 64 * h + 64, :] = o
            stat_ref[0, h : h + 1, :] = m
            stat_ref[0, 2 + h : 3 + h, :] = l


def project_near(order, spots, tgt, hidden_in, memory, out_grad, vec, weights):
    half, D = hidden_in.shape[1:]
    pairs = D // 128
    x = pl.BlockSpec((1, half, D), lambda i, p: (p[4], 0, 0))
    other = pl.BlockSpec((1, half, D), lambda i, p: (1 - p[4], 0, 0))
    pair = lambda i: jnp.maximum(i - 1, 0)
    big = pltpu.VMEM((half, D), BF)
    return order.call(
        near_kernel, spots, tgt, hidden_in, memory, memory, out_grad, vec, *weights, scalars=1, name="project_near", us=14,
        grid=(1 + pairs,), in_specs=[full(tgt.shape), x, x, other, other, full(vec.shape)] + [full((D, D))] * 5,
        out_specs=[still((half, D))] * 7 + [pl.BlockSpec((128, half), lambda i, p: (pair(i), 0)),
                                            pl.BlockSpec((1, 8, half), lambda i, p: (pair(i), 0, 0))],
        out_shape=[shaped(half, D)] * 7 + [shaped(D, half, dtype=F32), shaped(pairs, 8, half, dtype=F32)],
        scratch_shapes=[big] * 3 + [pltpu.VMEM((64, half), BF), pltpu.VMEM((half, 128), BF)])


class Loads:
    def __init__(self, sem):
        self.sem = sem
        self.copies = []

    def add(self, src, dst):
        self.copies.append(pltpu.make_async_copy(src, dst, self.sem.at[len(self.copies)]))
        return self.copies[-1]


def columns(p, width=128):
    return pl.ds(pl.multiple_of(p * width, width), width)


def self_kernel(spot_ref, vec_ref, seg_ref, mix_ref, stat_ref, hin_ref, hgot_ref, qn_ref, kn_ref, vn_ref, wq_ref, wk_ref, wv_ref, wo_ref, wc_ref,
                l_ref, n_ref, r_ref, low_ref, cq_ref, oh_ref, mk_ref, cross_mk_ref, h_out, q_out, k_out, v_out, m_out,
                h_s, q_s, k_s, v_s, m_s, wq_s, wk_s, wv_s, wo_s, wc_s, sem, *, pairs):
    v = lambda i: vec_ref[i : i + 1, :]
    at = pl.program_id(0)
    half = hgot_ref.shape[0]
    s = spot_ref[4]
    near = pl.ds(pl.multiple_of(s * half, half), half)
    far = pl.ds(pl.multiple_of((1 - s) * half, half), half)
    loads = Loads(sem)
    got = loads.add(hgot_ref, h_s.at[far])
    in_q, in_k, in_v = loads.add(wq_ref, wq_s), loads.add(wk_ref, wk_s), loads.add(wv_ref, wv_s)
    own = [loads.add(hin_ref.at[s], h_s.at[near])]
    own += [loads.add(a, b.at[near]) for a, b in ((qn_ref, q_s), (kn_ref, k_s), (vn_ref, v_s))]
    later = [loads.add(wo_ref, wo_s), loads.add(wc_ref, wc_s)]
    outs = [loads.add(a, b) for a, b in ((h_s, h_out), (q_s, q_out), (k_s, k_out), (v_s, v_out))]
    mixed_out = loads.add(m_s, m_out)

    @pl.when(at == 0)
    def _():
        for c in (got, in_q, in_k, in_v, *own, *later):
            c.start()
        one_hot(seg_ref[0:1, :], oh_ref)
        mask_of(seg_ref[0:1, :], mk_ref)
        mask_of(seg_ref[1:2, :], cross_mk_ref)
        got.wait()
        x = h_s[far, :]
        in_q.wait()
        q_s[far, :] = (dot(x, wq_s[...]) + v(V_QB)).astype(BF)
        in_k.wait()
        k_s[far, :] = dot(x, wk_s[...]).astype(BF)
        in_v.wait()
        v_s[far, :] = (dot(x, wv_s[...]) + v(V_VB)).astype(BF)
        for c in own:
            c.wait()
        for c in outs:
            c.start()

    @pl.when((at > 0) & (at <= pairs))
    def _():
        cols = columns(at - 1)

        args = lambda q, k: (q_s[q, cols], k_s[k, cols], v_s[k, cols], oh_ref[:, q], mk_ref[k, :])
        lo, hi = pl.ds(0, half), pl.ds(half, half)
        near_sums = [(mix_ref[64 * h : 64 * h + 64, :], stat_ref[0, h : h + 1, :], stat_ref[0, 2 + h : 3 + h, :]) for h in (0, 1)]
        heads = attend_rest(s == 0, near_sums, args(far, far), args(hi, lo))
        for i, rows in enumerate((lo, hi)):
            for h in (0, 1):
                l_ref[0, h : h + 1, rows] = heads[h][i][1]
            m_s[rows, cols] = jnp.concatenate([heads[h][i][0] for h in (0, 1)], 0).T.astype(BF)

    @pl.when(at == pairs + 1)
    def _():
        mixed_out.start()
        for c in later:
            c.wait()

    @pl.when(at > pairs)
    def _():
        rows = pl.ds(pl.multiple_of((at - pairs - 1) * half, half), half)
        x = h_s[rows, :].astype(F32) + (dot(m_s[rows, :], wo_s[...]) + v(V_OB))
        n, r = norm_stats(x)
        n_ref[...] = n
        r_ref[...] = r
        low = (n * v(V_G1) + v(V_B1)).astype(BF)
        low_ref[...] = low
        cq_ref[...] = (dot(low, wc_s[...]) + v(V_CQB)).astype(BF)

    @pl.when(at == pairs + 2)
    def _():
        for c in (*outs, mixed_out):
            c.wait()


def self_forward(order, spots, vec, segs, near_mix, near_stats, hidden_in, hidden_got, near, weights):
    half, D = hidden_got.shape
    T, pairs = 2 * half, D // 128
    token = lambda width: pl.BlockSpec((half, width), lambda i, p: (jnp.maximum(i - pairs - 1, 0), 0))
    hbm = pl.BlockSpec(memory_space=pl.ANY)
    masks = [(64, T), (T, 128), (T, 128)]
    pair = lambda i: jnp.clip(i - 1, 0, pairs - 1)
    return order.call(
        functools.partial(self_kernel, pairs=pairs), spots, vec, segs, near_mix, near_stats, hidden_in, hidden_got, *near, *weights,
        scalars=1, name="self_forward", us=25, grid=(pairs + 3,),
        in_specs=[full(vec.shape), full(segs.shape), pl.BlockSpec((128, half), lambda i, p: (pair(i), 0)),
                  pl.BlockSpec((1, 8, half), lambda i, p: (pair(i), 0, 0))] + [hbm] * 10,
        out_specs=[pl.BlockSpec((1, 8, T), lambda i, p: (pair(i), 0, 0)),
                   token(D), token(1), token(D), token(D)] + [still(s) for s in masks] + [hbm] * 5,
        out_shape=[shaped(pairs, 8, T, dtype=F32), shaped(T, D, dtype=F32), shaped(T, 1, dtype=F32), shaped(T, D), shaped(T, D)]
        + [shaped(*s) for s in masks] + [shaped(T, D)] * 5,
        scratch_shapes=[pltpu.VMEM((T, D), BF)] * 5 + [pltpu.VMEM((D, D), BF)] * 5 + [pltpu.SemaphoreType.DMA((15,))])


def cross_kernel(spot_ref, vec_ref, oh_ref, mask_ref, cq_ref, min_ref, mgot_ref, kn_ref, vn_ref, uk_ref, uv_ref,
                 l_ref, m_out, k_out, v_out, c_out, m_s, k_s, v_s, q_s, c_s, uk_s, uv_s, sem, *, pairs, bq):
    at = pl.program_id(0)
    half = mgot_ref.shape[0]
    s = spot_ref[4]
    near = pl.ds(pl.multiple_of(s * half, half), half)
    far = pl.ds(pl.multiple_of((1 - s) * half, half), half)
    loads = Loads(sem)
    got = loads.add(mgot_ref, m_s.at[far])
    in_k, in_v = loads.add(uk_ref, uk_s), loads.add(uv_ref, uv_s)
    own = [loads.add(min_ref.at[s], m_s.at[near]), loads.add(cq_ref, q_s)]
    own += [loads.add(kn_ref, k_s.at[near]), loads.add(vn_ref, v_s.at[near])]
    outs = [loads.add(a, b) for a, b in ((m_s, m_out), (k_s, k_out), (v_s, v_out))]

    @pl.when(at == 0)
    def _():
        for c in (got, in_k, in_v, *own):
            c.start()
        got.wait()
        x = m_s[far, :]
        in_k.wait()
        k_s[far, :] = dot(x, uk_s[...]).astype(BF)
        in_v.wait()
        v_s[far, :] = (dot(x, uv_s[...]) + vec_ref[V_CVB : V_CVB + 1, :]).astype(BF)
        for c in own:
            c.wait()
        for c in outs:
            c.start()

    @pl.when(at > 0)
    def _():
        cols = columns(at - 1)

        def put_total(h, i, row):
            l_ref[0, h : h + 1, i * bq : (i + 1) * bq] = row

        blocks = attend_pair(q_s[:, cols], k_s[:, cols], v_s[:, cols], oh_ref[...], mask_ref[...], put_total, bq)
        for i, b in enumerate(blocks):
            c_out[i * bq : (i + 1) * bq, :] = b

    @pl.when(at == pairs)
    def _():
        for c in outs:
            c.wait()


def cross_forward(order, spots, vec, oh, mask, cq, memory, memory_got, near, weights):
    half, D = memory_got.shape
    T, pairs = 2 * half, D // 128
    hbm = pl.BlockSpec(memory_space=pl.ANY)
    pair = lambda i: jnp.maximum(i - 1, 0)
    return order.call(
        functools.partial(cross_kernel, pairs=pairs, bq=512), spots, vec, oh, mask, cq, memory, memory_got, *near, *weights,
        scalars=1, name="cross_forward", us=23, grid=(pairs + 1,),
        in_specs=[full(a.shape) for a in (vec, oh, mask)] + [hbm] * 7,
        out_specs=[pl.BlockSpec((1, 8, T), lambda i, p: (pair(i), 0, 0))] + [hbm] * 3
        + [pl.BlockSpec((T, 128), lambda i, p: (0, pair(i)))],
        out_shape=[shaped(pairs, 8, T, dtype=F32)] + [shaped(T, D)] * 4,
        scratch_shapes=[pltpu.VMEM((T, D), BF)] * 4 + [pltpu.VMEM((16, 128), BF)] + [pltpu.VMEM((D, D), BF)] * 2
        + [pltpu.SemaphoreType.DMA((10,))])


def ffn_kernel(spot_ref, vec_ref, bin_ref, n1_ref, cm_ref, og_ref, oggot_ref, wco_ref, win_ref, wout_ref,
               own_ref, other_ref, sb_ref, cmb_ref, vo_ref, vi_ref, all_ref,
               act_s, ib_s, cm_s, og_s, wco_s, win_s, wout_s, fb_s, low_s, cb_s, stage_s, stage_sem, sem, *, parts):
    v = lambda i: vec_ref[i : i + 1, :]
    t = pl.program_id(0)
    half, D = oggot_ref.shape
    s = spot_ref[4]
    loads = Loads(sem)
    in_cm, in_co = loads.add(cm_ref, cm_s), loads.add(wco_ref, wco_s)
    in_up, in_down = loads.add(win_ref, win_s), loads.add(wout_ref, wout_s)
    in_og = [loads.add(og_ref.at[s], og_s.at[s]), loads.add(oggot_ref, og_s.at[1 - s])]

    def need(*copies):
        @pl.when(t == 0)
        def _():
            for c in copies:
                c.wait()

    @pl.when(t == 0)
    def _():
        for c in loads.copies:
            c.start()
        vo_ref[...] = jnp.zeros_like(vo_ref)
        vi_ref[...] = jnp.zeros_like(vi_ref)

    @pl.when(t < 2)
    def _():
        need(in_cm, in_co)
        rows = pl.ds(pl.multiple_of(t * half, half), half)
        first = n1_ref[...] * v(V_G1) + v(V_B1)
        n2, r2 = norm_stats(first + (dot(cm_s[rows, :], wco_s[...]) + v(V_COB)))
        second = n2 * v(V_G2) + v(V_B2)
        low = second.astype(BF)
        low_s[rows, :] = low
        need(in_up, in_down, *in_og)
        width = win_s.shape[1] // parts
        branch = None
        up = lambda c: dot(low, win_s[:, c * width : (c + 1) * width]) + bin_ref[:, c * width : (c + 1) * width]
        x = up(0)
        late = None
        for c in range(parts):
            cols = slice(c * width, (c + 1) * width)
            coming = up(c + 1) if c + 1 < parts else None
            act, slope = gelu_pair(x)
            ib_s[rows, cols] = slope.astype(BF)
            act = act.astype(BF)
            act_s[rows, cols] = act
            if late is not None:
                term = dot(late[1], wout_s[late[0], :])
                branch = term if branch is None else branch + term
            late = cols, act
            x = coming
        term = dot(late[1], wout_s[late[0], :])
        branch = term if branch is None else branch + term
        n3, r3 = norm_stats(second + (branch + v(V_FOB)))
        ho = (n3 * v(V_G3) + v(V_B3)).astype(BF)

        @pl.when(t == s)
        def _():
            own_ref[...] = ho

        @pl.when(t != s)
        def _():
            other_ref[...] = ho

        e = og_s[t].astype(F32)
        third = norm_back(e, n3, r3, v(V_G3))
        fb = third.astype(BF)
        fb_s[rows, :] = fb
        vo_ref[0:1, :] += sums(e * n3)
        vo_ref[1:2, :] += sums(e)
        vo_ref[2:3, :] += sums(fb.astype(F32))
        e = third
        up = lambda c: nt(fb, wout_s[c * width : (c + 1) * width, :])
        x = up(0)
        late = None
        for c in range(parts):
            cols = slice(c * width, (c + 1) * width)
            coming = up(c + 1) if c + 1 < parts else None
            ib = (x * ib_s[rows, cols].astype(F32)).astype(BF)
            ib_s[rows, cols] = ib
            vi_ref[:, cols] += sums(ib.astype(F32))
            if late is not None:
                e = e + nt(late[1], win_s[:, late[0]])
            late = cols, ib
            x = coming
        e = e + nt(late[1], win_s[:, late[0]])
        back = norm_back(e, n2, r2, v(V_G2))
        sb_ref[...] = back
        cb = back.astype(BF)
        cb_s[rows, :] = cb
        vo_ref[3:4, :] += sums(e * n2)
        vo_ref[4:5, :] += sums(e)
        vo_ref[5:6, :] += sums(cb.astype(F32))
        cmb_ref[...] = nt(cb, wco_s[...]).astype(BF)

    t = t - 2
    slot = t % 2

    def tall(b, slot):
        return pltpu.make_async_copy(stage_s.at[slot], all_ref.at[b, :, pl.ds(0, 4)], stage_sem.at[slot])

    def flat(b, slot):
        return pltpu.make_async_copy(stage_s.at[slot], all_ref.at[:, :, 4 + b], stage_sem.at[slot])

    @pl.when((t >= 2) & (t < 6))
    def _():
        tall(t - 2, slot).wait()

    @pl.when(t >= 6)
    def _():
        flat(t - 6, slot).wait()

    def put(x, g):
        stage_s[slot] = tn(x, g).astype(BF).reshape(4, 4, 48, D)

    @pl.when((t >= 0) & (t < 4))
    def _():
        put(act_s[:, columns(t, D)], fb_s[...])
        tall(t, slot).start()

    @pl.when((t >= 4) & (t < 8))
    def _():
        put(low_s[...], ib_s[:, columns(t - 4, D)])
        flat(t - 4, slot).start()

    @pl.when(t == 8)
    def _():
        put(cm_s[...], cb_s[...])
        flat(4, 0).start()
        flat(3, 1).wait()
        flat(4, 0).wait()


def ffn_both(order, spots, vec, bin_, n1, cm, out_grad, out_grad_got, weights):
    half, D = out_grad_got.shape
    T, FF = 2 * half, bin_.shape[1]
    token = lambda width: pl.BlockSpec((half, width), lambda i, p: (jnp.minimum(i, 1), 0))
    hbm = pl.BlockSpec(memory_space=pl.ANY)
    big = lambda *shape: pltpu.VMEM(shape, BF)
    return order.call(
        functools.partial(ffn_kernel, parts=6), spots, vec, bin_, n1, cm, out_grad, out_grad_got, *weights,
        scalars=1, name="ffn_both", us=60, grid=(11,),
        in_specs=[full(vec.shape), full(bin_.shape), token(D)] + [hbm] * 6,
        out_specs=[still((half, D)), still((half, D)), token(D), token(D), still((8, D)), still((1, FF)), hbm],
        out_shape=[shaped(half, D), shaped(half, D), shaped(T, D, dtype=F32), shaped(T, D),
                   shaped(8, D, dtype=F32), shaped(1, FF, dtype=F32), shaped(4, 4, 9, 48, D)],
        scratch_shapes=[big(T, FF), big(T, FF), big(T, D), big(2, half, D), big(D, D), big(D, FF), big(FF, D), big(T, D), big(T, D),
                        big(T, D), big(2, 4, 4, 48, D), pltpu.SemaphoreType.DMA((2,)), pltpu.SemaphoreType.DMA((6,))])


def cross_back_kernel(spot_ref, q_ref, k_ref, v_ref, do_ref, o_ref, l_ref, oh_ref, mask_ref, wk_in, wv_in,
                      dq_ref, dk_ref, dv_ref, own_ref, other_ref, acc_s, dk_s, dv_s, wk_s, wv_s, sem, *, pairs, bk):
    at = pl.program_id(0)
    half = own_ref.shape[0]
    loads = Loads(sem)
    loads.add(wk_in, wk_s), loads.add(wv_in, wv_s)

    @pl.when(at == 0)
    def _():
        for c in loads.copies:
            c.start()

    @pl.when(at < pairs)
    def _():
        out = {"q": dq_ref, "k": dk_ref, "v": dv_ref}

        def put(name, rows, block):
            out[name][rows, :] = block
            if name != "q":
                {"k": dk_s, "v": dv_s}[name][rows, columns(at)] = block

        attend_pair_back(q_ref[...], k_ref[...], v_ref[...], do_ref[...], o_ref[...], [l_ref[0, h : h + 1, :] for h in (0, 1)],
                         oh_ref[...], mask_ref[...], acc_s, put, bk, False)

    @pl.when(at == pairs)
    def _():
        for c in loads.copies:
            c.wait()

    t = at - pairs

    @pl.when(t >= 0)
    def _():
        rows = pl.ds(pl.multiple_of(t * half, half), half)
        mg = (nt(dk_s[rows, :], wk_s[...]) + nt(dv_s[rows, :], wv_s[...])).astype(BF)

        @pl.when(t == spot_ref[4])
        def _():
            own_ref[...] = mg

        @pl.when(t != spot_ref[4])
        def _():
            other_ref[...] = mg


def cross_back(order, spots, q, k, v, do, o, totals, oh, mask, weights):
    T, D = q.shape
    pairs, half = D // 128, T // 2
    p_in = lambda i: jnp.minimum(i, pairs - 1)
    pair = pl.BlockSpec((T, 128), lambda i, p: (0, p_in(i)))
    hbm = pl.BlockSpec(memory_space=pl.ANY)
    return order.call(
        functools.partial(cross_back_kernel, pairs=pairs, bk=512), spots, q, k, v, do, o, totals, oh, mask, *weights,
        scalars=1, name="cross_back", us=38, grid=(pairs + 2,),
        in_specs=[pair] * 5 + [pl.BlockSpec((1, 8, T), lambda i, p: (p_in(i), 0, 0)), full(oh.shape), full(mask.shape), hbm, hbm],
        out_specs=[pair] * 3 + [still((half, D))] * 2, out_shape=[shaped(T, D)] * 3 + [shaped(half, D)] * 2,
        scratch_shapes=[pltpu.VMEM((128, T), F32)] + [pltpu.VMEM((T, D), BF)] * 2 + [pltpu.VMEM((D, D), BF)] * 2
        + [pltpu.SemaphoreType.DMA((2,))])


def middle_kernel(spot_ref, vec_ref, q_ref, n_ref, r_ref, sb_ref,
                  k_in, v_in, low_in, src_in, mix_in, wq_in, wo_in,
                  fb_ref, mb_ref, vo_ref, send_ref, keep_ref,
                  dq_s, dk_s, dv_s, back_s, low_s, src_s, mix_s, wq_s, wo_s, sem):
    v = lambda i: vec_ref[i : i + 1, :]
    t = pl.program_id(0)
    half, D = mb_ref.shape
    loads = Loads(sem)
    first = [loads.add(wq_in, wq_s), loads.add(wo_in, wo_s)]
    last = [loads.add(a, b) for a, b in ((low_in, low_s), (src_in, src_s), (mix_in, mix_s), (k_in, dk_s), (v_in, dv_s))]

    @pl.when(t == 0)
    def _():
        for c in loads.copies:
            c.start()
        vo_ref[...] = jnp.zeros_like(vo_ref)
        for c in first:
            c.wait()

    @pl.when(t < 2)
    def _():
        rows = pl.ds(pl.multiple_of(t * half, half), half)
        dq = q_ref[...]
        dq_s[rows, :] = dq
        n = n_ref[...]
        e = sb_ref[...] + nt(dq, wq_s[...])
        back = norm_back(e, n, r_ref[...], v(V_G1))
        fb_ref[...] = back
        low = back.astype(BF)
        back_s[rows, :] = low
        vo_ref[0:1, :] += sums(e * n)
        vo_ref[1:2, :] += sums(e)
        vo_ref[2:3, :] += sums(low.astype(F32))
        vo_ref[3:4, :] += sums(dq.astype(F32))
        mb_ref[...] = nt(low, wo_s[...]).astype(BF)

    @pl.when(t == 2)
    def _():
        for c in last:
            c.wait()
        vo_ref[4:5, :] = sums(dv_s[...].astype(F32))

    for i, (x, g) in enumerate(((low_s, dq_s), (src_s, dk_s), (src_s, dv_s), (mix_s, back_s))):
        @pl.when(t == 2 + i)
        def _():
            total = tn(x[...], g[...]).astype(BF)
            def put_piece(which, x, zl, zh, rows):
                for k in range(2):
                    (send_ref, keep_ref)[which][at_of(PLACES, x=x, y=k, zl=zl, zh=zh) + (0,)] = rows[:, D // 2 * k : D // 2 * (k + 1)]

            place_rows(spot_ref[0], total, 48, put_piece)


def middle(order, spots, vec, dq, dk, dv, n1, r1, sb, low, source, mixed, weights):
    T, D = n1.shape
    half = T // 2
    token = lambda width: pl.BlockSpec((half, width), lambda i, p: (jnp.minimum(i, 1), 0))
    out = pl.BlockSpec((2, 2, 2, 2, 1, 48, D // 2), lambda i, p: (0, 0, 0, 0, jnp.maximum(i - 2, 0), 0, 0))
    hbm = pl.BlockSpec(memory_space=pl.ANY)
    square, rect = pltpu.VMEM((D, D), BF), pltpu.VMEM((T, D), BF)
    return order.call(
        middle_kernel, spots, vec, dq, n1, r1, sb, dk, dv, low, source, mixed, *weights, scalars=1, name="middle", us=18,
        grid=(6,),
        in_specs=[full(vec.shape)] + [token(D), token(D), token(1), token(D)] + [hbm] * 7,
        out_specs=[token(D), token(D), still((8, D)), out, out],
        out_shape=[shaped(T, D, dtype=F32), shaped(T, D), shaped(8, D, dtype=F32)]
        + [shaped(2, 2, 2, 2, 4, 48, D // 2)] * 2,
        scratch_shapes=[rect] * 7 + [square] * 2 + [pltpu.SemaphoreType.DMA((7,))])


def back_kernel(spot_ref, *refs, n, plain):
    own_ref, other_ref = refs[-2:]
    total = refs[2 * n][...] if plain else None
    for g, w in zip(refs[:n], refs[n : 2 * n]):
        term = nt(g[...], w[...])
        total = term if total is None else total + term
    total = total.astype(BF)

    @pl.when(pl.program_id(0) == spot_ref[4])
    def _():
        own_ref[...] = total

    @pl.when(pl.program_id(0) != spot_ref[4])
    def _():
        other_ref[...] = total


def back_rows(order, spots, grads, weights, plain=None):
    T, D = grads[0].shape
    half, n = T // 2, len(grads)
    more = [] if plain is None else [plain]
    r = pl.BlockSpec((half, D), lambda i, p: (i, 0))
    return order.call(
        functools.partial(back_kernel, n=n, plain=plain is not None), spots, *grads, *weights, *more,
        scalars=1, name="back_rows", us=9, grid=(2,), in_specs=[r] * n + [full((D, D))] * n + [r] * len(more),
        out_specs=[still((half, D))] * 2, out_shape=[shaped(half, D)] * 2)


def place_rows(core, total, height, put):
    for j in range(total.shape[0] // (2 * height)):
        even = total[2 * j * height : (2 * j + 1) * height]
        odd = total[(2 * j + 1) * height : (2 * j + 2) * height]
        put(1, j % 2, (j // 2) % 2, j // 4, jnp.where(core == 0, even, odd))
        put(0, j % 2, (j // 2) % 2, j // 4, jnp.where(core == 0, odd, even))


PLACES = "y", "zl", "x", "zh"
GROUP_LINKS = *PLACES, "gather"


def at_of(order, **place):
    return tuple(place[name] for name in order)


def self_back_kernel(spot_ref, q_ref, k_ref, v_ref, do_ref, o_ref, l_ref, oh_ref, mk_ref, vf_ref, v1_ref, vi_ref, h_in,
                     dq_ref, dk_ref, dv_ref, send_ref, keep_ref, acc_s, g_s, h_s, sem, *, pairs, bk):
    at = pl.program_id(0)
    hidden = pltpu.make_async_copy(h_in, h_s, sem)
    D = 128 * pairs
    wide = D // 2

    @pl.when(at == 0)
    def _():
        hidden.start()

    @pl.when(at < pairs)
    def _():
        out = {"q": (dq_ref, 0), "k": (dk_ref, 1), "v": (dv_ref, 2)}

        def put(name, rows, block):
            ref, i = out[name]
            ref[rows, :] = block
            g_s[i, rows, columns(at)] = block

        attend_pair_back(q_ref[...], k_ref[...], v_ref[...], do_ref[...], o_ref[...], [l_ref[0, h : h + 1, :] for h in (0, 1)],
                         oh_ref[...], mk_ref[...], acc_s, put, bk, True)

    core = spot_ref[0]
    height = 3 * 48 + 16

    def at_row(x, y, zl, zh):
        place = {"x": x, "y": y, "zl": zl, "zh": zh}
        row = 0
        for name in PLACES:
            row = 2 * row + place[name]
        return height * row

    for i in range(3):
        @pl.when(at == pairs + i)
        def _():
            if i == 0:
                hidden.wait()

            def put_piece(which, x, zl, zh, rows):
                for k in range(2):
                    row = at_row(x, k, zl, zh) + 48 * i
                    (send_ref, keep_ref)[which][row : row + 48, :] = rows[:, wide * k : wide * (k + 1)]

            place_rows(core, tn(h_s[...], g_s[i]).astype(BF), 48, put_piece)

    @pl.when(at == pairs + 2)
    def _():
        row_of = lambda i: sums(g_s[i].astype(F32))
        rows = jnp.concatenate([vf_ref[0:6, :], v1_ref[0:5, :], row_of(0), row_of(2), jnp.zeros((3, D), F32)], 0)
        spread = jnp.broadcast_to(vi_ref[...], (16, vi_ref.shape[1]))
        for first, part, w in ((0, rows, 48), (128, spread, 192)):
            for j in range(8):
                even = part[:, 2 * j * w : (2 * j + 1) * w].astype(BF)
                odd = part[:, (2 * j + 1) * w : (2 * j + 2) * w].astype(BF)
                row = at_row(j % 2, 0, (j // 2) % 2, j // 4) + 144
                keep_ref[row : row + 16, first : first + w] = jnp.where(core == 0, even, odd)
                send_ref[row : row + 16, first : first + w] = jnp.where(core == 0, odd, even)


def self_back(order, spots, q, k, v, do, o, totals, oh, mk, vectors, hidden, moves):
    T, D = q.shape
    pairs = D // 128
    p_in = lambda i: jnp.minimum(i, pairs - 1)
    pair = pl.BlockSpec((T, 128), lambda i, p: (0, p_in(i)))
    rows = 16 * (3 * 48 + 16)
    return order.call(
        functools.partial(self_back_kernel, pairs=pairs, bk=256), spots, q, k, v, do, o, totals, oh, mk, *vectors, hidden,
        scalars=1, name="self_back", us=30, grid=(pairs + 3,), moves=moves,
        in_specs=[pair] * 5 + [pl.BlockSpec((1, 8, T), lambda i, p: (p_in(i), 0, 0))]
        + [full(a.shape) for a in (oh, mk, *vectors)] + [pl.BlockSpec(memory_space=pl.ANY)],
        out_specs=[pair] * 3 + [still((rows, D // 2))] * 2, out_shape=[shaped(T, D)] * 3 + [shaped(rows, D // 2)] * 2,
        scratch_shapes=[pltpu.VMEM((128, T), F32), pltpu.VMEM((3, T, D), BF), pltpu.VMEM((T, D), BF), pltpu.SemaphoreType.DMA])


def fold_kernel(spot_ref, keep_ref, keep_other_ref, got_ref, got_other_ref, sum_ref, send_ref):
    sum_ref[...] = keep_ref[0] + got_ref[0]
    send_ref[...] = keep_other_ref[0] + got_other_ref[0]


def small_fold_kernel(spot_ref, *refs, items, keeps, gots):
    keep_refs, got_refs, outs = refs[:keeps], refs[keeps : keeps + gots], refs[keeps + gots :]
    for i, (came, spots, messages) in enumerate(items):
        keep, out = keep_refs[i], outs[i]
        rows = out.shape[0]

        def piece(p):
            part = lambda first: pl.ds(pl.multiple_of(first + p * rows, 16), rows)
            total = keep[part(0), :]
            for g, at in came:
                total = total + got_refs[g][part(at), :]
            return total

        mine = 0
        for s in spots:
            mine = 2 * mine + spot_ref[s]
        out[...] = piece(mine)
        for n, (m, first) in enumerate(messages):
            outs[keeps + m][first : first + rows, :] = out[...] if not spots else piece(mine ^ (n + 1))


LINKS = {"core": ([("dp", 1, 16)], (0,)), "x": ([("dp", 2, 16)], (1,)), "zl": ([("dp", 4, 16)], (2,)), "zh": ([("dp", 8, 16)], (3,)),
         "z": ([("dp", 8, 16), ("dp", 4, 16), ("dp", 12, 16)], (2, 3)), "y": ([("seq", 1, 2)], (4,)),
         "sum": ([("seq", 1, 2)], ()), "gather": ([("seq", 1, 2)], ())}


class Sum:
    def __init__(self, keep, got, *links):
        self.keep, self.gots = keep, [(got, 0)]
        self.links, self.step = links, 0

    def link(self):
        return self.links[self.step] if self.step < len(self.links) else None


def first_swap(send, keep, after=None):
    if after is not None:
        send, _ = lax.optimization_barrier((send, after))
    flat = lambda a: a.reshape(-1, a.shape[-1])
    return flat(keep), swap(flat(send), *LINKS["core"][0][0])


def advance(order, spots, *groups):
    groups = [g for g in groups if g.link() is not None]
    links = [LINKS[g.link()] for g in groups]
    rows = [g.keep.shape[0] >> len(places) for g, (_, places) in zip(groups, links)]
    if len(groups) == 1 and len(links[0][1]) == 1 and len(groups[0].gots) == 1:
        (g,), ((to,), (which,)), (r,) = groups, links[0], rows
        width = g.keep.shape[1]
        steps = next(s for s in (2, 1) if r % (16 * s) == 0)
        keep, got = g.keep.reshape(2, r, width), g.gots[0][0].reshape(2, r, width)
        mine = pl.BlockSpec((1, r // steps, width), lambda i, p: (p[which], i, 0))
        other = pl.BlockSpec((1, r // steps, width), lambda i, p: (1 - p[which], i, 0))
        g.keep, send = order.call(
            fold_kernel, spots, keep, keep, got, got, scalars=1, name="fold", us=3, grid=(steps,),
            in_specs=[mine, other, mine, other], out_specs=[pl.BlockSpec((r // steps, width), lambda i, p: (i, 0))] * 2,
            out_shape=[shaped(r, width)] * 2)
        g.gots = [(swap(send, *to), 0)]
        g.step += 1
        return
    gots = []
    for g in groups:
        for a, _ in g.gots:
            if not any(a is b for b in gots):
                gots.append(a)
    messages, heights, items = [], [], []
    for g, (tos, places), r in zip(groups, links, rows):
        sent = []
        for to in tos:
            key = to, g.keep.shape[1]
            if key not in messages:
                messages.append(key)
                heights.append(0)
            m = messages.index(key)
            sent.append((m, heights[m]))
            heights[m] += r
        items.append(([(next(n for n, b in enumerate(gots) if a is b), at) for a, at in g.gots], places, sent))
    shapes = [(r, g.keep.shape[1]) for r, g in zip(rows, groups)] + [(h, w) for h, (_, w) in zip(heights, messages)]
    arrays = [g.keep for g in groups] + gots
    out = order.call(
        functools.partial(small_fold_kernel, items=items, keeps=len(groups), gots=len(gots)), spots, *arrays, scalars=1,
        name="fold", us=3, grid=(1,), in_specs=[full(a.shape) for a in arrays],
        out_specs=[still(s) for s in shapes], out_shape=[shaped(*s) for s in shapes])
    came = [swap(out[len(groups) + m], *to) for m, (to, _) in enumerate(messages)]
    for i, g in enumerate(groups):
        g.keep = out[i]
        g.gots = [(came[m], first) for m, first in items[i][2]]
        g.step += 1


def finish_ffn_kernel(spot_ref, own_ref, got_ref, fi, fo, co):
    f32 = lambda v: v.astype(F32)
    D = own_ref.shape[1]
    for half in range(2):
        @pl.when(pl.program_id(0) == half)
        def _():
            part = lambda first, rows: f32(own_ref[first : first + rows, :] + got_ref[first : first + rows, :])
            fo[...] = part(96 * half, 96)
            for b in range(2):
                fi[:, D * b : D * (b + 1)] = part(192 + 96 * half + 48 * b, 48)
            if half:
                co[...] = part(384, 48)


def finish_ffn(order, spots, own, got, moves):
    D = own.shape[1]
    shapes = (48, 4 * D), (192, D), (48, D)
    return order.call(
        finish_ffn_kernel, spots, own, got, scalars=1, name="finish_ffn", us=3, grid=(2,), moves=moves,
        in_specs=[full(own.shape), full(got.shape)],
        out_specs=[pl.BlockSpec((48, 2 * D), lambda i, p: (0, i)), pl.BlockSpec((96, D), lambda i, p: (i, 0)), still((48, D))],
        out_shape=[shaped(*s, dtype=F32) for s in shapes])


def finish_kernel(spot_ref, *refs, groups, ats):
    ins, (sq, sk, sv, so, cq, ck, cv, *vectors) = refs[: 2 * groups], refs[2 * groups :]
    f32 = lambda v: v.astype(F32)
    unit = lambda v, u: f32(v[48 * u : 48 * u + 48])
    first = spot_ref[4] == 0
    pairs = []
    for i, at in enumerate(ats):
        own = ins[2 * i][...]
        pairs.append((own, ins[2 * i + 1][at : at + own.shape[0], :]))
    join = lambda own, got: (jnp.where(first, own, got), jnp.where(first, got, own))
    cross, own = join(*pairs[0]), join(*pairs[1])
    w = own[0].shape[1]
    for k in range(2):
        cols = slice(k * w, (k + 1) * w)
        for i, o in enumerate((cq, ck, cv, so)):
            o[:, cols] = unit(cross[k], i)
        for i, o in enumerate((sq, sk, sv)):
            o[:, cols] = unit(own[k], i)
    rows = f32(own[0][144:160])
    for i, o in enumerate(vectors[:13]):
        o[...] = rows[i : i + 1, :48]
    vectors[13][...] = rows[0:1, 128:320]


def finish(order, spots, *groups):
    D = 2 * groups[0].keep.shape[1]
    arrays = [a for g in groups for a in (g.keep, g.gots[0][0])]
    shapes = [(48, D)] * 7 + [(1, 48)] * 13 + [(1, 192)]
    return order.call(
        functools.partial(finish_kernel, groups=len(groups), ats=[g.gots[0][1] for g in groups]), spots, *arrays, scalars=1,
        name="finish", us=3, grid=(1,), in_specs=[full(a.shape) for a in arrays], out_specs=[still(s) for s in shapes],
        out_shape=[shaped(*s, dtype=F32) for s in shapes])


def swap(block, ax, bit, size):
    return lax.ppermute(block, ax, [(i, i ^ bit) for i in range(size)])


def two(s, first, second):
    return jnp.where(s == 0, jnp.concatenate([first, second], 0), jnp.concatenate([second, first], 0))


def pick(array, index, axis):
    return lax.dynamic_index_in_dim(array, index, axis, keepdims=False)


def whole_rows(
    hidden_in, memory, tgt_segment, src_segment, out_grad,
    self_query, query_bias, self_key, self_value, value_bias, self_output, output_bias,
    first_gain, first_shift,
    cross_query, cross_query_bias, cross_key, cross_value, cross_value_bias, cross_output,
    cross_output_bias, second_gain, second_shift,
    ffn_in, ffn_in_bias, ffn_out, ffn_out_bias, third_gain, third_shift,
):
    f32 = lambda v: v.astype(F32)
    s = lax.axis_index("seq")
    dp = lax.axis_index("dp")
    place = dp % 2, (dp // 2) % 2, (dp // 4) % 2, dp // 8, s
    spots = jnp.stack(place).astype(jnp.int32)
    order = Order()
    segs = jnp.stack([tgt_segment, src_segment])
    segs_own, segs_got = pick(segs, s, 1), swap(pick(segs, 1 - s, 1), "seq", 1, 2)
    segs = jnp.where(s == 0, jnp.concatenate([segs_own, segs_got], 1), jnp.concatenate([segs_got, segs_own], 1))
    hidden_got = swap(pick(hidden_in, 1 - s, 0), "seq", 1, 2)
    vec = jnp.stack([query_bias, value_bias, output_bias, first_gain, first_shift, cross_query_bias, cross_value_bias,
                     cross_output_bias, second_gain, second_shift, ffn_out_bias, third_gain, third_shift]).astype(F32)
    bin_ = f32(ffn_in_bias).reshape(1, -1)
    *near_self, near_key, near_value, memory_far, out_grad_far, near_mix, near_stats = project_near(
        order, spots, tgt_segment, hidden_in, memory, out_grad, vec, [self_query, self_key, self_value, cross_key, cross_value])
    memory_far, hidden_got, segs = lax.optimization_barrier((memory_far, hidden_got, segs))
    memory_got = swap(memory_far, "seq", 1, 2)
    (self_totals, n1, r1, first_low, cross_queries, self_oh, self_mk, cross_mk,
     hidden, queries, key_rows, value_rows, self_mixed) = self_forward(
        order, spots, vec, segs, near_mix, near_stats, hidden_in, hidden_got, near_self,
        [self_query, self_key, self_value, self_output, cross_query])
    out_grad_far, memory_got, r1 = lax.optimization_barrier((out_grad_far, memory_got, r1))
    out_grad_got = swap(out_grad_far, "seq", 1, 2)
    cross_totals, source, memory_keys, memory_values, cross_mixed = cross_forward(
        order, spots, vec, self_oh, cross_mk, cross_queries, memory, memory_got, [near_key, near_value], [cross_key, cross_value])
    ho, ho_far, second_back, cross_mixed_back, v_ffn, v_in, ffn_all = ffn_both(
        order, spots, vec, bin_, n1, cross_mixed, out_grad, out_grad_got, [cross_output, ffn_in, ffn_out])
    ho_got = swap(ho_far, "seq", 1, 2)
    ffn_sum = lax.psum_scatter(ffn_all.reshape(16, 432, -1), "dp", scatter_dimension=0, tiled=False)
    cross_query_back, memory_key_back, memory_value_back, mg, mg_far = cross_back(
        order, spots, cross_queries, memory_keys, memory_values, cross_mixed_back, cross_mixed, cross_totals, self_oh, cross_mk,
        [cross_key, cross_value])
    mg_far, ho_got = lax.optimization_barrier((mg_far, ho_got))
    mg_got = swap(mg_far, "seq", 1, 2)
    first_back, self_mixed_back, v_first, *pairs = middle(
        order, spots, vec, cross_query_back, memory_key_back, memory_value_back, n1, r1, second_back, first_low, source,
        self_mixed, [cross_query, self_output])
    cross_sum = Sum(*first_swap(*pairs, mg_got), *GROUP_LINKS)
    advance(order, spots, cross_sum)
    query_back, key_back, value_back, send, keep, hidden_out, memory_grad = self_back(
        order, spots, queries, key_rows, value_rows, self_mixed_back, self_mixed, self_totals, self_oh, self_mk,
        [v_ffn, v_first, v_in], hidden, [(ho, ho_got), (mg, mg_got)])
    self_sum = Sum(*first_swap(send, keep, cross_sum.gots[0][0]), *GROUP_LINKS)
    advance(order, spots, self_sum)
    advance(order, spots, cross_sum)
    hg, hg_far = back_rows(
        order, spots, [query_back, key_back, value_back], [self_query, self_key, self_value], first_back)
    hg_far, came, hg = lax.optimization_barrier((hg_far, self_sum.gots[0][0], hg))
    self_sum.gots = [(came, 0)]
    hg_got = swap(hg_far, "seq", 1, 2)
    ffn_sum, hg = lax.optimization_barrier((ffn_sum, hg))
    ffn_got = swap(ffn_sum, "seq", 1, 2)
    advance(order, spots, cross_sum, self_sum)
    advance(order, spots, cross_sum, self_sum)
    order.last.append(hg_got)
    advance(order, spots, cross_sum, self_sum)
    g_fi, g_fo, g_co, hidden_grad = finish_ffn(order, spots, ffn_sum, ffn_got, [(hg, hg_got)])
    advance(order, spots, cross_sum, self_sum)
    g_sq, g_sk, g_sv, g_so, g_cq, g_ck, g_cv, *v, v_fi = finish(order, spots, cross_sum, self_sum)
    (g3, b3, fob, g2, b2, cob, g1, b1, ob, cqb, cvb, qb, vb) = [a.reshape(-1) for a in v]
    return (
        hidden_out, hidden_grad, memory_grad,
        g_sq, qb, g_sk, g_sv, vb, g_so, ob, g1, b1, g_cq, cqb, g_ck, g_cv, cvb, g_co, cob, g2, b2,
        g_fi, v_fi.reshape(-1), g_fo, fob, g3, b3,
    )


def solution(mesh):
    in_specs = (
        P("dp", "seq", None),
        P("dp", "seq", None),
        P("dp", "seq"),
        P("dp", "seq"),
        P("dp", "seq", None),
        P(),
        P(),
        P(),
        P(),
        P(),
        P(),
        P(),
        P(),
        P(),
        P(),
        P(),
        P(),
        P(),
        P(),
        P(),
        P(),
        P(),
        P(),
        P(),
        P(),
        P(),
        P(),
        P(),
        P(),
    )
    out_specs = (
        P("dp", "seq", None),
        P("dp", "seq", None),
        P("dp", "seq", None),
        P("dp", None),
        P("dp"),
        P("dp", None),
        P("dp", None),
        P("dp"),
        P("dp", None),
        P("dp"),
        P("dp"),
        P("dp"),
        P("dp", None),
        P("dp"),
        P("dp", None),
        P("dp", None),
        P("dp"),
        P("dp", None),
        P("dp"),
        P("dp"),
        P("dp"),
        P("dp", None),
        P("dp"),
        P("dp", None),
        P("dp"),
        P("dp"),
        P("dp"),
    )
    rows_form = mesh.shape["seq"] == 2 and mesh.shape["dp"] == 16

    def on_device(*arrays):
        if rows_form and arrays[0].shape[0] == 2:
            return whole_rows(*arrays)
        return split_rows(*arrays)

    return jax.shard_map(
        on_device, mesh=mesh, in_specs=in_specs, out_specs=out_specs, check_vma=False
    )
```
